256 devices in a mesh: group: 16 (over z, core), tp: 16 (over y, x).
Axes of the slice: x: 4, y: 4, z: 8, core: 2. Of those that a mesh axis runs over, the one named last changes fastest.
Arguments:
- prompt_states: bfloat16 [64, 64, 4096], P('group', None, 'tp')
- ctx_weight: bfloat16 [4096, 3072], P('tp'), may hold values from -0.125 to 0.125
- image_prompt: int32 [64], replicated, may hold values from 0 to 63, each once
- image_lengths: int32 [16, 4], P('group'), may hold values from 1 to 128, 256 in all within a row
- latents: bfloat16 [16, 256, 3072], P('group', 'tp'), may hold values from -6 to 6
- img_mod: float32 [16, 4, 2, 3, 3072], P('group'), may hold values from -3 to 3
- txt_mod: float32 [16, 4, 2, 2, 3072], P('group'), may hold values from -3 to 3
- img_qkv: bfloat16 [3072, 3, 2048], P(None, None, 'tp'), may hold values from -0.109375 to 0.109375
- txt_kv: bfloat16 [3072, 2, 2048], P(None, None, 'tp'), may hold values from -0.109375 to 0.109375
- qk_gain: float32 [3, 128], replicated, may hold values from 0.7 to 2.2
- img_proj: bfloat16 [2048, 3072], P('tp'), may hold values from -0.125 to 0.125
Outputs:
- denoised: bfloat16 [16, 256, 3072], P('group', 'tp')
The draws below stay inside these ranges and needn't reach their ends.
Inputs may be any that keep to these rules, and one draw needn't show every extreme that they name: `image_prompt`: image 4 * g + k is image k of group g; every prompt conditions exactly one image. `image_lengths`: the image tokens of a group sum to 256; every group has one image of exactly 128 tokens.
All inputs are finite; a program needn't handle non-finite values.
Results may differ from the reference program's by a relative error of at most 0.025.
Values may be sent and summed in bfloat16 or wider, within the bound.
A program may use at most 64 MiB of HBM per device.

```python
import math
import jax
import jax.numpy as jnp
import numpy as np
from jax import lax

TEXT_WIDTH = 4096
MODEL_WIDTH = 3072
HEAD_COUNT = 16
HEAD_DIM = 128
PER_RANK = 4
TEXT_TOKENS = 64
IMAGE_ROWS = 256
STEP_COUNT = 2
PROMPT_COUNT = 64
N_GROUP = 16
N_TP = 16


def draw_prompt_states(key, part):
    key = jax.random.fold_in(key, 7)
    subkeys = jax.random.split(key, 3)
    dims_all = (PROMPT_COUNT, TEXT_TOKENS, TEXT_WIDTH)
    column = jnp.arange(TEXT_WIDTH, dtype=jnp.float32) / TEXT_WIDTH
    row_scale = jnp.exp(jax.random.uniform(subkeys[1], (PROMPT_COUNT, TEXT_TOKENS, 1), minval=0.0, maxval=math.log(10.0)))
    col_scale = jnp.exp(jax.random.uniform(subkeys[2], (TEXT_WIDTH,), minval=0.0, maxval=math.log(10.0)))
    values = jax.random.normal(subkeys[0], dims_all)
    rising = jnp.exp(math.log(3.0) * column)
    return (values * row_scale * col_scale * rising / 10.0).astype(jnp.bfloat16)


def strengthened(entries, own_key, source, target, shards_of, factor):
    def block_of(dim):
        return (jnp.arange(entries.shape[dim]) // (entries.shape[dim] // shards_of)).reshape((-1,) + (1,) * (entries.ndim - 1 - dim))

    near = jax.random.permutation(own_key, shards_of)[block_of(target)]
    second = (block_of(target) + shards_of // 2) % shards_of
    return jnp.where((block_of(source) == near) | (block_of(source) == second), factor * entries, entries)


def levels(rng, extent, cuts, least, high):
    loudness = 1.0
    for position, shards_of in cuts:
        draws = jax.random.uniform(jax.random.fold_in(jax.random.fold_in(rng, 6), position), (shards_of,), jnp.float32, least / len(cuts), high / len(cuts))
        loudness = loudness * jnp.repeat(jnp.exp(draws), extent[position] // shards_of).reshape((-1,) + (1,) * (len(extent) - 1 - position))
    return loudness


def profile(number_of, total, most, skew):
    weights = [(1 << 20) // math.isqrt(grade ** skew) + 1 for grade in range(2, number_of + 1)]
    spare, holding = total - most - (number_of - 1), [1] * (number_of - 1)
    while spare > 0:
        movable = [i for i in range(number_of - 1) if holding[i] < most]
        whole, budget = sum([weights[i] for i in movable]), spare
        for i in movable:
            addition = min(most - holding[i], max(1, budget * weights[i] // whole), spare)
            holding[i] = holding[i] + addition
            spare = spare - addition
    return np.array([most] + holding)


def uneven(stream_key, amount, total, most, lean):
    if amount == 2:
        one = jax.random.randint(stream_key, (), max(1, total - most), min(most, total - 1) + 1)
        return jnp.stack([one, total - one])
    tallies = jnp.asarray(profile(amount, total, most, lean), jnp.int32)
    pairs = (amount - 1) // 2
    source_of, sink = tallies[1:1 + 2 * pairs:2], tallies[2:2 + 2 * pairs:2]
    margin = jnp.minimum(source_of - 1, most - sink)
    moved = jax.random.randint(jax.random.fold_in(stream_key, 1), (pairs,), 0, 1 << 20) % (margin + 1)
    tallies = tallies.at[1:1 + 2 * pairs:2].set(source_of - moved).at[2:2 + 2 * pairs:2].set(sink + moved)
    return tallies[jax.random.permutation(jax.random.fold_in(stream_key, 2), amount)]


def bell_draw(own_key, dims, width, limit, cuts=(), kind=jnp.bfloat16):
    drawn = width * jax.random.normal(own_key, dims, jnp.float32)
    if cuts:
        drawn = drawn * levels(own_key, dims, cuts, -0.22, 0.18)
    return jnp.clip(drawn, -limit, limit).astype(kind)


def bell_draw_with(own_key, dims, scale, most, cuts, heavy, kind=jnp.bfloat16):
    result = scale * jax.random.normal(own_key, dims, jnp.float32)
    if cuts:
        result = result * levels(own_key, dims, cuts, -0.22, 0.18)
    return jnp.clip(strengthened(result, jax.random.fold_in(own_key, 3), *heavy), -most, most).astype(kind)


def setup_inputs(seed: int = 0) -> dict:
    arg_keys = jax.random.split(jax.random.key(seed), 12)
    prompt_states = draw_prompt_states(jax.random.fold_in(arg_keys[11], 71), 0)
    ctx_weight = bell_draw_with(arg_keys[1], (TEXT_WIDTH, MODEL_WIDTH), TEXT_WIDTH ** -0.5, 0.125, ((0, 16),), (0, 1, 16, 2.0))
    image_prompt = jax.random.permutation(arg_keys[2], PROMPT_COUNT).astype(jnp.int32)
    image_lengths = jax.vmap(lambda own: uneven(own, PER_RANK, IMAGE_ROWS, IMAGE_ROWS // 2, 2))(jax.random.split(arg_keys[3], N_GROUP)).reshape((N_GROUP, PER_RANK)).astype(jnp.int32)
    latents = bell_draw(arg_keys[4], (N_GROUP, IMAGE_ROWS, MODEL_WIDTH), 1.0, 6.0, ((0, 16), (1, 16)))
    img_mod = bell_draw(arg_keys[5], (N_GROUP, PER_RANK, STEP_COUNT, 3, MODEL_WIDTH), 0.6, 3.0, ((0, 16),), jnp.float32)
    txt_mod = bell_draw(arg_keys[6], (N_GROUP, PER_RANK, STEP_COUNT, 2, MODEL_WIDTH), 0.6, 3.0, ((0, 16),), jnp.float32)
    img_qkv = bell_draw(arg_keys[7], (MODEL_WIDTH, 3, HEAD_COUNT * HEAD_DIM), MODEL_WIDTH ** -0.5, 0.109375, ((2, 16),))
    txt_kv = bell_draw(arg_keys[8], (MODEL_WIDTH, 2, HEAD_COUNT * HEAD_DIM), MODEL_WIDTH ** -0.5, 0.109375, ((2, 16),))
    qk_gain = jnp.clip(jnp.exp(jax.random.uniform(arg_keys[9], (3, HEAD_DIM), jnp.float32, math.log(0.7), math.log(2.2))), 0.7, 2.2)
    img_proj = bell_draw(arg_keys[10], (HEAD_COUNT * HEAD_DIM, MODEL_WIDTH), (HEAD_COUNT * HEAD_DIM) ** -0.5, 0.125, ((0, 16),))
    return {"prompt_states": prompt_states, "ctx_weight": ctx_weight, "image_prompt": image_prompt, "image_lengths": image_lengths, "latents": latents, "img_mod": img_mod, "txt_mod": txt_mod, "img_qkv": img_qkv, "txt_kv": txt_kv, "qk_gain": qk_gain, "img_proj": img_proj}


def layer_norm(values):
    centered = values - lax.optimization_barrier(jnp.mean(values, -1, keepdims=True))
    return centered * lax.rsqrt(lax.optimization_barrier(jnp.mean(centered * centered, -1, keepdims=True)) + 1e-06)

def rms_scale(values, gain_row):
    return values * lax.rsqrt(lax.optimization_barrier(jnp.mean(values * values, -1, keepdims=True)) + 1e-06) * gain_row

def attend_block(query_block, segment_block, keys_all, values_all, segment_keys):
    scores = jnp.einsum('qhd,khd->hqk', query_block.astype(jnp.float32), keys_all.astype(jnp.float32), precision=lax.Precision.HIGHEST) * HEAD_DIM ** (-0.5)
    allowed = (segment_block[:, None] == segment_keys[None, :])[None]
    expsum = jnp.where(allowed, jnp.exp(scores), 0.0)
    weights = (expsum / lax.optimization_barrier(jnp.sum(expsum, -1, keepdims=True))).astype(jnp.bfloat16)
    return jnp.einsum('hqk,khd->qhd', weights.astype(jnp.float32), values_all.astype(jnp.float32), precision=lax.Precision.HIGHEST).astype(jnp.bfloat16)

def attention(queries, keys_all, values_all, segment_rows, segment_keys):
    rows_total = queries.shape[0]
    block_rows = min(512, rows_total)
    block_count = rows_total // block_rows
    query_blocks = queries.reshape((block_count, block_rows) + queries.shape[1:])
    segment_blocks = segment_rows.reshape(block_count, block_rows)

    def attend_pair(packed):
        return attend_block(packed[0], packed[1], keys_all, values_all, segment_keys)
    outputs = lax.map(attend_pair, (query_blocks, segment_blocks))
    return outputs.reshape(rows_total, -1)

def head_groups(attended, img_proj):
    local_width = HEAD_COUNT * HEAD_DIM // N_TP

    def add_group(group_number, running):
        first = (group_number * local_width).astype(jnp.int32)
        head_cols = lax.dynamic_slice_in_dim(attended, first, local_width, 1)
        proj_rows = lax.dynamic_slice_in_dim(img_proj, first, local_width, 0)
        term = jnp.dot(head_cols, proj_rows, preferred_element_type=jnp.float32)
        rounded = lax.optimization_barrier(term.astype(jnp.bfloat16))
        return running + rounded.astype(jnp.float32)
    return lax.fori_loop(jnp.int32(0), jnp.int32(N_TP), add_group, jnp.zeros((IMAGE_ROWS, MODEL_WIDTH), jnp.float32))

def reference(prompt_states, ctx_weight, image_prompt, image_lengths, latents, img_mod, txt_mod, img_qkv, txt_kv, qk_gain, img_proj):
    flat_text = prompt_states.reshape(PROMPT_COUNT * TEXT_TOKENS, TEXT_WIDTH)
    embedded = jnp.dot(flat_text, ctx_weight, preferred_element_type=jnp.float32).astype(jnp.bfloat16)
    embedded = embedded.reshape(PROMPT_COUNT, TEXT_TOKENS, MODEL_WIDTH)
    qkv_flat = img_qkv.reshape(MODEL_WIDTH, 3 * HEAD_COUNT * HEAD_DIM)
    kv_flat = txt_kv.reshape(MODEL_WIDTH, 2 * HEAD_COUNT * HEAD_DIM)
    text_segments = jnp.repeat(jnp.arange(PER_RANK, dtype=jnp.int32), TEXT_TOKENS)

    def one_group(packed):
        latent_group, lengths, image_mod, text_mod, prompt_ids = packed
        slot_text = embedded[prompt_ids]
        text_ln = layer_norm(slot_text.astype(jnp.float32))
        bounds = jnp.cumsum(lengths)
        row_ids = jnp.arange(IMAGE_ROWS, dtype=jnp.int32)
        segments = lax.optimization_barrier(jnp.sum((row_ids[:, None] >= bounds[None, :]).astype(jnp.int32), 1)).astype(jnp.int32)
        segment_keys = jnp.concatenate([text_segments, segments])
        latent = latent_group
        for step_index in range(STEP_COUNT):
            text_in = text_ln * (1.0 + text_mod[:, step_index, 1][:, None, :]) + text_mod[:, step_index, 0][:, None, :]
            text_in = text_in.astype(jnp.bfloat16).reshape(PER_RANK * TEXT_TOKENS, MODEL_WIDTH)
            text_kv = jnp.dot(text_in, kv_flat, preferred_element_type=jnp.float32).reshape(PER_RANK * TEXT_TOKENS, 2, HEAD_COUNT, HEAD_DIM)
            keys_text = rms_scale(text_kv[:, 0], qk_gain[2]).astype(jnp.bfloat16)
            vals_text = text_kv[:, 1].astype(jnp.bfloat16)
            image_in = layer_norm(latent.astype(jnp.float32)) * (1.0 + image_mod[segments, step_index, 1]) + image_mod[segments, step_index, 0]
            image_in = image_in.astype(jnp.bfloat16)
            projected = jnp.dot(image_in, qkv_flat, preferred_element_type=jnp.float32).reshape(IMAGE_ROWS, 3, HEAD_COUNT, HEAD_DIM)
            queries = rms_scale(projected[:, 0], qk_gain[0]).astype(jnp.bfloat16)
            keys_img = rms_scale(projected[:, 1], qk_gain[1]).astype(jnp.bfloat16)
            vals_img = projected[:, 2].astype(jnp.bfloat16)
            keys_all = jnp.concatenate([keys_text, keys_img], 0)
            values_all = jnp.concatenate([vals_text, vals_img], 0)
            attended = attention(queries, keys_all, values_all, segments, segment_keys)
            update = head_groups(attended, img_proj)
            latent = (latent.astype(jnp.float32) + image_mod[segments, step_index, 2] * update).astype(jnp.bfloat16)
        return latent
    return lax.map(one_group, (latents, image_lengths, img_mod, txt_mod, image_prompt.reshape(N_GROUP, PER_RANK)))
```

```python
import functools

import jax
import jax.numpy as jnp
from jax import lax
from jax.experimental import pallas as pl
from jax.experimental.pallas import tpu as pltpu
from jax.sharding import PartitionSpec as P

MESH = pl.DeviceIdType.MESH
F32, BF16 = jnp.float32, jnp.bfloat16
WIDTH, HALF, QUARTER = 3072, 1536, 768
ROWS = 16
SIDE = 4
DEPTH = 8
HEAD = 128
OFFSETS = (0, 3, 1, 2)
RELAY_RIGHT, RELAY_LEFT = (0, 3), (1, 2)


def layer_norm(values):
    centered = values - jnp.mean(values, -1, keepdims=True)
    return centered * lax.rsqrt(jnp.mean(centered * centered, -1, keepdims=True) + 1e-6)


def rms_scale(values, gain_row):
    return values * lax.rsqrt(jnp.mean(values * values, -1, keepdims=True) + 1e-6) * gain_row


class Place:
    def __init__(self):
        self.group, self.tp = lax.axis_index("group"), lax.axis_index("tp")
        self.x, self.y = lax.rem(self.tp, SIDE), self.tp // SIDE
        self.z, self.core = self.group // 2, lax.rem(self.group, 2)

    def along(self, axis, step):
        if axis == 0:
            return (self.group, self.y * SIDE + lax.rem(self.x + step + SIDE, SIDE))
        return (self.group, lax.rem(self.y + step + SIDE, SIDE) * SIDE + self.x)

    def slot(self, half, first, second):
        dx, dy = (first, second) if half == 0 else (second, first)
        return lax.rem(self.y + dy + SIDE, SIDE) * SIDE + lax.rem(self.x + dx + SIDE, SIDE)

    def up(self, step):
        return (lax.rem(self.z + step + DEPTH, DEPTH) * 2 + self.core, self.tp)

    def sibling(self):
        return (self.z * 2 + 1 - self.core, self.tp)


class Sends:
    def __init__(self, sems):
        self.sems, self.pending = sems, []

    def start(self, src, dst, recv, device):
        copy = pltpu.make_async_remote_copy(
            src_ref=src,
            dst_ref=dst,
            send_sem=self.sems.at[len(self.pending)],
            recv_sem=recv,
            device_id=device,
            device_id_type=MESH,
        )
        copy.start()
        self.pending.append(copy)

    def finish(self):
        for copy in self.pending:
            copy.wait_send()


def arrived(ref, sem):
    pltpu.make_async_copy(ref, ref, sem).wait()


class Gather:
    def __init__(self, place, buf, sems, send_sems):
        self.place, self.buf, self.sems, self.sends = place, buf, sems, Sends(send_sems)

    def send(self, half, axis, step, slot, part=None):
        if part is None:
            ref, sem = self.buf.at[half, slot], self.sems.at[half, slot, 0]
        else:
            ref = self.buf.at[half, slot, :, pl.ds(part * QUARTER, QUARTER)]
            sem = self.sems.at[half, slot, part]
        self.sends.start(ref, ref, sem, self.place.along(axis, step))

    def wait(self, half, slot, part=None):
        if part is None:
            ref, sem = self.buf.at[half, slot], self.sems.at[half, slot, 0]
        else:
            ref = self.buf.at[half, slot, :, pl.ds(part * QUARTER, QUARTER)]
            sem = self.sems.at[half, slot, part]
        arrived(ref, sem)

    def start(self):
        place = self.place
        for half in (0, 1):
            first, second = half, 1 - half
            own = place.slot(half, 0, 0)
            for step in (1, -1):
                self.send(half, first, step, own)
            for step in (1, -1):
                self.send(half, second, step, own)

    def neighbours(self):
        place = self.place
        for half in (0, 1):
            first, second = half, 1 - half
            for offset, way, part in ((-1, 1, 0), (1, -1, 1)):
                slot = place.slot(half, offset, 0)
                self.wait(half, slot)
                self.send(half, first, way, slot, part)
                for step in (1, -1):
                    self.send(half, second, step, slot)

    def relay(self, half, index):
        second = 1 - half
        step = 1 if index in RELAY_RIGHT else -1
        slot = self.place.slot(half, OFFSETS[index], -step)
        self.wait(half, slot)
        self.send(half, second, step, slot)

    def opposite(self):
        for half in (0, 1):
            self.relay(half, 0)
        for half in (0, 1):
            slot = self.place.slot(half, 2, 0)
            for part in (0, 1):
                self.wait(half, slot, part)
            for step in (1, -1):
                self.send(half, 1 - half, step, slot)

    def relays(self):
        for index in (1, 2, 3):
            for half in (0, 1):
                self.relay(half, index)

    def finish(self, half):
        for index in range(4):
            step = 1 if index in RELAY_RIGHT else -1
            self.wait(half, self.place.slot(half, OFFSETS[index], step))
            self.wait(half, self.place.slot(half, OFFSETS[index], 2))


class Scatter:
    def __init__(self, place, buf, relayed, left, right, mid, relayed2, left2, right2, sems, sems2, send_sems):
        self.place, self.buf = place, buf
        self.relayed, self.left, self.right = relayed, left, right
        self.mid, self.relayed2, self.left2, self.right2 = mid, relayed2, left2, right2
        self.sems, self.sems2, self.sends = sems, sems2, Sends(send_sems)

    def start(self):
        place = self.place
        for half in (0, 1):
            for way, (classes, step) in enumerate(((RELAY_RIGHT, 1), (RELAY_LEFT, -1))):
                for order, index in enumerate(classes):
                    self.sends.start(
                        self.buf.at[half, place.slot(half, 2, OFFSETS[index])],
                        self.relayed.at[half, way, order],
                        self.sems.at[half, 2, way * 2 + order],
                        place.along(half, step),
                    )
        for half in (0, 1):
            for index in RELAY_LEFT:
                self.sends.start(
                    self.buf.at[half, place.slot(half, 1, OFFSETS[index])],
                    self.left.at[half, index],
                    self.sems.at[half, 0, index],
                    place.along(half, 1),
                )
            for index in RELAY_RIGHT:
                self.sends.start(
                    self.buf.at[half, place.slot(half, -1, OFFSETS[index])],
                    self.right.at[half, index],
                    self.sems.at[half, 1, index],
                    place.along(half, -1),
                )

    def relays(self):
        place = self.place
        for order in (1, 0):
            for half in (0, 1):
                for way, (classes, step) in enumerate(((RELAY_RIGHT, 1), (RELAY_LEFT, -1))):
                    index = classes[order]
                    landed = self.relayed.at[half, way, order]
                    arrived(landed, self.sems.at[half, 2, way * 2 + order])
                    slot = place.slot(half, step, OFFSETS[index])
                    total = self.buf[half, slot].astype(F32) + landed[...].astype(F32)
                    self.buf[half, slot] = total.astype(BF16)
                    self.sends.start(
                        self.buf.at[half, slot],
                        (self.left if step == 1 else self.right).at[half, index],
                        self.sems.at[half, way, index],
                        place.along(half, step),
                    )

    def sums(self):
        place = self.place
        for index in (3, 1, 2, 0):
            for half in (0, 1):
                arrived(self.left.at[half, index], self.sems.at[half, 0, index])
                arrived(self.right.at[half, index], self.sems.at[half, 1, index])
                slot = place.slot(half, 0, OFFSETS[index])
                total = self.buf[half, slot].astype(F32) + self.left[half, index].astype(F32)
                total = total + self.right[half, index].astype(F32)
                self.mid[half, index] = total.astype(BF16)
                axis = 1 - half
                low, high = pl.ds(0, QUARTER), pl.ds(QUARTER, QUARTER)
                if index == 3:
                    for part, (cols, step) in enumerate(((low, 1), (high, -1))):
                        self.sends.start(
                            self.mid.at[half, 3, :, cols],
                            self.relayed2.at[half, part],
                            self.sems2.at[half, part],
                            place.along(axis, step),
                        )
                if index == 2:
                    self.sends.start(
                        self.mid.at[half, 2, :, high],
                        self.left2.at[half, :, high],
                        self.sems2.at[half, 2],
                        place.along(axis, 1),
                    )
                if index == 1:
                    self.sends.start(
                        self.mid.at[half, 1, :, low],
                        self.right2.at[half, :, low],
                        self.sems2.at[half, 3],
                        place.along(axis, -1),
                    )

    def last(self):
        place = self.place
        for half in (0, 1):
            axis = 1 - half
            for part, index, step, target in ((0, 2, 1, self.left2), (1, 1, -1, self.right2)):
                cols = pl.ds(part * QUARTER, QUARTER)
                arrived(self.relayed2.at[half, part], self.sems2.at[half, part])
                total = self.mid[half, index, :, cols].astype(F32) + self.relayed2[half, part].astype(F32)
                self.mid[half, index, :, cols] = total.astype(BF16)
                self.sends.start(
                    self.mid.at[half, index, :, cols],
                    target.at[half, :, cols],
                    self.sems2.at[half, 4 + part],
                    place.along(axis, step),
                )

    def result(self, half):
        low, high = pl.ds(0, QUARTER), pl.ds(QUARTER, QUARTER)
        arrived(self.left2.at[half, :, high], self.sems2.at[half, 2])
        arrived(self.right2.at[half, :, low], self.sems2.at[half, 3])
        arrived(self.left2.at[half, :, low], self.sems2.at[half, 4])
        arrived(self.right2.at[half, :, high], self.sems2.at[half, 5])
        total = self.mid[half, 0].astype(F32) + self.left2[half].astype(F32)
        return total + self.right2[half].astype(F32)

    def run(self):
        self.start()
        self.relays()
        self.sums()
        self.last()


class Handoff:
    def __init__(self, place, buf, sems, send_sems):
        self.place, self.buf, self.sems, self.sends = place, buf, sems, Sends(send_sems)

    def slot(self, step):
        return lax.rem(self.place.z + step + DEPTH, DEPTH) * 2 + self.place.core

    def piece(self, slot, part):
        if part is None:
            return self.buf.at[slot], self.sems.at[slot, 0]
        return self.buf.at[slot, :, pl.ds(part * HALF, HALF)], self.sems.at[slot, part]

    def send(self, slot, device, part=None):
        ref, sem = self.piece(slot, part)
        self.sends.start(ref, ref, sem, device)

    def wait(self, slot, part=None):
        ref, sem = self.piece(slot, part)
        arrived(ref, sem)

    def start(self):
        own = self.slot(0)
        for step in (1, -1):
            self.send(own, self.place.up(step))
        self.send(own, self.place.sibling())

    def step(self, number):
        for way in (1, -1):
            slot = self.slot(-way * number)
            if number < 4:
                self.wait(slot)
                part = None if number < 3 else (0 if way == 1 else 1)
                self.send(slot, self.place.up(way), part)
                self.send(slot, self.place.sibling())
        if number == 4:
            slot = self.slot(4)
            self.wait(slot, 0)
            self.wait(slot, 1)
            self.send(slot, self.place.sibling())

    def finish(self):
        for step in range(DEPTH):
            slot = lax.rem(self.place.z + step, DEPTH) * 2 + 1 - self.place.core
            self.wait(slot)


def kernel(
    prompt_ids,
    lengths,
    prompt_hbm,
    ctx_hbm,
    latent_hbm,
    imod_hbm,
    tmod_hbm,
    qkv_hbm,
    txt_hbm,
    gain,
    proj_hbm,
    out,
    prompt,
    ctx,
    latent,
    imod,
    tmod,
    qkv_w,
    txt_raw,
    txt_w,
    proj_w,
    local_sems,
    gathered,
    gather_sems,
    gather_sends,
    sc_buf,
    sc_relayed,
    sc_left,
    sc_right,
    sc_mid,
    sc_relayed2,
    sc_left2,
    sc_right2,
    sc_sems,
    sc_sems2,
    sc_sends,
    handed,
    hand_sems,
    hand_sends,
    x_state,
    text_in,
    text_kv,
    tscale,
):
    place = Place()

    loads = []

    def load(src, dst):
        copy = pltpu.make_async_copy(src, dst, local_sems.at[len(loads)])
        copy.start()
        loads.append(copy)
        return copy

    barrier = pltpu.get_barrier_semaphore()
    partners = [place.along(axis, step) for axis in (0, 1) for step in (1, -1)]
    partners += [place.up(1), place.up(-1), place.sibling()]
    for partner in partners:
        pl.semaphore_signal(barrier, inc=1, device_id=partner, device_id_type=MESH)

    load_prompt = load(prompt_hbm, prompt)
    load_ctx = load(ctx_hbm, ctx)
    load_latent = load(latent_hbm, latent)
    load_imod = load(imod_hbm, imod)
    load_tmod = load(tmod_hbm, tmod)
    load_qkv = [load(qkv_hbm.at[part], qkv_w.at[:, pl.ds(part * HEAD, HEAD)]) for part in range(3)]
    load_txt = load(txt_hbm, txt_raw)
    load_proj = load(proj_hbm, proj_w)

    bounds, running = [], 0
    for image in range(4):
        running = running + lengths[0, image]
        bounds.append(running)

    def segments_of(row_ids):
        return sum((row_ids >= bound).astype(jnp.int32) for bound in bounds)

    rows_iota = lax.broadcasted_iota(jnp.int32, (16 * ROWS, 1), 0)
    lanes_iota = lax.broadcasted_iota(jnp.int32, (1, 16 * ROWS), 1)
    mine = segments_of(place.tp * ROWS + lax.broadcasted_iota(jnp.int32, (ROWS, 1), 0))

    def modulation(step, kind, cols):
        rows = jnp.zeros((ROWS, cols.size), F32)
        for image in range(4):
            rows = jnp.where(mine == image, imod[image, kind, step : step + 1, cols], rows)
        return rows

    whole = pl.ds(0, WIDTH)
    halves = (pl.ds(0, HALF), pl.ds(HALF, HALF))

    def gather_of(which):
        return Gather(place, gathered.at[which], gather_sems.at[which], gather_sends.at[which])

    def scatter_of(which):
        return Scatter(
            place,
            *[
                ref.at[which]
                for ref in (
                    sc_buf,
                    sc_relayed,
                    sc_left,
                    sc_right,
                    sc_mid,
                    sc_relayed2,
                    sc_left2,
                    sc_right2,
                    sc_sems,
                    sc_sems2,
                    sc_sends,
                )
            ],
        )

    def put_block(which, values):
        for half in (0, 1):
            gathered[which, half, place.tp] = values[:, half * HALF : (half + 1) * HALF]

    load_prompt.wait()
    row = lax.broadcasted_iota(jnp.int32, (256, 256), 0)
    col = lax.broadcasted_iota(jnp.int32, (256, 256), 1)
    source = lax.rem(row // 4, 4) * 64 + (row // 16) * 4 + lax.rem(row, 4)
    order = (col == source).astype(BF16)
    ordered = jnp.dot(order, prompt[...], preferred_element_type=F32).astype(BF16)
    load_ctx.wait()

    def spread(which, left, weight_of):
        for half in (0, 1):
            for piece in range(HALF // 512):
                product = jnp.dot(left, weight_of(half * HALF + piece * 512), preferred_element_type=F32)
                sc_buf[which, half, :, :, pl.ds(piece * 512, 512)] = product.astype(BF16).reshape(16, ROWS, 512)

    spread(0, ordered, lambda at: ctx[:, pl.ds(at, 512)])

    pl.semaphore_wait(barrier, len(partners))
    text_scatter = scatter_of(0)
    text_scatter.start()

    load_latent.wait()
    load_imod.wait()
    x_state[...] = latent[...].astype(F32)

    def modulated(step):
        values = layer_norm(x_state[...])
        return (values * (1.0 + modulation(step, 1, whole)) + modulation(step, 0, whole)).astype(BF16)

    put_block(0, modulated(0))
    text_scatter.relays()
    text_scatter.sums()
    text_scatter.last()
    first_gather = gather_of(0)
    first_gather.start()

    handoff = Handoff(place, handed, hand_sems, hand_sends)
    for half in (0, 1):
        handed[place.group, :, halves[half]] = text_scatter.result(half).astype(BF16)
    handoff.start()
    first_gather.neighbours()
    handoff.step(1)
    first_gather.opposite()
    handoff.step(2)
    first_gather.relays()
    handoff.step(3)
    handoff.step(4)

    load_txt.wait()
    unweave = (col == lax.rem(row, 128) * 2 + row // 128).astype(BF16)

    def part_weights(chunk, carry):
        mixed = txt_raw[pl.ds(pl.multiple_of(chunk * 256, 256), 256), :]
        parted = jnp.dot(unweave, mixed, preferred_element_type=F32).astype(BF16)
        at = pl.ds(pl.multiple_of(chunk * 128, 128), 128)
        txt_w[at, 0:HEAD] = parted[:128]
        txt_w[at, HEAD:] = parted[128:]
        return carry

    lax.fori_loop(0, 24, part_weights, 0)

    load_tmod.wait()
    slot_image = lax.broadcasted_iota(jnp.int32, (ROWS, 1), 0) // 4
    for step in (0, 1):
        for kind in (0, 1):
            rows = jnp.zeros((ROWS, WIDTH), F32)
            for image in range(4):
                rows = jnp.where(slot_image == image, tmod[image, step, kind : kind + 1, :], rows)
            tscale[step, kind] = rows + float(kind)

    handoff.finish()
    pick_row = lax.broadcasted_iota(jnp.int32, (ROWS, 256), 0)
    pick_col = lax.broadcasted_iota(jnp.int32, (ROWS, 256), 1)
    wanted = jnp.zeros((ROWS, 256), jnp.int32)
    for image in range(4):
        wanted = jnp.where(pick_row // 4 == image, prompt_ids[place.group * 4 + image] * 4, wanted)
    pick = (pick_col == wanted + lax.rem(pick_row, 4)).astype(BF16)
    slot_text = jnp.concatenate(
        [
            jnp.dot(
                pick,
                handed[:, :, pl.ds(piece * 512, 512)].reshape(256, 512),
                preferred_element_type=F32,
            )
            for piece in range(6)
        ],
        axis=1,
    )
    put_block(2, layer_norm(slot_text).astype(BF16))
    text_gather = gather_of(2)
    text_gather.start()

    def project_image(which, gather):
        total = None
        for half in (0, 1):
            gather.finish(half)
            term = jnp.dot(
                gathered[which, half].reshape(256, HALF),
                qkv_w[pl.ds(half * HALF, HALF), :],
                preferred_element_type=F32,
            )
            total = term if total is None else total + term
        queries = rms_scale(total[:, :HEAD], gain[0:1]).astype(BF16)
        keys = rms_scale(total[:, HEAD : 2 * HEAD], gain[1:2]).astype(BF16)
        return queries, keys, total[:, 2 * HEAD :].astype(BF16)

    def project_text(step):
        for half in (0, 1):

            def modulate(owner, carry):
                normed = gathered[2, half, owner].astype(F32)
                scaled = normed * tscale[step, 1, :, halves[half]] + tscale[step, 0, :, halves[half]]
                text_in[half, owner] = scaled.astype(BF16)
                return carry

            lax.fori_loop(0, 16, modulate, 0)
        total = None
        for half in (0, 1):
            term = jnp.dot(
                text_in[half].reshape(256, HALF),
                txt_w[pl.ds(half * HALF, HALF), :],
                preferred_element_type=F32,
            )
            total = term if total is None else total + term
        text_kv[:, :HEAD] = rms_scale(total[:, :HEAD], gain[2:3]).astype(BF16)
        text_kv[:, HEAD:] = total[:, HEAD:].astype(BF16)

    segment_rows = segments_of(rows_iota)
    text_allowed = segment_rows == lax.rem(lanes_iota // 4, 4)
    image_allowed = segment_rows == segments_of(lanes_iota)

    def weigh(queries, keys, allowed):
        scores = lax.dot_general(queries, keys, (((1,), (1,)), ((), ())), preferred_element_type=F32)
        return jnp.where(allowed, jnp.exp(scores * HEAD**-0.5), 0.0)

    def attend(queries, keys, values):
        text_part = weigh(queries, text_kv[:, :HEAD], text_allowed)
        image_part = weigh(queries, keys, image_allowed)
        norm = jnp.sum(text_part, -1, keepdims=True) + jnp.sum(image_part, -1, keepdims=True)
        mixed = jnp.dot(text_part.astype(BF16), text_kv[:, HEAD:], preferred_element_type=F32)
        mixed = mixed + jnp.dot(image_part.astype(BF16), values, preferred_element_type=F32)
        return (mixed / norm).astype(BF16)

    def advance(step, scatter):
        for half in (0, 1):
            update = scatter.result(half)
            gate = modulation(step, 2, halves[half])
            state = x_state[:, halves[half]] + gate * update
            x_state[:, halves[half]] = state.astype(BF16).astype(F32)

    for copy in load_qkv:
        copy.wait()
    queries, keys, values = project_image(0, first_gather)
    text_gather.neighbours()
    text_gather.opposite()
    text_gather.relays()
    for half in (0, 1):
        text_gather.finish(half)
    project_text(0)
    load_proj.wait()

    def scatter_update(which, queries, keys, values):
        attended = attend(queries, keys, values)
        spread(which, attended, lambda at: proj_w[:, pl.ds(at, 512)])
        scatter = scatter_of(which)
        scatter.start()
        return scatter

    first_scatter = scatter_update(1, queries, keys, values)
    first_scatter.relays()
    project_text(1)
    first_scatter.sums()
    first_scatter.last()
    advance(0, first_scatter)

    put_block(1, modulated(1))
    second_gather = gather_of(1)
    second_gather.start()
    second_gather.neighbours()
    second_gather.opposite()
    second_gather.relays()
    queries, keys, values = project_image(1, second_gather)
    second_scatter = scatter_update(2, queries, keys, values)
    second_scatter.relays()
    second_scatter.sums()
    second_scatter.last()
    advance(1, second_scatter)
    out[...] = x_state[...].astype(BF16)

    for part in (text_scatter, first_gather, handoff, text_gather, first_scatter, second_gather, second_scatter):
        part.sends.finish()


def on_device(
    prompt_states,
    ctx_weight,
    image_prompt,
    image_lengths,
    latents,
    img_mod,
    txt_mod,
    img_qkv,
    txt_kv,
    qk_gain,
    img_proj,
):
    anywhere = pl.BlockSpec(memory_space=pl.ANY)
    scalars = pl.BlockSpec(memory_space=pltpu.SMEM)
    in_vmem = pl.BlockSpec(memory_space=pltpu.VMEM)
    dma = pltpu.SemaphoreType.DMA
    block = (ROWS, HALF)
    denoised = pl.pallas_call(
        kernel,
        out_shape=jax.ShapeDtypeStruct((ROWS, WIDTH), BF16),
        in_specs=[scalars, scalars] + [anywhere] * 7 + [in_vmem, anywhere],
        out_specs=in_vmem,
        scratch_shapes=[
            pltpu.VMEM((256, 256), BF16),
            pltpu.VMEM((256, WIDTH), BF16),
            pltpu.VMEM((ROWS, WIDTH), BF16),
            pltpu.VMEM((4, 3, 2, WIDTH), F32),
            pltpu.VMEM((4, 2, 2, WIDTH), F32),
            pltpu.VMEM((WIDTH, 3 * HEAD), BF16),
            pltpu.VMEM((2 * WIDTH, HEAD), BF16),
            pltpu.VMEM((WIDTH, 2 * HEAD), BF16),
            pltpu.VMEM((HEAD, WIDTH), BF16),
            dma((10,)),
            pltpu.VMEM((3, 2, 16) + block, BF16),
            dma((3, 2, 16, 2)),
            dma((3, 36)),
            pltpu.VMEM((3, 2, 16) + block, BF16),
            pltpu.VMEM((3, 2, 2, 2) + block, BF16),
            pltpu.VMEM((3, 2, 4) + block, BF16),
            pltpu.VMEM((3, 2, 4) + block, BF16),
            pltpu.VMEM((3, 2, 4) + block, BF16),
            pltpu.VMEM((3, 2, 2, ROWS, QUARTER), BF16),
            pltpu.VMEM((3, 2) + block, BF16),
            pltpu.VMEM((3, 2) + block, BF16),
            dma((3, 2, 3, 4)),
            dma((3, 2, 6)),
            dma((3, 36)),
            pltpu.VMEM((16, ROWS, WIDTH), BF16),
            dma((16, 2)),
            dma((24,)),
            pltpu.VMEM((ROWS, WIDTH), F32),
            pltpu.VMEM((2, 16) + block, BF16),
            pltpu.VMEM((256, 2 * HEAD), BF16),
            pltpu.VMEM((2, 2, ROWS, WIDTH), F32),
        ],
        compiler_params=pltpu.CompilerParams(
            collective_id=0, has_side_effects=True, vmem_limit_bytes=56 * 1024 * 1024
        ),
    )(
        image_prompt,
        image_lengths,
        prompt_states.reshape(256, 256),
        ctx_weight,
        latents[0],
        jnp.transpose(img_mod[0], (0, 2, 1, 3)),
        txt_mod[0],
        jnp.transpose(img_qkv, (1, 0, 2)),
        txt_kv.reshape(2 * WIDTH, HEAD),
        qk_gain,
        img_proj,
    )
    return denoised[None]


def solution(mesh):
    placed = (
        P("group", None, "tp"),
        P("tp", None),
        P(),
        P("group", None),
        P("group", "tp", None),
        P("group", None, None, None, None),
        P("group", None, None, None, None),
        P(None, None, "tp"),
        P(None, None, "tp"),
        P(),
        P("tp", None),
    )
    return jax.shard_map(
        on_device, mesh=mesh, in_specs=placed, out_specs=P("group", "tp", None), check_vma=False
    )
```

```python
import functools

import jax
import jax.numpy as jnp
from jax import lax
from jax.experimental import pallas as pl
from jax.experimental.pallas import tpu as pltpu
from jax.sharding import PartitionSpec as P

MESH = pl.DeviceIdType.MESH
F32, BF16 = jnp.float32, jnp.bfloat16
WIDTH, HALF = 3072, 1536
ROWS = 16
SIDE = 4
DEPTH = 8
HEAD = 128
STEPS = (1, -1, 2)


def layer_norm(values):
    centered = values - jnp.mean(values, -1, keepdims=True)
    return centered * lax.rsqrt(jnp.mean(centered * centered, -1, keepdims=True) + 1e-6)


def rms_scale(values, gain_row):
    return values * lax.rsqrt(jnp.mean(values * values, -1, keepdims=True) + 1e-6) * gain_row


class Place:
    def __init__(self):
        self.group, self.tp = lax.axis_index("group"), lax.axis_index("tp")
        self.x, self.y = lax.rem(self.tp, SIDE), self.tp // SIDE
        self.z, self.core = self.group // 2, lax.rem(self.group, 2)

    def along(self, axis, step):
        if axis == 0:
            return (self.group, self.y * SIDE + lax.rem(self.x + step + SIDE, SIDE))
        return (self.group, lax.rem(self.y + step + SIDE, SIDE) * SIDE + self.x)

    def slot(self, half, first, second):
        dx, dy = (first, second) if half == 0 else (second, first)
        return lax.rem(self.y + dy + SIDE, SIDE) * SIDE + lax.rem(self.x + dx + SIDE, SIDE)

    def up(self, step):
        return (lax.rem(self.z + step + DEPTH, DEPTH) * 2 + self.core, self.tp)

    def sibling(self):
        return (self.z * 2 + 1 - self.core, self.tp)


def await_bytes(ref, sem):
    pltpu.make_async_copy(ref, ref, sem).wait()


def push(src, dst, send, recv, device):
    pltpu.make_async_remote_copy(
        src_ref=src, dst_ref=dst, send_sem=send, recv_sem=recv, device_id=device, device_id_type=MESH
    ).start()


class Gather:
    def __init__(self, place, buf, sems, send, pieces):
        self.place, self.buf, self.sems, self.send, self.pieces = place, buf, sems, send, pieces

    def cols(self, piece):
        return pl.ds(piece * (HALF // self.pieces), HALF // self.pieces)

    def pass_on(self, piece, half, slot, axis, base):
        ref = self.buf.at[half, slot, :, self.cols(piece)]
        for index, step in enumerate(STEPS):
            push(ref, ref, self.send, self.sems.at[piece, half, base + index], self.place.along(axis, step))

    def start(self, piece):
        for base in (0, 3):
            for half in (0, 1):
                own = self.place.slot(half, 0, 0)
                self.pass_on(piece, half, own, half if base == 0 else 1 - half, base)

    def forward(self, piece):
        for index, step in enumerate(STEPS):
            for half in (0, 1):
                slot = self.place.slot(half, -step, 0)
                await_bytes(self.buf.at[half, slot, :, self.cols(piece)], self.sems.at[piece, half, index])
                self.pass_on(piece, half, slot, 1 - half, 3)

    def finish(self, piece, half):
        for index in range(3):
            await_bytes(self.buf.at[half, pl.ds(0, 4), :, self.cols(piece)], self.sems.at[piece, half, 3 + index])

    def close(self):
        await_bytes(self.buf.at[:, pl.ds(0, 15)], self.send)


class Scatter:
    def __init__(self, place, buf, landed, mid, own, landed2, sems, send, pieces):
        self.place, self.buf, self.landed, self.mid = place, buf, landed, mid
        self.own, self.landed2, self.sems, self.send, self.pieces = own, landed2, sems, send, pieces

    def cols(self, piece):
        return pl.ds(piece * (HALF // self.pieces), HALF // self.pieces)

    def at(self, half, first, second):
        a, b = (self.place.x, self.place.y) if half == 0 else (self.place.y, self.place.x)
        return lax.rem(a + first + SIDE, SIDE), lax.rem(b + second + SIDE, SIDE)

    def start(self, piece):
        for order, second in enumerate((2, 1, -1, 0)):
            for half in (0, 1):
                for index, step in enumerate(STEPS):
                    one, two = self.at(half, step, second)
                    push(
                        self.buf.at[half, one, two, :, self.cols(piece)],
                        self.landed.at[half, index, order, :, self.cols(piece)],
                        self.send.at[0],
                        self.sems.at[piece, half, order],
                        self.place.along(half, step),
                    )

    def sums(self, piece):
        cols = self.cols(piece)
        for order, second in enumerate((2, 1, -1, 0)):
            for half in (0, 1):
                await_bytes(self.landed.at[half, :, order, :, cols], self.sems.at[piece, half, order])
                one, two = self.at(half, 0, second)
                total = self.buf[half, one, two, :, cols].astype(F32)
                for index in range(3):
                    total = total + self.landed[half, index, order, :, cols].astype(F32)
                if second == 0:
                    self.own[half, :, cols] = total
                else:
                    self.mid[half, order, :, cols] = total.astype(BF16)
                    push(
                        self.mid.at[half, order, :, cols],
                        self.landed2.at[half, order, :, cols],
                        self.send.at[1],
                        self.sems.at[piece, half, 4],
                        self.place.along(1 - half, second),
                    )

    def result(self, piece, half):
        cols = self.cols(piece)
        await_bytes(self.landed2.at[half, :, :, cols], self.sems.at[piece, half, 4])
        total = self.own[half, :, cols]
        for index in range(3):
            total = total + self.landed2[half, index, :, cols].astype(F32)
        return total

    def close(self):
        await_bytes(self.buf.at[:, pl.ds(0, 3)], self.send.at[0])
        await_bytes(self.mid, self.send.at[1])


class Handoff:
    def __init__(self, place, buf, sems, sibling_sem, send, pieces):
        self.place, self.buf, self.sems, self.sibling_sem = place, buf, sems, sibling_sem
        self.send, self.pieces = send, pieces

    def slot(self, step):
        return lax.rem(self.place.z + step + DEPTH, DEPTH) * 2 + self.place.core

    def piece(self, slot, piece):
        return self.buf.at[slot, :, pl.ds(piece * (WIDTH // self.pieces), WIDTH // self.pieces)]

    def carries(self, number, piece, side):
        return number < 4 or (piece >= self.pieces // 2) == (side == 1)

    def onward(self, number, piece, side):
        way = (1, -1)[side]
        ref = self.piece(self.slot(-way * number), piece)
        push(ref, ref, self.send, self.sems.at[number, piece, side], self.place.up(way))

    def across(self, slot):
        ref = self.buf.at[slot]
        push(ref, ref, self.send, self.sibling_sem, self.place.sibling())

    def start(self, piece):
        for side in (0, 1):
            self.onward(0, piece, side)

    def step(self, number, piece):
        for side in (0, 1):
            if self.carries(number, piece, side):
                slot = self.slot(-(1, -1)[side] * number)
                await_bytes(self.piece(slot, piece), self.sems.at[number - 1, piece, side])
                if number < 4 and self.carries(number + 1, piece, side):
                    self.onward(number, piece, side)

    def share(self, number):
        if number == 0 or number == 4:
            self.across(self.slot(number))
        else:
            self.across(self.slot(number))
            self.across(self.slot(-number))

    def finish(self):
        await_bytes(self.buf.at[pl.ds(0, DEPTH)], self.sibling_sem)

    def close(self):
        await_bytes(self.buf.at[pl.ds(0, 15)], self.send)


class Update:
    def __init__(self, place, weights, outgoing, incoming, products, landed, sems, send):
        self.place, self.weights, self.outgoing, self.incoming = place, weights, outgoing, incoming
        self.products, self.landed, self.sems, self.send = products, landed, sems, send

    def positions(self, half):
        return (self.place.x, self.place.y) if half == 0 else (self.place.y, self.place.x)

    def start(self, attended):
        blocks = attended.reshape(SIDE, SIDE, ROWS, HEAD)
        self.outgoing[0] = blocks
        for one in range(SIDE):
            for two in range(SIDE):
                self.outgoing[1, one, two] = blocks[two, one]
        for half in (0, 1):
            second = self.positions(half)[1]
            for step in (2, 1, -1):
                push(
                    self.outgoing.at[half, lax.rem(second + step + SIDE, SIDE)],
                    self.incoming.at[half, second],
                    self.send.at[0],
                    self.sems.at[half, 0],
                    self.place.along(1 - half, step),
                )
            self.incoming[half, second] = self.outgoing[half, second]

    def multiply(self):
        for half in (0, 1):
            first = self.positions(half)[0]
            await_bytes(self.incoming.at[half, pl.ds(0, 3)], self.sems.at[half, 0])
            left = jnp.concatenate([self.incoming[half, other].reshape(4 * ROWS, HEAD) for other in range(SIDE)], 1)
            for piece in range(3):
                cols = pl.ds(piece * 512, 512)
                right = self.weights[half, :, :, :, cols].reshape(SIDE * HEAD, 512)
                product = jnp.dot(left, right, preferred_element_type=F32)
                self.products[half, :, :, cols] = product.astype(BF16).reshape(SIDE, ROWS, 512)
            for index, step in enumerate(STEPS):
                push(
                    self.products.at[half, lax.rem(first + step + SIDE, SIDE)],
                    self.landed.at[half, index],
                    self.send.at[1],
                    self.sems.at[half, 1],
                    self.place.along(half, step),
                )

    def result(self, half):
        first = self.positions(half)[0]
        await_bytes(self.landed.at[half], self.sems.at[half, 1])
        total = self.products[half, first].astype(F32)
        for index in range(3):
            total = total + self.landed[half, index].astype(F32)
        return total

    def close(self):
        await_bytes(self.outgoing.at[:, pl.ds(0, 3)], self.send.at[0])
        await_bytes(self.landed, self.send.at[1])


class ProjectionWeights:
    def __init__(self, place, buf, sems, sibling_sem, send):
        self.place, self.buf, self.sems, self.sibling_sem, self.send = place, buf, sems, sibling_sem, send

    def second(self, half, step):
        return lax.rem((self.place.y if half == 0 else self.place.x) + step + SIDE, SIDE)

    def start(self):
        for step_index, step in enumerate(STEPS):
            for half in (0, 1):
                ref = self.buf.at[half, self.second(half, 0), self.place.core]
                push(ref, ref, self.send, self.sems.at[half, step_index], self.place.along(1 - half, step))

    def share(self):
        for index, step in enumerate(STEPS):
            for half in (0, 1):
                ref = self.buf.at[half, self.second(half, -step), self.place.core]
                await_bytes(ref, self.sems.at[half, index])
                push(ref, ref, self.send, self.sibling_sem, self.place.sibling())

    def finish(self):
        await_bytes(self.buf.at[0, pl.ds(0, 3)], self.sibling_sem)

    def close(self):
        await_bytes(self.buf.at[:, pl.ds(0, 3)], self.send)


def kernel(
    prompt_ids,
    lengths,
    prompt_hbm,
    ctx_hbm,
    latent_hbm,
    imod_hbm,
    tmod_hbm,
    qkv_hbm,
    txt_hbm,
    gain,
    proj_hbm,
    out,
    prompt,
    ctx,
    latent,
    imod,
    tmod,
    qkv_w,
    txt_raw,
    txt_w,
    proj_w,
    local_sems,
    proj_sems,
    proj_sibling,
    proj_send,
    gathered,
    gather_sems,
    gather_sends,
    sc_buf,
    sc_landed,
    sc_mid,
    sc_own,
    sc_landed2,
    sc_sems,
    sc_sends,
    handed,
    hand_sems,
    hand_sibling,
    hand_send,
    up_outgoing,
    up_incoming,
    up_products,
    up_landed,
    up_sems,
    up_sends,
    x_state,
    rows_mod,
    text_in,
    text_kv,
    tscale,
):
    place = Place()

    barrier = pltpu.get_barrier_semaphore()
    partners = [place.along(axis, step) for axis in (0, 1) for step in STEPS]
    partners += [place.up(1), place.up(-1), place.sibling()]
    for partner in partners:
        pl.semaphore_signal(barrier, inc=1, device_id=partner, device_id_type=MESH)

    loads = []

    def load(src, dst):
        copy = pltpu.make_async_copy(src, dst, local_sems.at[len(loads)])
        copy.start()
        loads.append(copy)
        return copy

    load_prompt = load(prompt_hbm, prompt)
    load_ctx = load(ctx_hbm, ctx)
    load_latent = load(latent_hbm, latent)
    load_imod = load(imod_hbm, imod)
    load_proj = [
        load(
            proj_hbm.at[pl.ds(share * 64, 64), pl.ds(half * HALF, HALF)],
            proj_w.at[half, place.y if half == 0 else place.x, share],
        )
        for half in (0, 1)
        for share in (0, 1)
    ]
    load_txt = load(txt_hbm, txt_raw)
    load_tmod = load(tmod_hbm, tmod)
    load_qkv = [load(qkv_hbm.at[part], qkv_w.at[:, pl.ds(part * HEAD, HEAD)]) for part in range(3)]

    bounds, running = [], 0
    for image in range(4):
        running = running + lengths[0, image]
        bounds.append(running)

    def segments_of(row_ids):
        return sum((row_ids >= bound).astype(jnp.int32) for bound in bounds)

    rows_iota = lax.broadcasted_iota(jnp.int32, (16 * ROWS, 1), 0)
    lanes_iota = lax.broadcasted_iota(jnp.int32, (1, 16 * ROWS), 1)
    halves = (pl.ds(0, HALF), pl.ds(HALF, HALF))

    load_prompt.wait()
    row = lax.broadcasted_iota(jnp.int32, (256, 256), 0)
    col = lax.broadcasted_iota(jnp.int32, (256, 256), 1)
    ordered = []
    for half in (0, 1):
        block = row // 16
        owner = block if half == 1 else lax.rem(block, 4) * 4 + block // 4
        source = lax.rem(row // 4, 4) * 64 + owner * 4 + lax.rem(row, 4)
        order = (col == source).astype(BF16)
        ordered.append(jnp.dot(order, prompt[...], preferred_element_type=F32).astype(BF16))
    load_ctx.wait()
    for half in (0, 1):
        for piece in range(3):
            weight = ctx[:, pl.ds(half * HALF + piece * 512, 512)]
            product = jnp.dot(ordered[half], weight, preferred_element_type=F32)
            sc_buf[half, :, :, :, pl.ds(piece * 512, 512)] = product.astype(BF16).reshape(4, 4, ROWS, 512)

    pl.semaphore_wait(barrier, len(partners))
    text_scatter = Scatter(place, sc_buf, sc_landed, sc_mid, sc_own, sc_landed2, sc_sems, sc_sends, 1)
    text_scatter.start(0)

    load_imod.wait()
    mine = segments_of(place.tp * ROWS + lax.broadcasted_iota(jnp.int32, (ROWS, 1), 0))
    for step in (0, 1):
        for kind in range(3):
            rows = jnp.zeros((ROWS, WIDTH), F32)
            for image in range(4):
                rows = jnp.where(mine == image, imod[image, kind, step : step + 1, :], rows)
            rows_mod[step, kind] = rows + 1.0 if kind == 1 else rows
    load_latent.wait()
    x_state[...] = latent[...].astype(F32)

    def put_block(which, values):
        for half in (0, 1):
            gathered[which, half, place.tp] = values[:, half * HALF : (half + 1) * HALF]

    def put_image(step):
        values = layer_norm(x_state[...])
        put_block(step, (values * rows_mod[step, 1] + rows_mod[step, 0]).astype(BF16))

    def gather_of(which):
        return Gather(place, gathered.at[which], gather_sems.at[which], gather_sends.at[which], 1)

    put_image(0)
    text_scatter.sums(0)
    first_gather = gather_of(0)
    first_gather.start(0)

    handoff = Handoff(place, handed, hand_sems, hand_sibling, hand_send, 2)
    for half in (0, 1):
        handed[place.group, :, halves[half]] = text_scatter.result(0, half).astype(BF16)
        handoff.start(half)
    handoff.share(0)

    def hand_step(number):
        for piece in (0, 1):
            handoff.step(number, piece)
        handoff.share(number)

    first_gather.forward(0)
    hand_step(1)
    for copy in load_proj:
        copy.wait()
    weights = ProjectionWeights(place, proj_w, proj_sems, proj_sibling, proj_send)
    weights.start()

    load_txt.wait()
    unweave = (col == lax.rem(row, 128) * 2 + row // 128).astype(BF16)

    def part_weights(chunk, carry):
        mixed = txt_raw[pl.ds(pl.multiple_of(chunk * 256, 256), 256), :]
        parted = jnp.dot(unweave, mixed, preferred_element_type=F32).astype(BF16)
        at = pl.ds(pl.multiple_of(chunk * 128, 128), 128)
        txt_w[at, 0:HEAD] = parted[:128]
        txt_w[at, HEAD:] = parted[128:]
        return carry

    lax.fori_loop(0, 12, part_weights, 0)
    hand_step(2)
    lax.fori_loop(12, 24, part_weights, 0)
    hand_step(3)

    load_tmod.wait()
    slot_image = lax.broadcasted_iota(jnp.int32, (ROWS, 1), 0) // 4
    for step in (0, 1):
        for kind in (0, 1):
            rows = jnp.zeros((ROWS, WIDTH), F32)
            for image in range(4):
                rows = jnp.where(slot_image == image, tmod[image, step, kind : kind + 1, :], rows)
            tscale[step, kind] = rows + float(kind)
    hand_step(4)

    pick_row = lax.broadcasted_iota(jnp.int32, (ROWS, 256), 0)
    pick_col = lax.broadcasted_iota(jnp.int32, (ROWS, 256), 1)
    wanted = jnp.zeros((ROWS, 256), jnp.int32)
    for image in range(4):
        wanted = jnp.where(pick_row // 4 == image, prompt_ids[place.group * 4 + image] * 4, wanted)
    pick = (pick_col == wanted + lax.rem(pick_row, 4)).astype(BF16)
    handoff.finish()
    slot_text = jnp.concatenate(
        [
            jnp.dot(
                pick,
                handed[:, :, pl.ds(piece * 512, 512)].reshape(256, 512),
                preferred_element_type=F32,
            )
            for piece in range(6)
        ],
        axis=1,
    )
    put_block(2, layer_norm(slot_text).astype(BF16))
    text_gather = gather_of(2)
    text_gather.start(0)

    def project_image(which, gather):
        total = None
        for half in (0, 1):
            gather.finish(0, half)
            term = jnp.dot(
                gathered[which, half].reshape(256, HALF),
                qkv_w[pl.ds(half * HALF, HALF), :],
                preferred_element_type=F32,
            )
            total = term if total is None else total + term
        queries = rms_scale(total[:, :HEAD], gain[0:1]).astype(BF16)
        keys = rms_scale(total[:, HEAD : 2 * HEAD], gain[1:2]).astype(BF16)
        return queries, keys, total[:, 2 * HEAD :].astype(BF16)

    def project_text(step):
        for half in (0, 1):

            def modulate(owner, carry):
                normed = gathered[2, half, owner].astype(F32)
                scaled = normed * tscale[step, 1, :, halves[half]] + tscale[step, 0, :, halves[half]]
                text_in[half, owner] = scaled.astype(BF16)
                return carry

            lax.fori_loop(0, 16, modulate, 0)
        total = None
        for half in (0, 1):
            term = jnp.dot(
                text_in[half].reshape(256, HALF),
                txt_w[pl.ds(half * HALF, HALF), :],
                preferred_element_type=F32,
            )
            total = term if total is None else total + term
        text_kv[:, :HEAD] = rms_scale(total[:, :HEAD], gain[2:3]).astype(BF16)
        text_kv[:, HEAD:] = total[:, HEAD:].astype(BF16)

    segment_rows = segments_of(rows_iota)
    text_allowed = segment_rows == lax.rem(lanes_iota // 4, 4)
    image_allowed = segment_rows == segments_of(lanes_iota)

    def weigh(queries, keys, allowed):
        scores = lax.dot_general(queries, keys, (((1,), (1,)), ((), ())), preferred_element_type=F32)
        return jnp.where(allowed, jnp.exp(scores * HEAD**-0.5), 0.0)

    def attend(queries, keys, values):
        text_part = weigh(queries, text_kv[:, :HEAD], text_allowed)
        image_part = weigh(queries, keys, image_allowed)
        norm = jnp.sum(text_part, -1, keepdims=True) + jnp.sum(image_part, -1, keepdims=True)
        mixed = jnp.dot(text_part.astype(BF16), text_kv[:, HEAD:], preferred_element_type=F32)
        mixed = mixed + jnp.dot(image_part.astype(BF16), values, preferred_element_type=F32)
        return (mixed / norm).astype(BF16)

    def update_of(which):
        parts = (up_outgoing, up_incoming, up_products, up_landed, up_sems, up_sends)
        return Update(place, proj_w, *[ref.at[which] for ref in parts])

    def advance(step, update):
        for half in (0, 1):
            gate = rows_mod[step, 2, :, halves[half]]
            state = x_state[:, halves[half]] + gate * update.result(half)
            x_state[:, halves[half]] = state.astype(BF16).astype(F32)

    weights.share()
    text_gather.forward(0)
    for copy in load_qkv:
        copy.wait()
    queries, keys, values = project_image(0, first_gather)
    weights.finish()
    for half in (0, 1):
        text_gather.finish(0, half)
    project_text(0)

    first_update = update_of(0)
    first_update.start(attend(queries, keys, values))
    first_update.multiply()
    project_text(1)
    advance(0, first_update)

    put_image(1)
    second_gather = gather_of(1)
    second_gather.start(0)
    second_gather.forward(0)
    queries, keys, values = project_image(1, second_gather)
    second_update = update_of(1)
    second_update.start(attend(queries, keys, values))
    second_update.multiply()
    advance(1, second_update)
    out[...] = x_state[...].astype(BF16)

    for part in (text_scatter, first_gather, handoff, weights, text_gather, first_update, second_gather, second_update):
        part.close()


def on_device(
    prompt_states,
    ctx_weight,
    image_prompt,
    image_lengths,
    latents,
    img_mod,
    txt_mod,
    img_qkv,
    txt_kv,
    qk_gain,
    img_proj,
):
    anywhere = pl.BlockSpec(memory_space=pl.ANY)
    scalars = pl.BlockSpec(memory_space=pltpu.SMEM)
    in_vmem = pl.BlockSpec(memory_space=pltpu.VMEM)
    dma = pltpu.SemaphoreType.DMA
    block = (ROWS, HALF)
    denoised = pl.pallas_call(
        kernel,
        out_shape=jax.ShapeDtypeStruct((ROWS, WIDTH), BF16),
        in_specs=[scalars, scalars] + [anywhere] * 7 + [in_vmem, anywhere],
        out_specs=in_vmem,
        scratch_shapes=[
            pltpu.VMEM((256, 256), BF16),
            pltpu.VMEM((256, WIDTH), BF16),
            pltpu.VMEM((ROWS, WIDTH), BF16),
            pltpu.VMEM((4, 3, 2, WIDTH), F32),
            pltpu.VMEM((4, 2, 2, WIDTH), F32),
            pltpu.VMEM((WIDTH, 3 * HEAD), BF16),
            pltpu.VMEM((2 * WIDTH, HEAD), BF16),
            pltpu.VMEM((WIDTH, 2 * HEAD), BF16),
            pltpu.VMEM((2, 4, 2, 64, HALF), BF16),
            dma((13,)),
            dma((2, 3)),
            dma,
            dma,
            pltpu.VMEM((3, 2, 16) + block, BF16),
            dma((3, 1, 2, 6)),
            dma((3,)),
            pltpu.VMEM((2, 4, 4) + block, BF16),
            pltpu.VMEM((2, 3, 4) + block, BF16),
            pltpu.VMEM((2, 3) + block, BF16),
            pltpu.VMEM((2,) + block, F32),
            pltpu.VMEM((2, 3) + block, BF16),
            dma((1, 2, 5)),
            dma((2,)),
            pltpu.VMEM((16, ROWS, WIDTH), BF16),
            dma((4, 2, 2)),
            dma,
            dma,
            pltpu.VMEM((2, 2, 4, 4, ROWS, HEAD), BF16),
            pltpu.VMEM((2, 2, 4, 4, ROWS, HEAD), BF16),
            pltpu.VMEM((2, 2, 4) + block, BF16),
            pltpu.VMEM((2, 2, 3) + block, BF16),
            dma((2, 2, 2)),
            dma((2, 2)),
            pltpu.VMEM((ROWS, WIDTH), F32),
            pltpu.VMEM((2, 3, ROWS, WIDTH), F32),
            pltpu.VMEM((2, 16) + block, BF16),
            pltpu.VMEM((256, 2 * HEAD), BF16),
            pltpu.VMEM((2, 2, ROWS, WIDTH), F32),
        ],
        compiler_params=pltpu.CompilerParams(
            collective_id=0, has_side_effects=True, vmem_limit_bytes=56 * 1024 * 1024
        ),
    )(
        image_prompt,
        image_lengths,
        prompt_states.reshape(256, 256),
        ctx_weight,
        latents[0],
        jnp.transpose(img_mod[0], (0, 2, 1, 3)),
        txt_mod[0],
        jnp.transpose(img_qkv, (1, 0, 2)),
        txt_kv.reshape(2 * WIDTH, HEAD),
        qk_gain,
        img_proj,
    )
    return denoised[None]


def solution(mesh):
    placed = (
        P("group", None, "tp"),
        P("tp", None),
        P(),
        P("group", None),
        P("group", "tp", None),
        P("group", None, None, None, None),
        P("group", None, None, None, None),
        P(None, None, "tp"),
        P(None, None, "tp"),
        P(),
        P("tp", None),
    )
    return jax.shard_map(
        on_device, mesh=mesh, in_specs=placed, out_specs=P("group", "tp", None), check_vma=False
    )
```

```python
import functools

import jax
import jax.numpy as jnp
from jax import lax
from jax.experimental import pallas as pl
from jax.experimental.pallas import tpu as pltpu
from jax.sharding import PartitionSpec as P

MESH = pl.DeviceIdType.MESH
F32, BF16 = jnp.float32, jnp.bfloat16
WIDTH, HALF, QUARTER = 3072, 1536, 768
ROWS = 16
SIDE = 4
DEPTH = 8
HEAD = 128
STEPS = (1, -1, 2)
SECONDS = (2, 1, -1, 0)
PIECES = 2


def layer_norm(values):
    centered = values - jnp.mean(values, -1, keepdims=True)
    return centered * lax.rsqrt(jnp.mean(centered * centered, -1, keepdims=True) + 1e-6)


def rms_scale(values, gain_row):
    return values * lax.rsqrt(jnp.mean(values * values, -1, keepdims=True) + 1e-6) * gain_row


class Place:
    def __init__(self):
        self.group, self.tp = lax.axis_index("group"), lax.axis_index("tp")
        self.x, self.y = lax.rem(self.tp, SIDE), self.tp // SIDE
        self.z, self.core = self.group // 2, lax.rem(self.group, 2)

    def along(self, axis, step):
        if axis == 0:
            return (self.group, self.y * SIDE + lax.rem(self.x + step + SIDE, SIDE))
        return (self.group, lax.rem(self.y + step + SIDE, SIDE) * SIDE + self.x)

    def slot(self, half, first, second):
        dx, dy = (first, second) if half == 0 else (second, first)
        return lax.rem(self.y + dy + SIDE, SIDE) * SIDE + lax.rem(self.x + dx + SIDE, SIDE)

    def up(self, step):
        return (lax.rem(self.z + step + DEPTH, DEPTH) * 2 + self.core, self.tp)

    def sibling(self):
        return (self.z * 2 + 1 - self.core, self.tp)


def await_bytes(ref, sem):
    pltpu.make_async_copy(ref, ref, sem).wait()


def push(src, dst, send, recv, device):
    pltpu.make_async_remote_copy(
        src_ref=src, dst_ref=dst, send_sem=send, recv_sem=recv, device_id=device, device_id_type=MESH
    ).start()


class Gather:
    def __init__(self, place, buf, sems, send, pieces, relays=False):
        self.place, self.buf, self.sems, self.send, self.pieces = place, buf, sems, send, pieces
        self.relays = relays

    def cols(self, piece):
        return pl.ds(piece * (HALF // self.pieces), HALF // self.pieces)

    def pass_on(self, piece, half, slot, axis, base, steps):
        ref = self.buf.at[half, slot, :, self.cols(piece)]
        for index, step in steps:
            push(ref, ref, self.send, self.sems.at[piece, half, base + index], self.place.along(axis, step))

    def second(self, piece, half, slot):
        steps = list(enumerate(STEPS))
        self.pass_on(piece, half, slot, 1 - half, 3, steps[:2] if self.relays else steps)

    def start(self, piece):
        for half in (0, 1):
            self.pass_on(piece, half, self.place.slot(half, 0, 0), half, 0, list(enumerate(STEPS)))
        for half in (0, 1):
            self.second(piece, half, self.place.slot(half, 0, 0))

    def forward(self, piece):
        for index, step in enumerate(STEPS):
            for half in (0, 1):
                slot = self.place.slot(half, -step, 0)
                await_bytes(self.buf.at[half, slot, :, self.cols(piece)], self.sems.at[piece, half, index])
                self.second(piece, half, slot)

    def await_source(self, piece, half, index):
        await_bytes(self.buf.at[half, pl.ds(0, 4), :, self.cols(piece)], self.sems.at[piece, half, 3 + index])

    def relay(self, piece):
        for index, firsts in enumerate(((0, 1), (2, 3))):
            step = STEPS[index]
            for half in (0, 1):
                self.await_source(piece, half, index)
                for first in firsts:
                    slot = self.place.slot(half, first, -step)
                    ref = self.buf.at[half, slot, :, self.cols(piece)]
                    push(ref, ref, self.send, self.sems.at[piece, half, 5], self.place.along(1 - half, step))

    def finish(self, piece, half):
        for index in range(2 if self.relays else 0, 3):
            self.await_source(piece, half, index)

    def close(self):
        await_bytes(self.buf.at[:, pl.ds(0, 15)], self.send)


class Scatter:
    def __init__(self, place, buf, landed, mid, own, landed2, sems, send, pieces):
        self.place, self.buf, self.landed, self.mid = place, buf, landed, mid
        self.own, self.landed2, self.sems, self.send, self.pieces = own, landed2, sems, send, pieces

    def cols(self, piece):
        return pl.ds(piece * (HALF // self.pieces), HALF // self.pieces)

    def at(self, half, first, second):
        a, b = (self.place.x, self.place.y) if half == 0 else (self.place.y, self.place.x)
        return lax.rem(a + first + SIDE, SIDE), lax.rem(b + second + SIDE, SIDE)

    def start(self, piece, orders):
        for order in orders:
            second = SECONDS[order]
            for half in (0, 1):
                for index, step in enumerate(STEPS):
                    one, two = self.at(half, step, second)
                    push(
                        self.buf.at[half, one, two, :, self.cols(piece)],
                        self.landed.at[half, index, order, :, self.cols(piece)],
                        self.send.at[0],
                        self.sems.at[piece, half, order],
                        self.place.along(half, step),
                    )

    def sums(self, piece, orders):
        cols = self.cols(piece)
        for order in orders:
            second = SECONDS[order]
            for half in (0, 1):
                await_bytes(self.landed.at[half, :, order, :, cols], self.sems.at[piece, half, order])
                one, two = self.at(half, 0, second)
                total = self.buf[half, one, two, :, cols].astype(F32)
                for index in range(3):
                    total = total + self.landed[half, index, order, :, cols].astype(F32)
                if second == 0:
                    self.own[half, :, cols] = total
                else:
                    self.mid[half, order, :, cols] = total.astype(BF16)
                    push(
                        self.mid.at[half, order, :, cols],
                        self.landed2.at[half, order, :, cols],
                        self.send.at[1],
                        self.sems.at[piece, half, 4],
                        self.place.along(1 - half, second),
                    )

    def result(self, piece, half):
        cols = self.cols(piece)
        await_bytes(self.landed2.at[half, :, :, cols], self.sems.at[piece, half, 4])
        total = self.own[half, :, cols]
        for index in range(3):
            total = total + self.landed2[half, index, :, cols].astype(F32)
        return total

    def close(self):
        await_bytes(self.buf.at[:, pl.ds(0, 3)], self.send.at[0])
        await_bytes(self.mid, self.send.at[1])


class Handoff:
    def __init__(self, place, buf, sems, sibling_sems, send):
        self.place, self.buf, self.sems, self.sibling_sems, self.send = place, buf, sems, sibling_sems, send

    def slot(self, step):
        return lax.rem(self.place.z + step + DEPTH, DEPTH) * 2 + self.place.core

    def carries(self, number, piece, side):
        return number < 4 or piece == side

    def onward(self, number, piece, side):
        way = (1, -1)[side]
        ref = self.buf.at[piece, self.slot(-way * number)]
        push(ref, ref, self.send, self.sems.at[number, piece, side], self.place.up(way))

    def across(self, piece, slot):
        ref = self.buf.at[piece, slot]
        push(ref, ref, self.send, self.sibling_sems.at[piece], self.place.sibling())

    def start(self, piece):
        for side in (0, 1):
            self.onward(0, piece, side)
        self.across(piece, self.slot(0))

    def step(self, number, piece):
        for side in (0, 1):
            if self.carries(number, piece, side):
                slot = self.slot(-(1, -1)[side] * number)
                await_bytes(self.buf.at[piece, slot], self.sems.at[number - 1, piece, side])
                if number < 4 and self.carries(number + 1, piece, side):
                    self.onward(number, piece, side)
                self.across(piece, slot)

    def finish(self, piece):
        await_bytes(self.buf.at[piece, pl.ds(0, DEPTH)], self.sibling_sems.at[piece])

    def close(self):
        await_bytes(self.buf.at[:, pl.ds(0, 15)], self.send)


class Update:
    def __init__(self, place, weights, outgoing, incoming, products, landed, sems, send):
        self.place, self.weights, self.outgoing, self.incoming = place, weights, outgoing, incoming
        self.products, self.landed, self.sems, self.send = products, landed, sems, send

    def positions(self, half):
        return (self.place.x, self.place.y) if half == 0 else (self.place.y, self.place.x)

    def start(self, attended):
        blocks = attended.reshape(SIDE, SIDE, ROWS, HEAD)
        self.outgoing[0] = blocks
        for one in range(SIDE):
            for two in range(SIDE):
                self.outgoing[1, one, two] = blocks[two, one]
        for half in (0, 1):
            second = self.positions(half)[1]
            for step in (2, 1, -1):
                push(
                    self.outgoing.at[half, lax.rem(second + step + SIDE, SIDE)],
                    self.incoming.at[half, second],
                    self.send.at[0],
                    self.sems.at[half, 0],
                    self.place.along(1 - half, step),
                )
            self.incoming[half, second] = self.outgoing[half, second]

    def multiply(self):
        for half in (0, 1):
            first = self.positions(half)[0]
            await_bytes(self.incoming.at[half, pl.ds(0, 3)], self.sems.at[half, 0])
            left = jnp.concatenate([self.incoming[half, other].reshape(4 * ROWS, HEAD) for other in range(SIDE)], 1)
            for piece in range(3):
                cols = pl.ds(piece * 512, 512)
                right = self.weights[half, :, :, :, cols].reshape(SIDE * HEAD, 512)
                product = jnp.dot(left, right, preferred_element_type=F32)
                self.products[half, :, :, cols] = product.astype(BF16).reshape(SIDE, ROWS, 512)
            for index, step in enumerate(STEPS):
                push(
                    self.products.at[half, lax.rem(first + step + SIDE, SIDE)],
                    self.landed.at[half, index],
                    self.send.at[1],
                    self.sems.at[half, 1],
                    self.place.along(half, step),
                )

    def result(self, half):
        first = self.positions(half)[0]
        await_bytes(self.landed.at[half], self.sems.at[half, 1])
        total = self.products[half, first].astype(F32)
        for index in range(3):
            total = total + self.landed[half, index].astype(F32)
        return total

    def close(self):
        await_bytes(self.outgoing.at[:, pl.ds(0, 3)], self.send.at[0])
        await_bytes(self.landed, self.send.at[1])


class ProjectionWeights:
    def __init__(self, place, buf, sems, sibling_sem, send):
        self.place, self.buf, self.sems, self.sibling_sem, self.send = place, buf, sems, sibling_sem, send

    def second(self, half, step):
        return lax.rem((self.place.y if half == 0 else self.place.x) + step + SIDE, SIDE)

    def share(self, half, step):
        ref = self.buf.at[half, self.second(half, step), self.place.core]
        push(ref, ref, self.send, self.sibling_sem, self.place.sibling())

    def start(self):
        for index, step in enumerate((1, -1)):
            for half in (0, 1):
                ref = self.buf.at[half, self.second(half, 0), self.place.core]
                push(ref, ref, self.send, self.sems.at[half, index], self.place.along(1 - half, step))

    def relay(self):
        for index, step in enumerate((1, -1)):
            for half in (0, 1):
                ref = self.buf.at[half, self.second(half, -step), self.place.core]
                await_bytes(ref, self.sems.at[half, index])
                part = self.buf.at[half, self.second(half, -step), self.place.core, pl.ds(index * 32, 32)]
                push(part, part, self.send, self.sems.at[half, 2 + index], self.place.along(1 - half, step))
                self.share(half, -step)

    def last(self):
        for half in (0, 1):
            for index in (0, 1):
                part = self.buf.at[half, self.second(half, 2), self.place.core, pl.ds(index * 32, 32)]
                await_bytes(part, self.sems.at[half, 2 + index])
            self.share(half, 2)

    def finish(self):
        await_bytes(self.buf.at[0, pl.ds(0, 3)], self.sibling_sem)

    def close(self):
        await_bytes(self.buf.at[:, pl.ds(0, 3)], self.send)


def kernel(
    prompt_ids,
    lengths,
    prompt_hbm,
    ctx_hbm,
    latent_hbm,
    imod_hbm,
    tmod_hbm,
    qkv_hbm,
    txt_hbm,
    gain,
    proj_hbm,
    out,
    prompt,
    ctx,
    latent,
    imod,
    tmod,
    qkv_w,
    txt_raw,
    txt_w,
    proj_w,
    local_sems,
    proj_sems,
    proj_sibling,
    proj_send,
    gathered,
    gather_sems,
    gather_sends,
    sc_buf,
    sc_landed,
    sc_mid,
    sc_own,
    sc_landed2,
    sc_sems,
    sc_sends,
    handed,
    hand_sems,
    hand_siblings,
    hand_send,
    up_outgoing,
    up_incoming,
    up_products,
    up_landed,
    up_sems,
    up_sends,
    x_state,
    rows_mod,
    text_in,
    text_kv,
    tscale,
    text_stats,
):
    place = Place()

    barrier = pltpu.get_barrier_semaphore()
    partners = [place.along(axis, step) for axis in (0, 1) for step in STEPS]
    partners += [place.up(1), place.up(-1), place.sibling()]
    for partner in partners:
        pl.semaphore_signal(barrier, inc=1, device_id=partner, device_id_type=MESH)

    loads = []

    def load(src, dst):
        copy = pltpu.make_async_copy(src, dst, local_sems.at[len(loads)])
        copy.start()
        loads.append(copy)
        return copy

    def part_of(half, piece):
        return pl.ds(half * HALF + piece * QUARTER, QUARTER)

    load_prompt = load(prompt_hbm, prompt)
    load_ctx = [
        [load(ctx_hbm.at[:, part_of(half, piece)], ctx.at[:, part_of(half, piece)]) for half in (0, 1)]
        for piece in range(PIECES)
    ]
    load_latent = load(latent_hbm, latent)
    load_imod = load(imod_hbm, imod)

    bounds, running = [], 0
    for image in range(4):
        running = running + lengths[0, image]
        bounds.append(running)

    def segments_of(row_ids):
        return sum((row_ids >= bound).astype(jnp.int32) for bound in bounds)

    rows_iota = lax.broadcasted_iota(jnp.int32, (16 * ROWS, 1), 0)
    lanes_iota = lax.broadcasted_iota(jnp.int32, (1, 16 * ROWS), 1)
    halves = (pl.ds(0, HALF), pl.ds(HALF, HALF))

    load_prompt.wait()
    row = lax.broadcasted_iota(jnp.int32, (256, 256), 0)
    col = lax.broadcasted_iota(jnp.int32, (256, 256), 1)
    ordered = []
    for half in (0, 1):
        block = row // 16
        owner = block if half == 1 else lax.rem(block, 4) * 4 + block // 4
        source = lax.rem(row // 4, 4) * 64 + owner * 4 + lax.rem(row, 4)
        order = (col == source).astype(BF16)
        ordered.append(jnp.dot(order, prompt[...], preferred_element_type=F32).astype(BF16))
    text_scatter = Scatter(place, sc_buf, sc_landed, sc_mid, sc_own, sc_landed2, sc_sems, sc_sends, PIECES)
    everything = range(len(SECONDS))

    def embed(piece):
        for half in (0, 1):
            load_ctx[piece][half].wait()
            product = jnp.dot(ordered[half], ctx[:, part_of(half, piece)], preferred_element_type=F32)
            cols = text_scatter.cols(piece)
            sc_buf[half, :, :, :, cols] = product.astype(BF16).reshape(4, 4, ROWS, QUARTER)

    embed(0)
    pl.semaphore_wait(barrier, len(partners))
    text_scatter.start(0, everything)
    embed(1)
    load_proj = [
        load(
            proj_hbm.at[pl.ds(share * 64, 64), pl.ds(half * HALF, HALF)],
            proj_w.at[half, place.y if half == 0 else place.x, share],
        )
        for half in (0, 1)
        for share in (0, 1)
    ]
    load_txt = load(txt_hbm, txt_raw)
    load_tmod = load(tmod_hbm, tmod)
    load_qkv = [load(qkv_hbm.at[part], qkv_w.at[:, pl.ds(part * HEAD, HEAD)]) for part in range(3)]

    load_imod.wait()
    mine = segments_of(place.tp * ROWS + lax.broadcasted_iota(jnp.int32, (ROWS, 1), 0))
    for step in (0, 1):
        for kind in range(3):
            rows = jnp.zeros((ROWS, WIDTH), F32)
            for image in range(4):
                rows = jnp.where(mine == image, imod[image, kind, step : step + 1, :], rows)
            rows_mod[step, kind] = rows + 1.0 if kind == 1 else rows
    load_latent.wait()
    x_state[...] = latent[...].astype(F32)

    def put_block(which, values):
        for half in (0, 1):
            gathered[which, half, place.tp] = values[:, half * HALF : (half + 1) * HALF]

    def put_image(step):
        values = layer_norm(x_state[...])
        put_block(step, (values * rows_mod[step, 1] + rows_mod[step, 0]).astype(BF16))

    def gather_of(which, pieces=1, relays=False):
        return Gather(place, gathered.at[which], gather_sems.at[which], gather_sends.at[which], pieces, relays)

    put_image(0)
    for order in everything:
        text_scatter.sums(0, (order,))
        text_scatter.start(1, (order,))

    handoff = Handoff(place, handed, hand_sems, hand_siblings, hand_send)

    def hand_out(piece):
        for half in (0, 1):
            cols = pl.ds(half * QUARTER, QUARTER)
            handed[piece, place.group, :, cols] = text_scatter.result(piece, half).astype(BF16)
        handoff.start(piece)

    text_scatter.sums(1, everything[:3])
    hand_out(0)
    text_scatter.sums(1, everything[3:])
    first_gather = gather_of(0, relays=True)
    first_gather.start(0)
    hand_out(1)
    handoff.step(1, 0)
    first_gather.forward(0)
    handoff.step(1, 1)
    handoff.step(2, 0)
    for copy in load_proj:
        copy.wait()
    weights = ProjectionWeights(place, proj_w, proj_sems, proj_sibling, proj_send)
    weights.start()

    load_txt.wait()
    unweave = (col == lax.rem(row, 128) * 2 + row // 128).astype(BF16)

    def part_weights(chunk, carry):
        mixed = txt_raw[pl.ds(pl.multiple_of(chunk * 256, 256), 256), :]
        parted = jnp.dot(unweave, mixed, preferred_element_type=F32).astype(BF16)
        at = pl.ds(pl.multiple_of(chunk * 128, 128), 128)
        txt_w[at, 0:HEAD] = parted[:128]
        txt_w[at, HEAD:] = parted[128:]
        return carry

    lax.fori_loop(0, 24, part_weights, 0)
    handoff.step(2, 1)
    handoff.step(3, 0)
    first_gather.relay(0)

    load_tmod.wait()
    slot_image = lax.broadcasted_iota(jnp.int32, (ROWS, 1), 0) // 4
    for step in (0, 1):
        for kind in (0, 1):
            rows = jnp.zeros((ROWS, WIDTH), F32)
            for image in range(4):
                rows = jnp.where(slot_image == image, tmod[image, step, kind : kind + 1, :], rows)
            tscale[step, kind] = rows + float(kind)
    handoff.step(3, 1)
    handoff.step(4, 0)
    weights.relay()

    pick_row = lax.broadcasted_iota(jnp.int32, (ROWS, 256), 0)
    pick_col = lax.broadcasted_iota(jnp.int32, (ROWS, 256), 1)
    wanted = jnp.zeros((ROWS, 256), jnp.int32)
    for image in range(4):
        wanted = jnp.where(pick_row // 4 == image, prompt_ids[place.group * 4 + image] * 4, wanted)
    pick = (pick_col == wanted + lax.rem(pick_row, 4)).astype(BF16)
    text_gather = gather_of(2, PIECES)

    def take_text(piece):
        handoff.finish(piece)
        for half in (0, 1):
            held = handed[piece, :, :, pl.ds(half * QUARTER, QUARTER)].reshape(256, QUARTER)
            taken = jnp.dot(pick, held, preferred_element_type=F32).astype(BF16)
            gathered[2, half, place.tp, :, text_gather.cols(piece)] = taken
        text_gather.start(piece)

    take_text(0)
    handoff.step(4, 1)
    take_text(1)
    text_gather.forward(0)
    weights.last()
    text_gather.forward(1)

    def project_image(which, gather):
        total = None
        for half in (0, 1):
            gather.finish(0, half)
            term = jnp.dot(
                gathered[which, half].reshape(256, HALF),
                qkv_w[pl.ds(half * HALF, HALF), :],
                preferred_element_type=F32,
            )
            total = term if total is None else total + term
        queries = rms_scale(total[:, :HEAD], gain[0:1]).astype(BF16)
        keys = rms_scale(total[:, HEAD : 2 * HEAD], gain[1:2]).astype(BF16)
        return queries, keys, total[:, 2 * HEAD :].astype(BF16)

    def project_text(step):
        for half in (0, 1):

            def modulate(owner, carry):
                center, scale = text_stats[0, owner], text_stats[1, owner]
                normed = (gathered[2, half, owner].astype(F32) - center[:, :1]) * scale[:, :1]
                scaled = normed * tscale[step, 1, :, halves[half]] + tscale[step, 0, :, halves[half]]
                text_in[half, owner] = scaled.astype(BF16)
                return carry

            lax.fori_loop(0, 16, modulate, 0)
        total = None
        for half in (0, 1):
            term = jnp.dot(
                text_in[half].reshape(256, HALF),
                txt_w[pl.ds(half * HALF, HALF), :],
                preferred_element_type=F32,
            )
            total = term if total is None else total + term
        text_kv[:, :HEAD] = rms_scale(total[:, :HEAD], gain[2:3]).astype(BF16)
        text_kv[:, HEAD:] = total[:, HEAD:].astype(BF16)

    segment_rows = segments_of(rows_iota)
    text_allowed = segment_rows == lax.rem(lanes_iota // 4, 4)
    image_allowed = segment_rows == segments_of(lanes_iota)

    def weigh(queries, keys, allowed):
        scores = lax.dot_general(queries, keys, (((1,), (1,)), ((), ())), preferred_element_type=F32)
        return jnp.where(allowed, jnp.exp(scores * HEAD**-0.5), 0.0)

    def attend(queries, keys, values):
        text_part = weigh(queries, text_kv[:, :HEAD], text_allowed)
        image_part = weigh(queries, keys, image_allowed)
        norm = jnp.sum(text_part, -1, keepdims=True) + jnp.sum(image_part, -1, keepdims=True)
        mixed = jnp.dot(text_part.astype(BF16), text_kv[:, HEAD:], preferred_element_type=F32)
        mixed = mixed + jnp.dot(image_part.astype(BF16), values, preferred_element_type=F32)
        return (mixed / norm).astype(BF16)

    def update_of(which):
        parts = (up_outgoing, up_incoming, up_products, up_landed, up_sems, up_sends)
        return Update(place, proj_w, *[ref.at[which] for ref in parts])

    def advance(step, update):
        for half in (0, 1):
            gate = rows_mod[step, 2, :, halves[half]]
            state = x_state[:, halves[half]] + gate * update.result(half)
            x_state[:, halves[half]] = state.astype(BF16).astype(F32)

    for copy in load_qkv:
        copy.wait()
    queries, keys, values = project_image(0, first_gather)
    weights.finish()

    means, squares = [], []
    for piece in range(PIECES):
        parts = []
        for half in (0, 1):
            text_gather.finish(piece, half)
            parts.append(gathered[2, half, :, :, text_gather.cols(piece)].reshape(256, QUARTER).astype(F32))
        mean = sum(jnp.sum(part, -1, keepdims=True) for part in parts) / HALF
        means.append(mean)
        squares.append(sum(jnp.sum((part - mean) * (part - mean), -1, keepdims=True) for part in parts))
    gap = (means[0] - means[1]) * 0.5
    deviation = lax.rsqrt((squares[0] + squares[1]) / WIDTH + gap * gap + 1e-6)
    text_stats[0] = jnp.broadcast_to((means[0] + means[1]) * 0.5, (256, HEAD)).reshape(16, ROWS, HEAD)
    text_stats[1] = jnp.broadcast_to(deviation, (256, HEAD)).reshape(16, ROWS, HEAD)
    project_text(0)

    first_update = update_of(0)
    first_update.start(attend(queries, keys, values))
    first_update.multiply()
    project_text(1)
    advance(0, first_update)

    put_image(1)
    second_gather = gather_of(1)
    second_gather.start(0)
    second_gather.forward(0)
    queries, keys, values = project_image(1, second_gather)
    second_update = update_of(1)
    second_update.start(attend(queries, keys, values))
    second_update.multiply()
    advance(1, second_update)
    out[...] = x_state[...].astype(BF16)

    for part in (text_scatter, first_gather, handoff, weights, text_gather, first_update, second_gather, second_update):
        part.close()


def on_device(
    prompt_states,
    ctx_weight,
    image_prompt,
    image_lengths,
    latents,
    img_mod,
    txt_mod,
    img_qkv,
    txt_kv,
    qk_gain,
    img_proj,
):
    anywhere = pl.BlockSpec(memory_space=pl.ANY)
    scalars = pl.BlockSpec(memory_space=pltpu.SMEM)
    in_vmem = pl.BlockSpec(memory_space=pltpu.VMEM)
    dma = pltpu.SemaphoreType.DMA
    block = (ROWS, HALF)
    denoised = pl.pallas_call(
        kernel,
        out_shape=jax.ShapeDtypeStruct((ROWS, WIDTH), BF16),
        in_specs=[scalars, scalars] + [anywhere] * 7 + [in_vmem, anywhere],
        out_specs=in_vmem,
        scratch_shapes=[
            pltpu.VMEM((256, 256), BF16),
            pltpu.VMEM((256, WIDTH), BF16),
            pltpu.VMEM((ROWS, WIDTH), BF16),
            pltpu.VMEM((4, 3, 2, WIDTH), F32),
            pltpu.VMEM((4, 2, 2, WIDTH), F32),
            pltpu.VMEM((WIDTH, 3 * HEAD), BF16),
            pltpu.VMEM((2 * WIDTH, HEAD), BF16),
            pltpu.VMEM((WIDTH, 2 * HEAD), BF16),
            pltpu.VMEM((2, 4, 2, 64, HALF), BF16),
            dma((16,)),
            dma((2, 4)),
            dma,
            dma,
            pltpu.VMEM((3, 2, 16) + block, BF16),
            dma((3, PIECES, 2, 6)),
            dma((3,)),
            pltpu.VMEM((2, 4, 4) + block, BF16),
            pltpu.VMEM((2, 3, 4) + block, BF16),
            pltpu.VMEM((2, 3) + block, BF16),
            pltpu.VMEM((2,) + block, F32),
            pltpu.VMEM((2, 3) + block, BF16),
            dma((PIECES, 2, 5)),
            dma((2,)),
            pltpu.VMEM((PIECES, 16) + block, BF16),
            dma((4, PIECES, 2)),
            dma((PIECES,)),
            dma,
            pltpu.VMEM((2, 2, 4, 4, ROWS, HEAD), BF16),
            pltpu.VMEM((2, 2, 4, 4, ROWS, HEAD), BF16),
            pltpu.VMEM((2, 2, 4) + block, BF16),
            pltpu.VMEM((2, 2, 3) + block, BF16),
            dma((2, 2, 2)),
            dma((2, 2)),
            pltpu.VMEM((ROWS, WIDTH), F32),
            pltpu.VMEM((2, 3, ROWS, WIDTH), F32),
            pltpu.VMEM((2, 16) + block, BF16),
            pltpu.VMEM((256, 2 * HEAD), BF16),
            pltpu.VMEM((2, 2, ROWS, WIDTH), F32),
            pltpu.VMEM((2, 16, ROWS, HEAD), F32),
        ],
        compiler_params=pltpu.CompilerParams(
            collective_id=0, has_side_effects=True, vmem_limit_bytes=56 * 1024 * 1024
        ),
    )(
        image_prompt,
        image_lengths,
        prompt_states.reshape(256, 256),
        ctx_weight,
        latents[0],
        jnp.transpose(img_mod[0], (0, 2, 1, 3)),
        txt_mod[0],
        jnp.transpose(img_qkv, (1, 0, 2)),
        txt_kv.reshape(2 * WIDTH, HEAD),
        qk_gain,
        img_proj,
    )
    return denoised[None]


def solution(mesh):
    placed = (
        P("group", None, "tp"),
        P("tp", None),
        P(),
        P("group", None),
        P("group", "tp", None),
        P("group", None, None, None, None),
        P("group", None, None, None, None),
        P(None, None, "tp"),
        P(None, None, "tp"),
        P(),
        P("tp", None),
    )
    return jax.shard_map(
        on_device, mesh=mesh, in_specs=placed, out_specs=P("group", "tp", None), check_vma=False
    )
```

```python
import functools

import jax
import jax.numpy as jnp
from jax import lax
from jax.experimental import pallas as pl
from jax.experimental.pallas import tpu as pltpu
from jax.sharding import PartitionSpec as P

MESH = pl.DeviceIdType.MESH
F32, BF16 = jnp.float32, jnp.bfloat16
WIDTH, HALF = 3072, 1536
ROWS = 16
SIDE = 4
DEPTH = 8
HEAD = 128
STEPS = (1, -1, 2)


def layer_norm(values):
    centered = values - jnp.mean(values, -1, keepdims=True)
    return centered * lax.rsqrt(jnp.mean(centered * centered, -1, keepdims=True) + 1e-6)


def rms_scale(values, gain_row):
    return values * lax.rsqrt(jnp.mean(values * values, -1, keepdims=True) + 1e-6) * gain_row


class Place:
    def __init__(self):
        self.group, self.tp = lax.axis_index("group"), lax.axis_index("tp")
        self.x, self.y = lax.rem(self.tp, SIDE), self.tp // SIDE
        self.z, self.core = self.group // 2, lax.rem(self.group, 2)

    def along(self, axis, step):
        if axis == 0:
            return (self.group, self.y * SIDE + lax.rem(self.x + step + SIDE, SIDE))
        return (self.group, lax.rem(self.y + step + SIDE, SIDE) * SIDE + self.x)

    def slot(self, half, first, second):
        dx, dy = (first, second) if half == 0 else (second, first)
        return lax.rem(self.y + dy + SIDE, SIDE) * SIDE + lax.rem(self.x + dx + SIDE, SIDE)

    def up(self, step):
        return (lax.rem(self.z + step + DEPTH, DEPTH) * 2 + self.core, self.tp)

    def sibling(self):
        return (self.z * 2 + 1 - self.core, self.tp)


def await_bytes(ref, sem):
    pltpu.make_async_copy(ref, ref, sem).wait()


def push(src, dst, send, recv, device):
    pltpu.make_async_remote_copy(
        src_ref=src, dst_ref=dst, send_sem=send, recv_sem=recv, device_id=device, device_id_type=MESH
    ).start()


class Gather:
    def __init__(self, place, buf, sems, send):
        self.place, self.buf, self.sems, self.send = place, buf, sems, send

    def pass_on(self, half, first, second, axis, step, sem):
        ref = self.buf.at[half, self.place.slot(half, first, second)]
        push(ref, ref, self.send, self.sems.at[half, sem], self.place.along(axis, step))

    def start(self):
        for index in (2, 0, 1):
            for half in (0, 1):
                self.pass_on(half, 0, 0, half, STEPS[index], index)
            if index == 2:
                for half in (0, 1):
                    self.pass_on(half, 0, 0, 1 - half, 2, 5)
        for index in (0, 1):
            for half in (0, 1):
                self.pass_on(half, 0, 0, 1 - half, STEPS[index], 3 + index)

    def forward(self):
        for index in (0, 1, 2):
            step = STEPS[index]
            for half in (0, 1):
                await_bytes(self.buf.at[half, self.place.slot(half, -step, 0)], self.sems.at[half, index])
                for other in (0, 1):
                    self.pass_on(half, -step, 0, 1 - half, STEPS[other], 6 + other)
            if index == 1:
                for half in (0, 1):
                    await_bytes(self.buf.at[half, self.place.slot(half, 0, 2)], self.sems.at[half, 5])
                    for onward in (2, 1, -1):
                        self.pass_on(half, 0, 2, half, onward, 8)

    def finish(self, half):
        for index in (0, 1):
            await_bytes(self.buf.at[half, self.place.slot(half, 0, -STEPS[index])], self.sems.at[half, 3 + index])
        for index in (6, 7, 8):
            await_bytes(self.buf.at[half, pl.ds(0, 3)], self.sems.at[half, index])

    def close(self):
        await_bytes(self.buf.at[:, pl.ds(0, 15)], self.send)


class Scatter:
    def __init__(self, place, buf, sides, line, mid, landed, sems, send, sent):
        self.place, self.buf, self.sides, self.line = place, buf, sides, line
        self.mid, self.landed, self.sems, self.send, self.sent = mid, landed, sems, send, sent

    def block(self, half, first, second):
        a, b = (self.place.x, self.place.y) if half == 0 else (self.place.y, self.place.x)
        return self.buf.at[half, lax.rem(a + first + SIDE, SIDE), lax.rem(b + second + SIDE, SIDE)]

    def start(self):
        for index in (2, 0, 1):
            for half in (0, 1):
                push(
                    self.block(half, STEPS[index], 2),
                    self.line.at[half, index],
                    self.send.at[0],
                    self.sems.at[half, 3],
                    self.place.along(half, STEPS[index]),
                )
            for half in (0, 1):
                for side in (0, 1):
                    push(
                        self.block(half, STEPS[index], STEPS[side]),
                        self.sides.at[half, index, side],
                        self.send.at[0],
                        self.sems.at[half, index],
                        self.place.along(1 - half, STEPS[side]),
                    )
        for half in (0, 1):
            for side in (0, 1):
                push(
                    self.block(half, 0, STEPS[side]),
                    self.landed.at[half, 3 + side],
                    self.send.at[0],
                    self.sems.at[half, 4],
                    self.place.along(1 - half, STEPS[side]),
                )

    def sums(self):
        for index in (2, 3, 0, 1):
            for half in (0, 1):
                if index < 3:
                    landed, own, axis, step = self.sides.at[half, index], (STEPS[index], 0), half, STEPS[index]
                    count, goal = 2, index
                else:
                    landed, own, axis, step = self.line.at[half], (0, 2), 1 - half, 2
                    count, goal = 3, 5
                await_bytes(landed, self.sems.at[half, index])
                total = self.block(half, *own)[...].astype(F32)
                for other in range(count):
                    total = total + landed[other].astype(F32)
                self.mid[half, index] = total.astype(BF16)
                push(
                    self.mid.at[half, index],
                    self.landed.at[half, goal],
                    self.send.at[1],
                    self.sems.at[half, 5],
                    self.place.along(axis, step),
                )

    def result(self, half):
        await_bytes(self.landed.at[half, pl.ds(0, 2)], self.sems.at[half, 4])
        await_bytes(self.landed.at[half, pl.ds(0, 4)], self.sems.at[half, 5])
        total = self.block(half, 0, 0)[...].astype(F32)
        for other in range(6):
            total = total + self.landed[half, other].astype(F32)
        return total

    def close(self):
        await_bytes(self.sent, self.send.at[0])
        await_bytes(self.mid, self.send.at[1])


class Handoff:
    def __init__(self, place, buf, sems, sibling_sems, send):
        self.place, self.buf, self.sems, self.sibling_sems, self.send = place, buf, sems, sibling_sems, send

    def slot(self, step):
        return lax.rem(self.place.z + step + DEPTH, DEPTH) * 2 + self.place.core

    def onward(self, piece, side, held, goal):
        way = (1, -1)[side]
        ref = self.buf.at[piece, self.slot(-way * held)]
        push(ref, ref, self.send, self.sems.at[piece, side, goal - 1], self.place.up(way * (goal - held)))

    def across(self, piece, slot):
        ref = self.buf.at[piece, slot]
        push(ref, ref, self.send, self.sibling_sems.at[piece], self.place.sibling())

    def take(self, piece, side, number):
        slot = self.slot(-(1, -1)[side] * number)
        await_bytes(self.buf.at[piece, slot], self.sems.at[piece, side, number - 1])
        return slot

    def start(self, piece):
        for goal in (2, 1):
            for side in (0, 1):
                self.onward(piece, side, 0, goal)
        self.across(piece, self.slot(0))

    def pass_on(self, piece):
        for side in (0, 1):
            slot = self.take(piece, side, 2)
            if piece == side:
                self.onward(piece, side, 2, 4)
            self.onward(piece, side, 2, 3)
            self.across(piece, slot)

    def near(self, piece):
        for side in (0, 1):
            self.across(piece, self.take(piece, side, 1))

    def far(self, piece):
        for side in (0, 1):
            self.across(piece, self.take(piece, side, 3))
        self.across(piece, self.take(piece, piece, 4))

    def finish(self, piece):
        await_bytes(self.buf.at[piece, pl.ds(0, DEPTH)], self.sibling_sems.at[piece])

    def close(self):
        await_bytes(self.buf.at[:, pl.ds(0, 15)], self.send)


class Update:
    def __init__(self, place, weights, outgoing, incoming, products, landed, sems, send):
        self.place, self.weights, self.outgoing, self.incoming = place, weights, outgoing, incoming
        self.products, self.landed, self.sems, self.send = products, landed, sems, send

    def positions(self, half):
        return (self.place.x, self.place.y) if half == 0 else (self.place.y, self.place.x)

    def start(self, attended):
        blocks = attended.reshape(SIDE, SIDE, ROWS, HEAD)
        self.outgoing[0] = blocks
        for one in range(SIDE):
            for two in range(SIDE):
                self.outgoing[1, one, two] = blocks[two, one]
        for half in (0, 1):
            second = self.positions(half)[1]
            for step in (2, 1, -1):
                push(
                    self.outgoing.at[half, lax.rem(second + step + SIDE, SIDE)],
                    self.incoming.at[half, second],
                    self.send.at[0],
                    self.sems.at[half, 0],
                    self.place.along(1 - half, step),
                )
            self.incoming[half, second] = self.outgoing[half, second]

    def multiply(self):
        for half in (0, 1):
            first = self.positions(half)[0]
            await_bytes(self.incoming.at[half, pl.ds(0, 3)], self.sems.at[half, 0])
            left = jnp.concatenate([self.incoming[half, other].reshape(4 * ROWS, HEAD) for other in range(SIDE)], 1)
            for piece in range(3):
                cols = pl.ds(piece * 512, 512)
                right = self.weights[half, :, :, :, cols].reshape(SIDE * HEAD, 512)
                product = jnp.dot(left, right, preferred_element_type=F32)
                self.products[half, :, :, cols] = product.astype(BF16).reshape(SIDE, ROWS, 512)
            for index, step in enumerate(STEPS):
                push(
                    self.products.at[half, lax.rem(first + step + SIDE, SIDE)],
                    self.landed.at[half, index],
                    self.send.at[1],
                    self.sems.at[half, 1],
                    self.place.along(half, step),
                )

    def result(self, half):
        first = self.positions(half)[0]
        await_bytes(self.landed.at[half], self.sems.at[half, 1])
        total = self.products[half, first].astype(F32)
        for index in range(3):
            total = total + self.landed[half, index].astype(F32)
        return total

    def close(self):
        await_bytes(self.outgoing.at[:, pl.ds(0, 3)], self.send.at[0])
        await_bytes(self.landed, self.send.at[1])


class ProjectionWeights:
    def __init__(self, place, buf, sems, sibling_sem, send):
        self.place, self.buf, self.sems, self.sibling_sem, self.send = place, buf, sems, sibling_sem, send

    def second(self, half, step):
        return lax.rem((self.place.y if half == 0 else self.place.x) + step + SIDE, SIDE)

    def share(self, half, step):
        ref = self.buf.at[half, self.second(half, step), self.place.core]
        push(ref, ref, self.send, self.sibling_sem, self.place.sibling())

    def start(self):
        for index, step in enumerate((1, -1)):
            for half in (0, 1):
                ref = self.buf.at[half, self.second(half, 0), self.place.core]
                push(ref, ref, self.send, self.sems.at[half, index], self.place.along(1 - half, step))

    def relay(self):
        for index, step in enumerate((1, -1)):
            for half in (0, 1):
                ref = self.buf.at[half, self.second(half, -step), self.place.core]
                await_bytes(ref, self.sems.at[half, index])
                part = self.buf.at[half, self.second(half, -step), self.place.core, pl.ds(index * 32, 32)]
                push(part, part, self.send, self.sems.at[half, 2 + index], self.place.along(1 - half, step))
                self.share(half, -step)

    def last(self):
        for half in (0, 1):
            for index in (0, 1):
                part = self.buf.at[half, self.second(half, 2), self.place.core, pl.ds(index * 32, 32)]
                await_bytes(part, self.sems.at[half, 2 + index])
            self.share(half, 2)

    def finish(self):
        await_bytes(self.buf.at[0, pl.ds(0, 3)], self.sibling_sem)

    def close(self):
        await_bytes(self.buf.at[:, pl.ds(0, 3)], self.send)


def kernel(
    prompt_ids,
    lengths,
    prompt_hbm,
    ctx_hbm,
    latent_hbm,
    imod_hbm,
    tmod_hbm,
    qkv_hbm,
    txt_hbm,
    gain,
    proj_hbm,
    out,
    prompt,
    ctx,
    latent,
    imod,
    tmod,
    qkv_w,
    txt_raw,
    txt_w,
    proj_w,
    local_sems,
    proj_sems,
    proj_sibling,
    proj_send,
    gathered,
    gather_sems,
    gather_sends,
    sc_buf,
    sc_sides,
    sc_line,
    sc_mid,
    sc_landed,
    sc_sems,
    sc_sends,
    handed,
    hand_sems,
    hand_siblings,
    hand_send,
    up_outgoing,
    up_incoming,
    up_products,
    up_landed,
    up_sems,
    up_sends,
    x_state,
    rows_mod,
    text_in,
    text_kv,
    tscale,
):
    place = Place()

    barrier = pltpu.get_barrier_semaphore()
    partners = [place.along(axis, step) for axis in (0, 1) for step in STEPS]
    partners += [place.up(1), place.up(-1), place.up(2), place.up(-2), place.sibling()]
    for partner in partners:
        pl.semaphore_signal(barrier, inc=1, device_id=partner, device_id_type=MESH)

    loads = []

    def load(src, dst):
        copy = pltpu.make_async_copy(src, dst, local_sems.at[len(loads)])
        copy.start()
        loads.append(copy)
        return copy

    halves = (pl.ds(0, HALF), pl.ds(HALF, HALF))
    load_prompt = load(prompt_hbm, prompt)
    load_ctx = [load(ctx_hbm.at[:, cols], ctx.at[:, cols]) for cols in halves]
    load_latent = load(latent_hbm, latent)
    load_imod = load(imod_hbm, imod)

    bounds, running = [], 0
    for image in range(4):
        running = running + lengths[0, image]
        bounds.append(running)

    def segments_of(row_ids):
        return sum((row_ids >= bound).astype(jnp.int32) for bound in bounds)

    rows_iota = lax.broadcasted_iota(jnp.int32, (16 * ROWS, 1), 0)
    lanes_iota = lax.broadcasted_iota(jnp.int32, (1, 16 * ROWS), 1)

    load_prompt.wait()
    row = lax.broadcasted_iota(jnp.int32, (256, 256), 0)
    col = lax.broadcasted_iota(jnp.int32, (256, 256), 1)
    ordered = []
    for half in (0, 1):
        block = row // 16
        owner = block if half == 1 else lax.rem(block, 4) * 4 + block // 4
        source = lax.rem(row // 4, 4) * 64 + owner * 4 + lax.rem(row, 4)
        order = (col == source).astype(BF16)
        ordered.append(jnp.dot(order, prompt[...], preferred_element_type=F32).astype(BF16))
    for half in (0, 1):
        load_ctx[half].wait()
        for piece in range(3):
            product = jnp.dot(ordered[half], ctx[:, pl.ds(half * HALF + piece * 512, 512)], preferred_element_type=F32)
            sc_buf[half, :, :, :, pl.ds(piece * 512, 512)] = product.astype(BF16).reshape(4, 4, ROWS, 512)

    pl.semaphore_wait(barrier, len(partners))
    text_scatter = Scatter(
        place, sc_buf, sc_sides, sc_line, sc_mid, sc_landed, sc_sems, sc_sends, gathered.at[1, :, pl.ds(0, 11)]
    )
    text_scatter.start()
    load_proj = [
        load(
            proj_hbm.at[pl.ds(share * 64, 64), pl.ds(half * HALF, HALF)],
            proj_w.at[half, place.y if half == 0 else place.x, share],
        )
        for half in (0, 1)
        for share in (0, 1)
    ]
    load_txt = load(txt_hbm, txt_raw)
    load_tmod = load(tmod_hbm, tmod)
    load_qkv = [load(qkv_hbm.at[part], qkv_w.at[:, pl.ds(part * HEAD, HEAD)]) for part in range(3)]

    load_imod.wait()
    mine = segments_of(place.tp * ROWS + lax.broadcasted_iota(jnp.int32, (ROWS, 1), 0))
    for step in (0, 1):
        for kind in range(3):
            rows = jnp.zeros((ROWS, WIDTH), F32)
            for image in range(4):
                rows = jnp.where(mine == image, imod[image, kind, step : step + 1, :], rows)
            rows_mod[step, kind] = rows + 1.0 if kind == 1 else rows
    load_latent.wait()
    x_state[...] = latent[...].astype(F32)

    def put_block(which, values):
        for half in (0, 1):
            gathered[which, half, place.tp] = values[:, half * HALF : (half + 1) * HALF]

    def put_image(step):
        values = layer_norm(x_state[...])
        put_block(step, (values * rows_mod[step, 1] + rows_mod[step, 0]).astype(BF16))

    def gather_of(which):
        return Gather(place, gathered.at[which], gather_sems.at[which], gather_sends.at[which])

    put_image(0)
    text_scatter.sums()
    first_gather = gather_of(0)
    first_gather.start()

    handoff = Handoff(place, handed, hand_sems, hand_siblings, hand_send)
    for half in (0, 1):
        handed[half, place.group] = text_scatter.result(half).astype(BF16)
        handoff.start(half)
    first_gather.forward()
    for half in (0, 1):
        handoff.pass_on(half)
    for copy in load_proj:
        copy.wait()
    weights = ProjectionWeights(place, proj_w, proj_sems, proj_sibling, proj_send)
    weights.start()

    for half in (0, 1):
        handoff.near(half)

    load_txt.wait()
    unweave = (col == lax.rem(row, 128) * 2 + row // 128).astype(BF16)

    def part_weights(chunk, carry):
        mixed = txt_raw[pl.ds(pl.multiple_of(chunk * 256, 256), 256), :]
        parted = jnp.dot(unweave, mixed, preferred_element_type=F32).astype(BF16)
        at = pl.ds(pl.multiple_of(chunk * 128, 128), 128)
        txt_w[at, 0:HEAD] = parted[:128]
        txt_w[at, HEAD:] = parted[128:]
        return carry

    lax.fori_loop(0, 24, part_weights, 0)
    load_tmod.wait()
    slot_image = lax.broadcasted_iota(jnp.int32, (ROWS, 1), 0) // 4
    for step in (0, 1):
        for kind in (0, 1):
            rows = jnp.zeros((ROWS, WIDTH), F32)
            for image in range(4):
                rows = jnp.where(slot_image == image, tmod[image, step, kind : kind + 1, :], rows)
            tscale[step, kind] = rows + float(kind)

    pick_row = lax.broadcasted_iota(jnp.int32, (ROWS, 256), 0)
    pick_col = lax.broadcasted_iota(jnp.int32, (ROWS, 256), 1)
    wanted = jnp.zeros((ROWS, 256), jnp.int32)
    for image in range(4):
        wanted = jnp.where(pick_row // 4 == image, prompt_ids[place.group * 4 + image] * 4, wanted)
    pick = (pick_col == wanted + lax.rem(pick_row, 4)).astype(BF16)
    for half in (0, 1):
        handoff.far(half)
    taken = []
    for half in (0, 1):
        handoff.finish(half)
        for piece in range(3):
            held = handed[half, :, :, pl.ds(piece * 512, 512)].reshape(256, 512)
            taken.append(jnp.dot(pick, held, preferred_element_type=F32))
    put_block(2, layer_norm(jnp.concatenate(taken, axis=1)).astype(BF16))
    text_gather = gather_of(2)
    text_gather.start()
    weights.relay()
    text_gather.forward()

    def project_image(which, gather):
        total = None
        for half in (0, 1):
            gather.finish(half)
            term = jnp.dot(
                gathered[which, half].reshape(256, HALF),
                qkv_w[pl.ds(half * HALF, HALF), :],
                preferred_element_type=F32,
            )
            total = term if total is None else total + term
        queries = rms_scale(total[:, :HEAD], gain[0:1]).astype(BF16)
        keys = rms_scale(total[:, HEAD : 2 * HEAD], gain[1:2]).astype(BF16)
        return queries, keys, total[:, 2 * HEAD :].astype(BF16)

    def project_text(step):
        for half in (0, 1):

            def modulate(owner, carry):
                normed = gathered[2, half, owner].astype(F32)
                scaled = normed * tscale[step, 1, :, halves[half]] + tscale[step, 0, :, halves[half]]
                text_in[half, owner] = scaled.astype(BF16)
                return carry

            lax.fori_loop(0, 16, modulate, 0)
        total = None
        for half in (0, 1):
            term = jnp.dot(
                text_in[half].reshape(256, HALF),
                txt_w[pl.ds(half * HALF, HALF), :],
                preferred_element_type=F32,
            )
            total = term if total is None else total + term
        text_kv[:, :HEAD] = rms_scale(total[:, :HEAD], gain[2:3]).astype(BF16)
        text_kv[:, HEAD:] = total[:, HEAD:].astype(BF16)

    segment_rows = segments_of(rows_iota)
    text_allowed = segment_rows == lax.rem(lanes_iota // 4, 4)
    image_allowed = segment_rows == segments_of(lanes_iota)

    def weigh(queries, keys, allowed):
        scores = lax.dot_general(queries, keys, (((1,), (1,)), ((), ())), preferred_element_type=F32)
        return jnp.where(allowed, jnp.exp(scores * HEAD**-0.5), 0.0)

    def attend(queries, keys, values):
        text_part = weigh(queries, text_kv[:, :HEAD], text_allowed)
        image_part = weigh(queries, keys, image_allowed)
        norm = jnp.sum(text_part, -1, keepdims=True) + jnp.sum(image_part, -1, keepdims=True)
        mixed = jnp.dot(text_part.astype(BF16), text_kv[:, HEAD:], preferred_element_type=F32)
        mixed = mixed + jnp.dot(image_part.astype(BF16), values, preferred_element_type=F32)
        return (mixed / norm).astype(BF16)

    def update_of(which):
        parts = (up_outgoing, up_incoming, up_products, up_landed, up_sems, up_sends)
        return Update(place, proj_w, *[ref.at[which] for ref in parts])

    def advance(step, update):
        for half in (0, 1):
            gate = rows_mod[step, 2, :, halves[half]]
            state = x_state[:, halves[half]] + gate * update.result(half)
            x_state[:, halves[half]] = state.astype(BF16).astype(F32)

    for copy in load_qkv:
        copy.wait()
    queries, keys, values = project_image(0, first_gather)
    weights.last()
    for half in (0, 1):
        text_gather.finish(half)
    project_text(0)

    first_update = update_of(0)
    first_update.start(attend(queries, keys, values))
    weights.finish()
    first_update.multiply()
    project_text(1)
    advance(0, first_update)

    put_image(1)
    second_gather = gather_of(1)
    second_gather.start()
    second_gather.forward()
    queries, keys, values = project_image(1, second_gather)
    second_update = update_of(1)
    second_update.start(attend(queries, keys, values))
    second_update.multiply()
    advance(1, second_update)
    out[...] = x_state[...].astype(BF16)

    for part in (text_scatter, first_gather, handoff, weights, text_gather, first_update, second_gather, second_update):
        part.close()


def on_device(
    prompt_states,
    ctx_weight,
    image_prompt,
    image_lengths,
    latents,
    img_mod,
    txt_mod,
    img_qkv,
    txt_kv,
    qk_gain,
    img_proj,
):
    anywhere = pl.BlockSpec(memory_space=pl.ANY)
    scalars = pl.BlockSpec(memory_space=pltpu.SMEM)
    in_vmem = pl.BlockSpec(memory_space=pltpu.VMEM)
    dma = pltpu.SemaphoreType.DMA
    block = (ROWS, HALF)
    denoised = pl.pallas_call(
        kernel,
        out_shape=jax.ShapeDtypeStruct((ROWS, WIDTH), BF16),
        in_specs=[scalars, scalars] + [anywhere] * 7 + [in_vmem, anywhere],
        out_specs=in_vmem,
        scratch_shapes=[
            pltpu.VMEM((256, 256), BF16),
            pltpu.VMEM((256, WIDTH), BF16),
            pltpu.VMEM((ROWS, WIDTH), BF16),
            pltpu.VMEM((4, 3, 2, WIDTH), F32),
            pltpu.VMEM((4, 2, 2, WIDTH), F32),
            pltpu.VMEM((WIDTH, 3 * HEAD), BF16),
            pltpu.VMEM((2 * WIDTH, HEAD), BF16),
            pltpu.VMEM((WIDTH, 2 * HEAD), BF16),
            pltpu.VMEM((2, 4, 2, 64, HALF), BF16),
            dma((14,)),
            dma((2, 4)),
            dma,
            dma,
            pltpu.VMEM((3, 2, 16) + block, BF16),
            dma((3, 2, 9)),
            dma((3,)),
            pltpu.VMEM((2, 4, 4) + block, BF16),
            pltpu.VMEM((2, 3, 2) + block, BF16),
            pltpu.VMEM((2, 3) + block, BF16),
            pltpu.VMEM((2, 4) + block, BF16),
            pltpu.VMEM((2, 6) + block, BF16),
            dma((2, 6)),
            dma((2,)),
            pltpu.VMEM((2, 16) + block, BF16),
            dma((2, 2, 4)),
            dma((2,)),
            dma,
            pltpu.VMEM((2, 2, 4, 4, ROWS, HEAD), BF16),
            pltpu.VMEM((2, 2, 4, 4, ROWS, HEAD), BF16),
            pltpu.VMEM((2, 2, 4) + block, BF16),
            pltpu.VMEM((2, 2, 3) + block, BF16),
            dma((2, 2, 2)),
            dma((2, 2)),
            pltpu.VMEM((ROWS, WIDTH), F32),
            pltpu.VMEM((2, 3, ROWS, WIDTH), F32),
            pltpu.VMEM((2, 16) + block, BF16),
            pltpu.VMEM((256, 2 * HEAD), BF16),
            pltpu.VMEM((2, 2, ROWS, WIDTH), F32),
        ],
        compiler_params=pltpu.CompilerParams(
            collective_id=0, has_side_effects=True, vmem_limit_bytes=56 * 1024 * 1024
        ),
    )(
        image_prompt,
        image_lengths,
        prompt_states.reshape(256, 256),
        ctx_weight,
        latents[0],
        jnp.transpose(img_mod[0], (0, 2, 1, 3)),
        txt_mod[0],
        jnp.transpose(img_qkv, (1, 0, 2)),
        txt_kv.reshape(2 * WIDTH, HEAD),
        qk_gain,
        img_proj,
    )
    return denoised[None]


def solution(mesh):
    placed = (
        P("group", None, "tp"),
        P("tp", None),
        P(),
        P("group", None),
        P("group", "tp", None),
        P("group", None, None, None, None),
        P("group", None, None, None, None),
        P(None, None, "tp"),
        P(None, None, "tp"),
        P(),
        P("tp", None),
    )
    return jax.shard_map(
        on_device, mesh=mesh, in_specs=placed, out_specs=P("group", "tp", None), check_vma=False
    )
```

```python
import functools

import jax
import jax.numpy as jnp
from jax import lax
from jax.experimental import pallas as pl
from jax.experimental.pallas import tpu as pltpu
from jax.sharding import PartitionSpec as P

MESH = pl.DeviceIdType.MESH
F32, BF16 = jnp.float32, jnp.bfloat16
WIDTH, HALF = 3072, 1536
ROWS = 16
SIDE = 4
DEPTH = 8
HEAD = 128
STEPS = (1, -1, 2)
LINES = (0, -1, 1, 2)


def layer_norm(values):
    centered = values - jnp.mean(values, -1, keepdims=True)
    return centered * lax.rsqrt(jnp.mean(centered * centered, -1, keepdims=True) + 1e-6)


def rms_scale(values, gain_row):
    return values * lax.rsqrt(jnp.mean(values * values, -1, keepdims=True) + 1e-6) * gain_row


class Place:
    def __init__(self):
        self.group, self.tp = lax.axis_index("group"), lax.axis_index("tp")
        self.x, self.y = lax.rem(self.tp, SIDE), self.tp // SIDE
        self.z, self.core = self.group // 2, lax.rem(self.group, 2)

    def along(self, axis, step):
        if axis == 0:
            return (self.group, self.y * SIDE + lax.rem(self.x + step + SIDE, SIDE))
        return (self.group, lax.rem(self.y + step + SIDE, SIDE) * SIDE + self.x)

    def slot(self, half, first, second):
        dx, dy = (first, second) if half == 0 else (second, first)
        return lax.rem(self.y + dy + SIDE, SIDE) * SIDE + lax.rem(self.x + dx + SIDE, SIDE)

    def up(self, step):
        return (lax.rem(self.z + step + DEPTH, DEPTH) * 2 + self.core, self.tp)

    def sibling(self):
        return (self.z * 2 + 1 - self.core, self.tp)


def await_bytes(ref, sem):
    pltpu.make_async_copy(ref, ref, sem).wait()


def push(src, dst, send, recv, device):
    pltpu.make_async_remote_copy(
        src_ref=src, dst_ref=dst, send_sem=send, recv_sem=recv, device_id=device, device_id_type=MESH
    ).start()


class Gather:
    def __init__(self, place, buf, sems, send):
        self.place, self.buf, self.sems, self.send = place, buf, sems, send

    def pass_on(self, half, first, second, axis, step, sem):
        ref = self.buf.at[half, self.place.slot(half, first, second)]
        push(ref, ref, self.send, self.sems.at[half, sem], self.place.along(axis, step))

    def start(self):
        for index in (2, 0, 1):
            for half in (0, 1):
                self.pass_on(half, 0, 0, half, STEPS[index], index)
            if index == 2:
                for half in (0, 1):
                    self.pass_on(half, 0, 0, 1 - half, 2, 5)
        for index in (0, 1):
            for half in (0, 1):
                self.pass_on(half, 0, 0, 1 - half, STEPS[index], 3 + index)

    def forward(self):
        for index in (0, 1, 2):
            step = STEPS[index]
            for half in (0, 1):
                await_bytes(self.buf.at[half, self.place.slot(half, -step, 0)], self.sems.at[half, index])
                for other in (0, 1):
                    self.pass_on(half, -step, 0, 1 - half, STEPS[other], 6 + other)
            if index == 1:
                for half in (0, 1):
                    await_bytes(self.buf.at[half, self.place.slot(half, 0, 2)], self.sems.at[half, 5])
                    for onward in (2, 1, -1):
                        self.pass_on(half, 0, 2, half, onward, 8)

    def finish_line(self, half, index):
        if index in (1, 2):
            await_bytes(self.buf.at[half, self.place.slot(half, 0, LINES[index])], self.sems.at[half, 2 + index])
        if index > 0:
            await_bytes(self.buf.at[half, pl.ds(0, 3)], self.sems.at[half, 5 + index])

    def finish(self, half):
        for index in range(4):
            self.finish_line(half, index)

    def close(self):
        await_bytes(self.buf.at[:, pl.ds(0, 15)], self.send)


class Scatter:
    def __init__(self, place, buf, sides, line, mid, landed, sems, send, sent):
        self.place, self.buf, self.sides, self.line = place, buf, sides, line
        self.mid, self.landed, self.sems, self.send, self.sent = mid, landed, sems, send, sent

    def block(self, half, first, second):
        a, b = (self.place.x, self.place.y) if half == 0 else (self.place.y, self.place.x)
        return self.buf.at[half, lax.rem(a + first + SIDE, SIDE), lax.rem(b + second + SIDE, SIDE)]

    def start(self):
        for index in (2, 0, 1):
            for half in (0, 1):
                push(
                    self.block(half, STEPS[index], 2),
                    self.line.at[half, index],
                    self.send.at[0],
                    self.sems.at[half, 3],
                    self.place.along(half, STEPS[index]),
                )
            for half in (0, 1):
                for side in (0, 1):
                    push(
                        self.block(half, STEPS[index], STEPS[side]),
                        self.sides.at[half, index, side],
                        self.send.at[0],
                        self.sems.at[half, index],
                        self.place.along(1 - half, STEPS[side]),
                    )
        for half in (0, 1):
            for side in (0, 1):
                push(
                    self.block(half, 0, STEPS[side]),
                    self.landed.at[half, 3 + side],
                    self.send.at[0],
                    self.sems.at[half, 4],
                    self.place.along(1 - half, STEPS[side]),
                )

    def sums(self):
        for index in (2, 3, 0, 1):
            for half in (0, 1):
                if index < 3:
                    landed, own, axis, step = self.sides.at[half, index], (STEPS[index], 0), half, STEPS[index]
                    count, goal = 2, index
                else:
                    landed, own, axis, step = self.line.at[half], (0, 2), 1 - half, 2
                    count, goal = 3, 5
                await_bytes(landed, self.sems.at[half, index])
                total = self.block(half, *own)[...].astype(F32)
                for other in range(count):
                    total = total + landed[other].astype(F32)
                self.mid[half, index] = total.astype(BF16)
                push(
                    self.mid.at[half, index],
                    self.landed.at[half, goal],
                    self.send.at[1],
                    self.sems.at[half, 5],
                    self.place.along(axis, step),
                )

    def result(self, half):
        await_bytes(self.landed.at[half, pl.ds(0, 2)], self.sems.at[half, 4])
        await_bytes(self.landed.at[half, pl.ds(0, 4)], self.sems.at[half, 5])
        total = self.block(half, 0, 0)[...].astype(F32)
        for other in range(6):
            total = total + self.landed[half, other].astype(F32)
        return total

    def close(self):
        await_bytes(self.sent, self.send.at[0])
        await_bytes(self.mid, self.send.at[1])


class Handoff:
    def __init__(self, place, buf, sems, send):
        self.place, self.buf, self.sems, self.send = place, buf, sems, send

    def slot(self, step):
        return lax.rem(self.place.z + step + DEPTH, DEPTH)

    def onward(self, piece, side, held, goal):
        way = (1, -1)[side]
        ref = self.buf.at[piece, self.slot(-way * held)]
        push(ref, ref, self.send, self.sems.at[piece, side, goal - 1], self.place.up(way * (goal - held)))

    def take(self, piece, side, number):
        await_bytes(self.buf.at[piece, self.slot(-(1, -1)[side] * number)], self.sems.at[piece, side, number - 1])

    def start(self, piece):
        for goal in (2, 1):
            for side in (0, 1):
                self.onward(piece, side, 0, goal)

    def pass_on(self, piece):
        for side in (0, 1):
            self.take(piece, side, 2)
            if piece == side:
                self.onward(piece, side, 2, 4)
            self.onward(piece, side, 2, 3)

    def finish(self, piece):
        for number in (1, 3):
            for side in (0, 1):
                self.take(piece, side, number)
        self.take(piece, piece, 4)

    def close(self):
        await_bytes(self.buf.at[:, pl.ds(0, 7)], self.send)


class Update:
    def __init__(self, place, weights, outgoing, incoming, products, landed, sems, send):
        self.place, self.weights, self.outgoing, self.incoming = place, weights, outgoing, incoming
        self.products, self.landed, self.sems, self.send = products, landed, sems, send

    def positions(self, half):
        return (self.place.x, self.place.y) if half == 0 else (self.place.y, self.place.x)

    def start(self, attended):
        blocks = attended.reshape(SIDE, SIDE, ROWS, HEAD)
        self.outgoing[0] = blocks
        for one in range(SIDE):
            for two in range(SIDE):
                self.outgoing[1, one, two] = blocks[two, one]
        for half in (0, 1):
            second = self.positions(half)[1]
            for step in (2, 1, -1):
                push(
                    self.outgoing.at[half, lax.rem(second + step + SIDE, SIDE)],
                    self.incoming.at[half, second],
                    self.send.at[0],
                    self.sems.at[half, 0],
                    self.place.along(1 - half, step),
                )
            self.incoming[half, second] = self.outgoing[half, second]

    def multiply(self):
        for half in (0, 1):
            first = self.positions(half)[0]
            await_bytes(self.incoming.at[half, pl.ds(0, 3)], self.sems.at[half, 0])
            left = jnp.concatenate([self.incoming[half, other].reshape(4 * ROWS, HEAD) for other in range(SIDE)], 1)
            for piece in range(3):
                cols = pl.ds(piece * 512, 512)
                right = self.weights[half, :, :, :, cols].reshape(SIDE * HEAD, 512)
                product = jnp.dot(left, right, preferred_element_type=F32)
                self.products[half, :, :, cols] = product.astype(BF16).reshape(SIDE, ROWS, 512)
            for index, step in enumerate(STEPS):
                push(
                    self.products.at[half, lax.rem(first + step + SIDE, SIDE)],
                    self.landed.at[half, index],
                    self.send.at[1],
                    self.sems.at[half, 1],
                    self.place.along(half, step),
                )

    def result(self, half):
        first = self.positions(half)[0]
        await_bytes(self.landed.at[half], self.sems.at[half, 1])
        total = self.products[half, first].astype(F32)
        for index in range(3):
            total = total + self.landed[half, index].astype(F32)
        return total

    def close(self):
        await_bytes(self.outgoing.at[:, pl.ds(0, 3)], self.send.at[0])
        await_bytes(self.landed, self.send.at[1])


class ProjectionWeights:
    def __init__(self, place, buf, sems, sibling_sem, send):
        self.place, self.buf, self.sems, self.sibling_sem, self.send = place, buf, sems, sibling_sem, send

    def second(self, half, step):
        return lax.rem((self.place.y if half == 0 else self.place.x) + step + SIDE, SIDE)

    def share(self, half, step):
        ref = self.buf.at[half, self.second(half, step), self.place.core]
        push(ref, ref, self.send, self.sibling_sem, self.place.sibling())

    def start(self):
        for index, step in enumerate((1, -1)):
            for half in (0, 1):
                ref = self.buf.at[half, self.second(half, 0), self.place.core]
                push(ref, ref, self.send, self.sems.at[half, index], self.place.along(1 - half, step))

    def relay(self):
        for index, step in enumerate((1, -1)):
            for half in (0, 1):
                ref = self.buf.at[half, self.second(half, -step), self.place.core]
                await_bytes(ref, self.sems.at[half, index])
                part = self.buf.at[half, self.second(half, -step), self.place.core, pl.ds(index * 32, 32)]
                push(part, part, self.send, self.sems.at[half, 2 + index], self.place.along(1 - half, step))
                self.share(half, -step)

    def last(self):
        for half in (0, 1):
            for index in (0, 1):
                part = self.buf.at[half, self.second(half, 2), self.place.core, pl.ds(index * 32, 32)]
                await_bytes(part, self.sems.at[half, 2 + index])
            self.share(half, 2)

    def finish(self):
        await_bytes(self.buf.at[0, pl.ds(0, 3)], self.sibling_sem)

    def close(self):
        await_bytes(self.buf.at[:, pl.ds(0, 3)], self.send)


def kernel(
    ids_hbm,
    lengths_hbm,
    prompt_hbm,
    ctx_hbm,
    latent_hbm,
    imod_hbm,
    tmod_hbm,
    qkv_hbm,
    txt_hbm,
    gain_hbm,
    proj_hbm,
    out,
    prompt,
    ctx,
    latent,
    imod,
    tmod,
    qkv_w,
    txt_raw,
    txt_w,
    proj_w,
    local_sems,
    proj_sems,
    proj_sibling,
    proj_send,
    gathered,
    gather_sems,
    gather_sends,
    sc_buf,
    sc_sides,
    sc_line,
    sc_mid,
    sc_landed,
    sc_sems,
    sc_sends,
    handed,
    hand_sems,
    hand_send,
    crossing,
    cross_sems,
    up_outgoing,
    up_incoming,
    up_products,
    up_landed,
    up_sems,
    up_sends,
    x_state,
    rows_mod,
    text_in,
    keys_all,
    values_all,
    bias,
    tscale,
    prompt_ids,
    lengths,
    gain,
):
    place = Place()

    barrier = pltpu.get_barrier_semaphore()
    partners = [place.along(axis, step) for axis in (0, 1) for step in STEPS]
    partners += [place.up(1), place.up(-1), place.up(2), place.up(-2), place.sibling()]
    for partner in partners:
        pl.semaphore_signal(barrier, inc=1, device_id=partner, device_id_type=MESH)

    loads = []

    def load(src, dst):
        copy = pltpu.make_async_copy(src, dst, local_sems.at[len(loads)])
        copy.start()
        loads.append(copy)
        return copy

    halves = (pl.ds(0, HALF), pl.ds(HALF, HALF))
    load_prompt = load(prompt_hbm, prompt)
    load_ctx = [load(ctx_hbm.at[:, cols], ctx.at[:, cols]) for cols in halves]
    load_lengths = load(lengths_hbm, lengths)
    load_latent = load(latent_hbm, latent)
    load_imod = load(imod_hbm, imod)

    def segments_of(row_ids):
        return sum((row_ids >= bound).astype(jnp.int32) for bound in bounds)

    rows_iota = lax.broadcasted_iota(jnp.int32, (16 * ROWS, 1), 0)
    lanes_iota = lax.broadcasted_iota(jnp.int32, (1, 16 * ROWS), 1)

    load_prompt.wait()
    row = lax.broadcasted_iota(jnp.int32, (256, 256), 0)
    col = lax.broadcasted_iota(jnp.int32, (256, 256), 1)
    ordered = []
    for half in (0, 1):
        block = row // 16
        owner = block if half == 1 else lax.rem(block, 4) * 4 + block // 4
        source = lax.rem(row // 4, 4) * 64 + owner * 4 + lax.rem(row, 4)
        order = (col == source).astype(BF16)
        ordered.append(jnp.dot(order, prompt[...], preferred_element_type=F32).astype(BF16))
    for half in (0, 1):
        load_ctx[half].wait()
        for piece in range(3):
            product = jnp.dot(ordered[half], ctx[:, pl.ds(half * HALF + piece * 512, 512)], preferred_element_type=F32)
            sc_buf[half, :, :, :, pl.ds(piece * 512, 512)] = product.astype(BF16).reshape(4, 4, ROWS, 512)

    pl.semaphore_wait(barrier, len(partners))
    text_scatter = Scatter(
        place, sc_buf, sc_sides, sc_line, sc_mid, sc_landed, sc_sems, sc_sends, gathered.at[1, :, pl.ds(0, 11)]
    )
    text_scatter.start()
    load_ids = load(ids_hbm, prompt_ids)
    load_gain = load(gain_hbm, gain)
    load_proj = [
        load(
            proj_hbm.at[pl.ds(share * 64, 64), pl.ds(half * HALF, HALF)],
            proj_w.at[half, place.y if half == 0 else place.x, share],
        )
        for half in (0, 1)
        for share in (0, 1)
    ]
    load_txt = load(txt_hbm, txt_raw)
    load_tmod = load(tmod_hbm, tmod)
    load_qkv = [load(qkv_hbm.at[part], qkv_w.at[:, pl.ds(part * HEAD, HEAD)]) for part in range(3)]

    load_lengths.wait()
    bounds, running = [], 0
    for image in range(4):
        running = running + lengths[0, image]
        bounds.append(running)

    load_imod.wait()
    mine = segments_of(place.tp * ROWS + lax.broadcasted_iota(jnp.int32, (ROWS, 1), 0))
    for step in (0, 1):
        for kind in range(3):
            rows = jnp.zeros((ROWS, WIDTH), F32)
            for image in range(4):
                rows = jnp.where(mine == image, imod[image, kind, step : step + 1, :], rows)
            rows_mod[step, kind] = rows + 1.0 if kind == 1 else rows
    load_latent.wait()
    x_state[...] = latent[...].astype(F32)

    def put_block(which, values):
        for half in (0, 1):
            gathered[which, half, place.tp] = values[:, half * HALF : (half + 1) * HALF]

    def put_image(step):
        values = layer_norm(x_state[...])
        put_block(step, (values * rows_mod[step, 1] + rows_mod[step, 0]).astype(BF16))

    def gather_of(which):
        return Gather(place, gathered.at[which], gather_sems.at[which], gather_sends.at[which])

    put_image(0)
    text_scatter.sums()
    first_gather = gather_of(0)
    first_gather.start()

    handoff = Handoff(place, handed, hand_sems, hand_send)
    for half in (0, 1):
        handed[half, place.z] = text_scatter.result(half).astype(BF16)
        handoff.start(half)
    first_gather.forward()
    for half in (0, 1):
        handoff.pass_on(half)
    for copy in load_proj:
        copy.wait()
    weights = ProjectionWeights(place, proj_w, proj_sems, proj_sibling, proj_send)
    weights.start()

    load_txt.wait()
    unweave = (col == lax.rem(row, 128) * 2 + row // 128).astype(BF16)

    def part_weights(chunk, carry):
        mixed = txt_raw[pl.ds(pl.multiple_of(chunk * 256, 256), 256), :]
        parted = jnp.dot(unweave, mixed, preferred_element_type=F32).astype(BF16)
        at = pl.ds(pl.multiple_of(chunk * 128, 128), 128)
        txt_w[at, 0:HEAD] = parted[:128]
        txt_w[at, HEAD:] = parted[128:]
        return carry

    lax.fori_loop(0, 24, part_weights, 0)
    load_tmod.wait()
    slot_image = lax.broadcasted_iota(jnp.int32, (ROWS, 1), 0) // 4
    for step in (0, 1):
        for kind in (0, 1):
            rows = jnp.zeros((ROWS, WIDTH), F32)
            for image in range(4):
                rows = jnp.where(slot_image == image, tmod[image, step, kind : kind + 1, :], rows)
            tscale[step, kind] = rows + float(kind)

    segment_rows = segments_of(rows_iota)
    bias[:, :256] = jnp.where(segment_rows == lax.rem(lanes_iota // 4, 4), 0.0, -1e30)
    bias[:, 256:] = jnp.where(segment_rows == segments_of(lanes_iota), 0.0, -1e30)
    values_all[:, HEAD:] = jnp.ones((512, HEAD), BF16)

    pick_row = lax.broadcasted_iota(jnp.int32, (2 * ROWS, HEAD), 0)
    pick_col = lax.broadcasted_iota(jnp.int32, (2 * ROWS, HEAD), 1)
    load_ids.wait()
    wanted = jnp.full((2 * ROWS, HEAD), -1, jnp.int32)
    for whose, group in enumerate((place.group, place.z * 2 + 1 - place.core)):
        for image in range(4):
            prompt_id = prompt_ids[group * 4 + image]
            held_at = prompt_id // 8 * 16 + lax.rem(prompt_id, 4) * 4
            held_at = jnp.where(lax.rem(prompt_id // 4, 2) == place.core, held_at, -64)
            wanted = jnp.where(pick_row // 4 == whose * 4 + image, held_at, wanted)
    pick = (pick_col == wanted + lax.rem(pick_row, 4)).astype(BF16)
    taken = []
    for half in (0, 1):
        handoff.finish(half)
        for piece in range(3):
            held = handed[half, :, :, pl.ds(piece * 512, 512)].reshape(HEAD, 512)
            both = jnp.dot(pick, held, preferred_element_type=F32)
            taken.append(both[:ROWS])
            crossing[0, :, pl.ds(half * HALF + piece * 512, 512)] = both[ROWS:].astype(BF16)
    push(crossing.at[0], crossing.at[1], cross_sems.at[0], cross_sems.at[1], place.sibling())
    await_bytes(crossing.at[1], cross_sems.at[1])
    taken = jnp.concatenate(taken, axis=1) + crossing[1].astype(F32)
    put_block(2, layer_norm(taken).astype(BF16))
    text_gather = gather_of(2)
    text_gather.start()
    weights.relay()
    text_gather.forward()

    def project_image(which, gather):
        total = None
        for half in (0, 1):
            gather.finish(half)
            term = jnp.dot(
                gathered[which, half].reshape(256, HALF),
                qkv_w[pl.ds(half * HALF, HALF), :],
                preferred_element_type=F32,
            )
            total = term if total is None else total + term
        keys_all[256:, :] = rms_scale(total[:, HEAD : 2 * HEAD], gain[1:2]).astype(BF16)
        values_all[256:, :HEAD] = total[:, 2 * HEAD :].astype(BF16)
        return rms_scale(total[:, :HEAD], gain[0:1]).astype(BF16)

    def modulate_text(step, half, slot):
        normed = gathered[2, half, slot].astype(F32)
        scaled = normed * tscale[step, 1, :, halves[half]] + tscale[step, 0, :, halves[half]]
        text_in[half, slot] = scaled.astype(BF16)

    def project_text():
        total = None
        for half in (0, 1):
            term = jnp.dot(
                text_in[half].reshape(256, HALF),
                txt_w[pl.ds(half * HALF, HALF), :],
                preferred_element_type=F32,
            )
            total = term if total is None else total + term
        keys_all[:256, :] = rms_scale(total[:, :HEAD], gain[2:3]).astype(BF16)
        values_all[:256, :HEAD] = total[:, HEAD:].astype(BF16)

    def attend(queries):
        scores = lax.dot_general(queries, keys_all[...], (((1,), (1,)), ((), ())), preferred_element_type=F32)
        parts = jnp.exp(scores * HEAD**-0.5 + bias[...]).astype(BF16)
        mixed = jnp.dot(parts, values_all[...], preferred_element_type=F32)
        return (mixed[:, :HEAD] / mixed[:, HEAD:]).astype(BF16)

    def update_of(which):
        parts = (up_outgoing, up_incoming, up_products, up_landed, up_sems, up_sends)
        return Update(place, proj_w, *[ref.at[which] for ref in parts])

    def advance(step, update):
        for half in (0, 1):
            gate = rows_mod[step, 2, :, halves[half]]
            state = x_state[:, halves[half]] + gate * update.result(half)
            x_state[:, halves[half]] = state.astype(BF16).astype(F32)

    for copy in load_qkv:
        copy.wait()
    load_gain.wait()
    queries = project_image(0, first_gather)
    weights.last()
    for index in range(4):
        for half in (0, 1):
            text_gather.finish_line(half, index)

            def modulate_line(first, carry):
                modulate_text(0, half, place.slot(half, first, LINES[index]))
                return carry

            lax.fori_loop(0, SIDE, modulate_line, 0)
    project_text()

    first_update = update_of(0)
    first_update.start(attend(queries))
    weights.finish()
    first_update.multiply()
    for half in (0, 1):

        def modulate_block(slot, carry):
            modulate_text(1, half, slot)
            return carry

        lax.fori_loop(0, 16, modulate_block, 0)
    project_text()
    advance(0, first_update)

    put_image(1)
    second_gather = gather_of(1)
    second_gather.start()
    second_gather.forward()
    queries = project_image(1, second_gather)
    second_update = update_of(1)
    second_update.start(attend(queries))
    second_update.multiply()
    advance(1, second_update)
    out[...] = x_state[...].astype(BF16)

    for part in (text_scatter, first_gather, handoff, weights, text_gather, first_update, second_gather, second_update):
        part.close()
    await_bytes(crossing.at[0], cross_sems.at[0])


def on_device(
    prompt_states,
    ctx_weight,
    image_prompt,
    image_lengths,
    latents,
    img_mod,
    txt_mod,
    img_qkv,
    txt_kv,
    qk_gain,
    img_proj,
):
    anywhere = pl.BlockSpec(memory_space=pl.ANY)
    scalars = pl.BlockSpec(memory_space=pltpu.SMEM)
    in_vmem = pl.BlockSpec(memory_space=pltpu.VMEM)
    dma = pltpu.SemaphoreType.DMA
    block = (ROWS, HALF)
    denoised = pl.pallas_call(
        kernel,
        out_shape=pltpu.VMEM((ROWS, WIDTH), BF16),
        in_specs=[anywhere] * 11,
        out_specs=in_vmem,
        scratch_shapes=[
            pltpu.VMEM((256, 256), BF16),
            pltpu.VMEM((256, WIDTH), BF16),
            pltpu.VMEM((ROWS, WIDTH), BF16),
            pltpu.VMEM((4, 3, 2, WIDTH), F32),
            pltpu.VMEM((4, 2, 2, WIDTH), F32),
            pltpu.VMEM((WIDTH, 3 * HEAD), BF16),
            pltpu.VMEM((2 * WIDTH, HEAD), BF16),
            pltpu.VMEM((WIDTH, 2 * HEAD), BF16),
            pltpu.VMEM((2, 4, 2, 64, HALF), BF16),
            dma((17,)),
            dma((2, 4)),
            dma,
            dma,
            pltpu.VMEM((3, 2, 16) + block, BF16),
            dma((3, 2, 9)),
            dma((3,)),
            pltpu.VMEM((2, 4, 4) + block, BF16),
            pltpu.VMEM((2, 3, 2) + block, BF16),
            pltpu.VMEM((2, 3) + block, BF16),
            pltpu.VMEM((2, 4) + block, BF16),
            pltpu.VMEM((2, 6) + block, BF16),
            dma((2, 6)),
            dma((2,)),
            pltpu.VMEM((2, 8) + block, BF16),
            dma((2, 2, 4)),
            dma,
            pltpu.VMEM((2, ROWS, WIDTH), BF16),
            dma((2,)),
            pltpu.VMEM((2, 2, 4, 4, ROWS, HEAD), BF16),
            pltpu.VMEM((2, 2, 4, 4, ROWS, HEAD), BF16),
            pltpu.VMEM((2, 2, 4) + block, BF16),
            pltpu.VMEM((2, 2, 3) + block, BF16),
            dma((2, 2, 2)),
            dma((2, 2)),
            pltpu.VMEM((ROWS, WIDTH), F32),
            pltpu.VMEM((2, 3, ROWS, WIDTH), F32),
            pltpu.VMEM((2, 16) + block, BF16),
            pltpu.VMEM((512, HEAD), BF16),
            pltpu.VMEM((512, 2 * HEAD), BF16),
            pltpu.VMEM((256, 512), F32),
            pltpu.VMEM((2, 2, ROWS, WIDTH), F32),
            pltpu.SMEM((64,), jnp.int32),
            pltpu.SMEM((1, 4), jnp.int32),
            pltpu.VMEM((3, HEAD), F32),
        ],
        compiler_params=pltpu.CompilerParams(
            collective_id=0, has_side_effects=True, vmem_limit_bytes=56 * 1024 * 1024
        ),
    )(
        image_prompt,
        image_lengths,
        prompt_states.reshape(256, 256),
        ctx_weight,
        latents[0],
        jnp.transpose(img_mod[0], (0, 2, 1, 3)),
        txt_mod[0],
        jnp.transpose(img_qkv, (1, 0, 2)),
        txt_kv.reshape(2 * WIDTH, HEAD),
        qk_gain,
        img_proj,
    )
    return denoised[None]


def solution(mesh):
    placed = (
        P("group", None, "tp"),
        P("tp", None),
        P(),
        P("group", None),
        P("group", "tp", None),
        P("group", None, None, None, None),
        P("group", None, None, None, None),
        P(None, None, "tp"),
        P(None, None, "tp"),
        P(),
        P("tp", None),
    )
    return jax.shard_map(
        on_device, mesh=mesh, in_specs=placed, out_specs=P("group", "tp", None), check_vma=False
    )
```

```python
import functools

import jax
import jax.numpy as jnp
from jax import lax
from jax.experimental import pallas as pl
from jax.experimental.pallas import tpu as pltpu
from jax.sharding import PartitionSpec as P

MESH = pl.DeviceIdType.MESH
F32, BF16 = jnp.float32, jnp.bfloat16
WIDTH, HALF = 3072, 1536
ROWS = 16
SIDE = 4
DEPTH = 8
HEAD = 128
STEPS = (1, -1, 2)
LINES = (0, -1, 1, 2)


def layer_norm(values):
    centered = values - jnp.mean(values, -1, keepdims=True)
    return centered * lax.rsqrt(jnp.mean(centered * centered, -1, keepdims=True) + 1e-6)


def rms_scale(values, gain_row):
    return values * lax.rsqrt(jnp.mean(values * values, -1, keepdims=True) + 1e-6) * gain_row


class Place:
    def __init__(self):
        self.group, self.tp = lax.axis_index("group"), lax.axis_index("tp")
        self.x, self.y = lax.rem(self.tp, SIDE), self.tp // SIDE
        self.z, self.core = self.group // 2, lax.rem(self.group, 2)

    def along(self, axis, step):
        if axis == 0:
            return (self.group, self.y * SIDE + lax.rem(self.x + step + SIDE, SIDE))
        return (self.group, lax.rem(self.y + step + SIDE, SIDE) * SIDE + self.x)

    def slot(self, half, first, second):
        dx, dy = (first, second) if half == 0 else (second, first)
        return lax.rem(self.y + dy + SIDE, SIDE) * SIDE + lax.rem(self.x + dx + SIDE, SIDE)

    def up(self, step):
        return (lax.rem(self.z + step + DEPTH, DEPTH) * 2 + self.core, self.tp)

    def sibling(self):
        return (self.z * 2 + 1 - self.core, self.tp)


def await_bytes(ref, sem):
    pltpu.make_async_copy(ref, ref, sem).wait()


def push(src, dst, send, recv, device):
    pltpu.make_async_remote_copy(
        src_ref=src, dst_ref=dst, send_sem=send, recv_sem=recv, device_id=device, device_id_type=MESH
    ).start()


class Gather:
    def __init__(self, place, buf, sems, send):
        self.place, self.buf, self.sems, self.send = place, buf, sems, send

    def pass_on(self, half, first, second, axis, step, sem):
        ref = self.buf.at[half, self.place.slot(half, first, second)]
        push(ref, ref, self.send, self.sems.at[half, sem], self.place.along(axis, step))

    def start(self):
        for index in (0, 1, 2):
            for half in (0, 1):
                self.pass_on(half, 0, 0, half, STEPS[index], index)
            if index == 1:
                for half in (0, 1):
                    self.pass_on(half, 0, 0, 1 - half, 2, 5)
        for index in (0, 1):
            for half in (0, 1):
                self.pass_on(half, 0, 0, 1 - half, STEPS[index], 3 + index)

    def forward(self):
        for index in (0, 1, 2):
            step = STEPS[index]
            for half in (0, 1):
                await_bytes(self.buf.at[half, self.place.slot(half, -step, 0)], self.sems.at[half, index])
                for other in (0, 1):
                    self.pass_on(half, -step, 0, 1 - half, STEPS[other], 6 + other)
            if index == 1:
                for half in (0, 1):
                    await_bytes(self.buf.at[half, self.place.slot(half, 0, 2)], self.sems.at[half, 5])
                    for onward in (2, 1, -1):
                        self.pass_on(half, 0, 2, half, onward, 8)

    def finish_line(self, half, index):
        if index in (1, 2):
            await_bytes(self.buf.at[half, self.place.slot(half, 0, LINES[index])], self.sems.at[half, 2 + index])
        if index > 0:
            await_bytes(self.buf.at[half, pl.ds(0, 3)], self.sems.at[half, 5 + index])

    def finish(self, half):
        for index in range(4):
            self.finish_line(half, index)

    def close(self):
        await_bytes(self.buf.at[:, pl.ds(0, 15)], self.send)


class Scatter:
    def __init__(self, place, buf, sides, line, mid, landed, sems, send, sent):
        self.place, self.buf, self.sides, self.line = place, buf, sides, line
        self.mid, self.landed, self.sems, self.send, self.sent = mid, landed, sems, send, sent

    def block(self, half, first, second):
        a, b = (self.place.x, self.place.y) if half == 0 else (self.place.y, self.place.x)
        return self.buf.at[half, lax.rem(a + first + SIDE, SIDE), lax.rem(b + second + SIDE, SIDE)]

    def start(self):
        for index in (2, 0, 1):
            for half in (0, 1):
                push(
                    self.block(half, STEPS[index], 2),
                    self.line.at[half, index],
                    self.send.at[0],
                    self.sems.at[half, 3],
                    self.place.along(half, STEPS[index]),
                )
            for half in (0, 1):
                for side in (0, 1):
                    push(
                        self.block(half, STEPS[index], STEPS[side]),
                        self.sides.at[half, index, side],
                        self.send.at[0],
                        self.sems.at[half, index],
                        self.place.along(1 - half, STEPS[side]),
                    )
        for half in (0, 1):
            for side in (0, 1):
                push(
                    self.block(half, 0, STEPS[side]),
                    self.landed.at[half, 3 + side],
                    self.send.at[0],
                    self.sems.at[half, 4],
                    self.place.along(1 - half, STEPS[side]),
                )

    def sums(self):
        for index in (2, 3, 0, 1):
            for half in (0, 1):
                if index < 3:
                    landed, own, axis, step = self.sides.at[half, index], (STEPS[index], 0), half, STEPS[index]
                    count, goal = 2, index
                else:
                    landed, own, axis, step = self.line.at[half], (0, 2), 1 - half, 2
                    count, goal = 3, 5
                await_bytes(landed, self.sems.at[half, index])
                total = self.block(half, *own)[...].astype(F32)
                for other in range(count):
                    total = total + landed[other].astype(F32)
                self.mid[half, index] = total.astype(BF16)
                push(
                    self.mid.at[half, index],
                    self.landed.at[half, goal],
                    self.send.at[1],
                    self.sems.at[half, 5],
                    self.place.along(axis, step),
                )

    def result(self, half):
        await_bytes(self.landed.at[half, pl.ds(0, 2)], self.sems.at[half, 4])
        await_bytes(self.landed.at[half, pl.ds(0, 4)], self.sems.at[half, 5])
        total = self.block(half, 0, 0)[...].astype(F32)
        for other in range(6):
            total = total + self.landed[half, other].astype(F32)
        return total

    def close(self):
        await_bytes(self.sent, self.send.at[0])
        await_bytes(self.mid, self.send.at[1])


class Handoff:
    def __init__(self, place, buf, sems, send):
        self.place, self.buf, self.sems, self.send = place, buf, sems, send

    def slot(self, step):
        return lax.rem(self.place.z + step + DEPTH, DEPTH)

    def onward(self, piece, side, held, goal):
        way = (1, -1)[side]
        ref = self.buf.at[piece, self.slot(-way * held)]
        push(ref, ref, self.send, self.sems.at[piece, side, goal - 1], self.place.up(way * (goal - held)))

    def take(self, piece, side, number):
        await_bytes(self.buf.at[piece, self.slot(-(1, -1)[side] * number)], self.sems.at[piece, side, number - 1])

    def start(self, piece, goal):
        for side in (0, 1):
            self.onward(piece, side, 0, goal)

    def pass_on(self, piece):
        for side in (0, 1):
            self.take(piece, side, 2)
            if piece == side:
                self.onward(piece, side, 2, 4)
            self.onward(piece, side, 2, 3)

    def finish(self, piece):
        for number in (1, 3):
            for side in (0, 1):
                self.take(piece, side, number)
        self.take(piece, piece, 4)

    def close(self):
        await_bytes(self.buf.at[:, pl.ds(0, 7)], self.send)


class Update:
    def __init__(self, place, weights, outgoing, incoming, products, landed, sems, send):
        self.place, self.weights, self.outgoing, self.incoming = place, weights, outgoing, incoming
        self.products, self.landed, self.sems, self.send = products, landed, sems, send

    def positions(self, half):
        return (self.place.x, self.place.y) if half == 0 else (self.place.y, self.place.x)

    def start(self, attended):
        blocks = attended.reshape(SIDE, SIDE, ROWS, HEAD)
        self.outgoing[0] = blocks
        for one in range(SIDE):
            for two in range(SIDE):
                self.outgoing[1, one, two] = blocks[two, one]
        for half in (0, 1):
            second = self.positions(half)[1]
            for step in (2, 1, -1):
                push(
                    self.outgoing.at[half, lax.rem(second + step + SIDE, SIDE)],
                    self.incoming.at[half, second],
                    self.send.at[0],
                    self.sems.at[half, 0],
                    self.place.along(1 - half, step),
                )
            self.incoming[half, second] = self.outgoing[half, second]

    def multiply(self):
        for half in (0, 1):
            first = self.positions(half)[0]
            await_bytes(self.incoming.at[half, pl.ds(0, 3)], self.sems.at[half, 0])
            left = jnp.concatenate([self.incoming[half, other].reshape(4 * ROWS, HEAD) for other in range(SIDE)], 1)
            for piece in range(3):
                cols = pl.ds(piece * 512, 512)
                right = self.weights[half, :, :, :, cols].reshape(SIDE * HEAD, 512)
                product = jnp.dot(left, right, preferred_element_type=F32)
                self.products[half, :, :, cols] = product.astype(BF16).reshape(SIDE, ROWS, 512)
            for index, step in ((2, 2), (0, 1), (1, -1)):
                push(
                    self.products.at[half, lax.rem(first + step + SIDE, SIDE)],
                    self.landed.at[half, index],
                    self.send.at[1],
                    self.sems.at[half, 1],
                    self.place.along(half, step),
                )

    def result(self, half):
        first = self.positions(half)[0]
        await_bytes(self.landed.at[half], self.sems.at[half, 1])
        total = self.products[half, first].astype(F32)
        for index in range(3):
            total = total + self.landed[half, index].astype(F32)
        return total

    def close(self):
        await_bytes(self.outgoing.at[:, pl.ds(0, 3)], self.send.at[0])
        await_bytes(self.landed, self.send.at[1])


class ProjectionWeights:
    def __init__(self, place, buf, sems, sibling_sem, send):
        self.place, self.buf, self.sems, self.sibling_sem, self.send = place, buf, sems, sibling_sem, send

    def second(self, half, step):
        return lax.rem((self.place.y if half == 0 else self.place.x) + step + SIDE, SIDE)

    def share(self, half, step):
        ref = self.buf.at[half, self.second(half, step), self.place.core]
        push(ref, ref, self.send, self.sibling_sem, self.place.sibling())

    def start(self):
        for index, step in enumerate((1, -1)):
            for half in (0, 1):
                ref = self.buf.at[half, self.second(half, 0), self.place.core]
                push(ref, ref, self.send, self.sems.at[half, index], self.place.along(1 - half, step))

    def relay(self):
        for index, step in enumerate((1, -1)):
            for half in (0, 1):
                ref = self.buf.at[half, self.second(half, -step), self.place.core]
                await_bytes(ref, self.sems.at[half, index])
                part = self.buf.at[half, self.second(half, -step), self.place.core, pl.ds(index * 32, 32)]
                push(part, part, self.send, self.sems.at[half, 2 + index], self.place.along(1 - half, step))
                self.share(half, -step)

    def last(self):
        for half in (0, 1):
            for index in (0, 1):
                part = self.buf.at[half, self.second(half, 2), self.place.core, pl.ds(index * 32, 32)]
                await_bytes(part, self.sems.at[half, 2 + index])
            self.share(half, 2)

    def finish(self):
        await_bytes(self.buf.at[0, pl.ds(0, 3)], self.sibling_sem)

    def close(self):
        await_bytes(self.buf.at[:, pl.ds(0, 3)], self.send)


def kernel(
    ids_hbm,
    lengths_hbm,
    prompt_hbm,
    ctx_hbm,
    latent_hbm,
    imod_hbm,
    tmod_hbm,
    qkv_hbm,
    txt_hbm,
    gain_hbm,
    proj_hbm,
    out,
    prompt,
    ctx,
    latent,
    imod,
    tmod,
    qkv_w,
    txt_raw,
    txt_w,
    proj_w,
    local_sems,
    proj_sems,
    proj_sibling,
    proj_send,
    gathered,
    gather_sems,
    gather_sends,
    sc_buf,
    sc_sides,
    sc_line,
    sc_mid,
    sc_landed,
    sc_sems,
    sc_sends,
    handed,
    hand_sems,
    hand_send,
    crossing,
    cross_sems,
    up_outgoing,
    up_incoming,
    up_products,
    up_landed,
    up_sems,
    up_sends,
    x_state,
    rows_mod,
    text_in,
    keys_all,
    values_all,
    bias,
    tscale,
    prompt_ids,
    lengths,
    gain,
):
    place = Place()

    barrier = pltpu.get_barrier_semaphore()
    partners = [place.along(axis, step) for axis in (0, 1) for step in STEPS]
    partners += [place.up(1), place.up(-1), place.up(2), place.up(-2), place.sibling()]
    for partner in partners:
        pl.semaphore_signal(barrier, inc=1, device_id=partner, device_id_type=MESH)

    loads = []

    def load(src, dst):
        copy = pltpu.make_async_copy(src, dst, local_sems.at[len(loads)])
        copy.start()
        loads.append(copy)
        return copy

    halves = (pl.ds(0, HALF), pl.ds(HALF, HALF))
    load_prompt = load(prompt_hbm, prompt)
    load_ctx = [load(ctx_hbm.at[:, cols], ctx.at[:, cols]) for cols in halves]
    load_lengths = load(lengths_hbm, lengths)
    load_latent = load(latent_hbm, latent)
    load_imod = load(imod_hbm, imod)

    def segments_of(row_ids):
        return sum((row_ids >= bound).astype(jnp.int32) for bound in bounds)

    rows_iota = lax.broadcasted_iota(jnp.int32, (16 * ROWS, 1), 0)
    lanes_iota = lax.broadcasted_iota(jnp.int32, (1, 16 * ROWS), 1)

    load_prompt.wait()
    row = lax.broadcasted_iota(jnp.int32, (256, 256), 0)
    col = lax.broadcasted_iota(jnp.int32, (256, 256), 1)
    ordered = []
    for half in (0, 1):
        block = row // 16
        owner = block if half == 1 else lax.rem(block, 4) * 4 + block // 4
        source = lax.rem(row // 4, 4) * 64 + owner * 4 + lax.rem(row, 4)
        order = (col == source).astype(BF16)
        ordered.append(jnp.dot(order, prompt[...], preferred_element_type=F32).astype(BF16))
    for half in (0, 1):
        load_ctx[half].wait()
        for piece in range(3):
            product = jnp.dot(ordered[half], ctx[:, pl.ds(half * HALF + piece * 512, 512)], preferred_element_type=F32)
            sc_buf[half, :, :, :, pl.ds(piece * 512, 512)] = product.astype(BF16).reshape(4, 4, ROWS, 512)

    pl.semaphore_wait(barrier, len(partners))
    text_scatter = Scatter(
        place, sc_buf, sc_sides, sc_line, sc_mid, sc_landed, sc_sems, sc_sends, gathered.at[1, :, pl.ds(0, 11)]
    )
    text_scatter.start()
    load_ids = load(ids_hbm, prompt_ids)
    load_gain = load(gain_hbm, gain)
    load_proj = [
        load(
            proj_hbm.at[pl.ds(share * 64, 64), pl.ds(half * HALF, HALF)],
            proj_w.at[half, place.y if half == 0 else place.x, share],
        )
        for half in (0, 1)
        for share in (0, 1)
    ]
    load_txt = load(txt_hbm, txt_raw)
    load_tmod = load(tmod_hbm, tmod)
    load_qkv = [load(qkv_hbm.at[part], qkv_w.at[:, pl.ds(part * HEAD, HEAD)]) for part in range(3)]

    load_lengths.wait()
    bounds, running = [], 0
    for image in range(4):
        running = running + lengths[0, image]
        bounds.append(running)

    load_imod.wait()
    mine = segments_of(place.tp * ROWS + lax.broadcasted_iota(jnp.int32, (ROWS, 1), 0))
    for step in (0, 1):
        for kind in range(3):
            rows = jnp.zeros((ROWS, WIDTH), F32)
            for image in range(4):
                rows = jnp.where(mine == image, imod[image, kind, step : step + 1, :], rows)
            rows_mod[step, kind] = rows + 1.0 if kind == 1 else rows
    load_latent.wait()
    x_state[...] = latent[...].astype(F32)

    def put_block(which, values):
        for half in (0, 1):
            gathered[which, half, place.tp] = values[:, half * HALF : (half + 1) * HALF]

    def put_image(step):
        values = layer_norm(x_state[...])
        put_block(step, (values * rows_mod[step, 1] + rows_mod[step, 0]).astype(BF16))

    def gather_of(which):
        return Gather(place, gathered.at[which], gather_sems.at[which], gather_sends.at[which])

    put_image(0)
    text_scatter.sums()
    first_gather = gather_of(0)
    first_gather.start()

    handoff = Handoff(place, handed, hand_sems, hand_send)
    for half in (0, 1):
        handed[half, place.z] = text_scatter.result(half).astype(BF16)
        handoff.start(half, 2)
    for half in (0, 1):
        handoff.start(half, 1)
    first_gather.forward()
    for half in (0, 1):
        handoff.pass_on(half)
    for copy in load_proj:
        copy.wait()
    weights = ProjectionWeights(place, proj_w, proj_sems, proj_sibling, proj_send)
    weights.start()

    load_txt.wait()
    unweave = (col == lax.rem(row, 128) * 2 + row // 128).astype(BF16)

    def part_weights(chunk, carry):
        mixed = txt_raw[pl.ds(pl.multiple_of(chunk * 256, 256), 256), :]
        parted = jnp.dot(unweave, mixed, preferred_element_type=F32).astype(BF16)
        at = pl.ds(pl.multiple_of(chunk * 128, 128), 128)
        txt_w[at, 0:HEAD] = parted[:128]
        txt_w[at, HEAD:] = parted[128:]
        return carry

    lax.fori_loop(0, 24, part_weights, 0)
    load_tmod.wait()
    slot_image = lax.broadcasted_iota(jnp.int32, (ROWS, 1), 0) // 4
    for step in (0, 1):
        for kind in (0, 1):
            rows = jnp.zeros((ROWS, WIDTH), F32)
            for image in range(4):
                rows = jnp.where(slot_image == image, tmod[image, step, kind : kind + 1, :], rows)
            tscale[step, kind] = rows + float(kind)

    segment_rows = segments_of(rows_iota)
    bias[:, :256] = jnp.where(segment_rows == lax.rem(lanes_iota // 4, 4), 0.0, -1e30)
    bias[:, 256:] = jnp.where(segment_rows == segments_of(lanes_iota), 0.0, -1e30)
    values_all[:, HEAD:] = jnp.ones((512, HEAD), BF16)

    pick_row = lax.broadcasted_iota(jnp.int32, (2 * ROWS, HEAD), 0)
    pick_col = lax.broadcasted_iota(jnp.int32, (2 * ROWS, HEAD), 1)
    load_ids.wait()
    wanted = jnp.full((2 * ROWS, HEAD), -1, jnp.int32)
    for whose, group in enumerate((place.group, place.z * 2 + 1 - place.core)):
        for image in range(4):
            prompt_id = prompt_ids[group * 4 + image]
            held_at = prompt_id // 8 * 16 + lax.rem(prompt_id, 4) * 4
            held_at = jnp.where(lax.rem(prompt_id // 4, 2) == place.core, held_at, -64)
            wanted = jnp.where(pick_row // 4 == whose * 4 + image, held_at, wanted)
    pick = (pick_col == wanted + lax.rem(pick_row, 4)).astype(BF16)
    taken = []
    for half in (0, 1):
        handoff.finish(half)
        for piece in range(3):
            held = handed[half, :, :, pl.ds(piece * 512, 512)].reshape(HEAD, 512)
            both = jnp.dot(pick, held, preferred_element_type=F32)
            taken.append(both[:ROWS])
            crossing[0, :, pl.ds(half * HALF + piece * 512, 512)] = both[ROWS:].astype(BF16)
    push(crossing.at[0], crossing.at[1], cross_sems.at[0], cross_sems.at[1], place.sibling())
    await_bytes(crossing.at[1], cross_sems.at[1])
    taken = jnp.concatenate(taken, axis=1) + crossing[1].astype(F32)
    put_block(2, layer_norm(taken).astype(BF16))
    text_gather = gather_of(2)
    text_gather.start()
    weights.relay()
    text_gather.forward()

    def project_image(which, gather):
        total = None
        for half in (0, 1):
            gather.finish(half)
            term = jnp.dot(
                gathered[which, half].reshape(256, HALF),
                qkv_w[pl.ds(half * HALF, HALF), :],
                preferred_element_type=F32,
            )
            total = term if total is None else total + term
        keys_all[256:, :] = rms_scale(total[:, HEAD : 2 * HEAD], gain[1:2]).astype(BF16)
        values_all[256:, :HEAD] = total[:, 2 * HEAD :].astype(BF16)
        return rms_scale(total[:, :HEAD], gain[0:1]).astype(BF16)

    def modulate_text(step, half, slot):
        normed = gathered[2, half, slot].astype(F32)
        scaled = normed * tscale[step, 1, :, halves[half]] + tscale[step, 0, :, halves[half]]
        text_in[half, slot] = scaled.astype(BF16)

    def project_text():
        total = None
        for half in (0, 1):
            term = jnp.dot(
                text_in[half].reshape(256, HALF),
                txt_w[pl.ds(half * HALF, HALF), :],
                preferred_element_type=F32,
            )
            total = term if total is None else total + term
        keys_all[:256, :] = rms_scale(total[:, :HEAD], gain[2:3]).astype(BF16)
        values_all[:256, :HEAD] = total[:, HEAD:].astype(BF16)

    def attend(queries):
        scores = lax.dot_general(queries, keys_all[...], (((1,), (1,)), ((), ())), preferred_element_type=F32)
        parts = jnp.exp(scores * HEAD**-0.5 + bias[...]).astype(BF16)
        mixed = jnp.dot(parts, values_all[...], preferred_element_type=F32)
        return (mixed[:, :HEAD] / mixed[:, HEAD:]).astype(BF16)

    def update_of(which):
        parts = (up_outgoing, up_incoming, up_products, up_landed, up_sems, up_sends)
        return Update(place, proj_w, *[ref.at[which] for ref in parts])

    def advance(step, update):
        for half in (0, 1):
            gate = rows_mod[step, 2, :, halves[half]]
            state = x_state[:, halves[half]] + gate * update.result(half)
            x_state[:, halves[half]] = state.astype(BF16).astype(F32)

    for copy in load_qkv:
        copy.wait()
    load_gain.wait()
    queries = project_image(0, first_gather)
    weights.last()
    for index in range(4):
        for half in (0, 1):
            text_gather.finish_line(half, index)

            def modulate_line(first, carry):
                modulate_text(0, half, place.slot(half, first, LINES[index]))
                return carry

            lax.fori_loop(0, SIDE, modulate_line, 0)
    project_text()

    first_update = update_of(0)
    first_update.start(attend(queries))
    weights.finish()
    first_update.multiply()
    for half in (0, 1):

        def modulate_block(slot, carry):
            modulate_text(1, half, slot)
            return carry

        lax.fori_loop(0, 16, modulate_block, 0)
    project_text()
    advance(0, first_update)

    put_image(1)
    second_gather = gather_of(1)
    second_gather.start()
    second_gather.forward()
    queries = project_image(1, second_gather)
    second_update = update_of(1)
    second_update.start(attend(queries))
    second_update.multiply()
    advance(1, second_update)
    out[...] = x_state[...].astype(BF16)

    for part in (text_scatter, first_gather, handoff, weights, text_gather, first_update, second_gather, second_update):
        part.close()
    await_bytes(crossing.at[0], cross_sems.at[0])


def on_device(
    prompt_states,
    ctx_weight,
    image_prompt,
    image_lengths,
    latents,
    img_mod,
    txt_mod,
    img_qkv,
    txt_kv,
    qk_gain,
    img_proj,
):
    anywhere = pl.BlockSpec(memory_space=pl.ANY)
    scalars = pl.BlockSpec(memory_space=pltpu.SMEM)
    in_vmem = pl.BlockSpec(memory_space=pltpu.VMEM)
    dma = pltpu.SemaphoreType.DMA
    block = (ROWS, HALF)
    denoised = pl.pallas_call(
        kernel,
        out_shape=pltpu.VMEM((ROWS, WIDTH), BF16),
        in_specs=[anywhere] * 11,
        out_specs=in_vmem,
        scratch_shapes=[
            pltpu.VMEM((256, 256), BF16),
            pltpu.VMEM((256, WIDTH), BF16),
            pltpu.VMEM((ROWS, WIDTH), BF16),
            pltpu.VMEM((4, 3, 2, WIDTH), F32),
            pltpu.VMEM((4, 2, 2, WIDTH), F32),
            pltpu.VMEM((WIDTH, 3 * HEAD), BF16),
            pltpu.VMEM((2 * WIDTH, HEAD), BF16),
            pltpu.VMEM((WIDTH, 2 * HEAD), BF16),
            pltpu.VMEM((2, 4, 2, 64, HALF), BF16),
            dma((17,)),
            dma((2, 4)),
            dma,
            dma,
            pltpu.VMEM((3, 2, 16) + block, BF16),
            dma((3, 2, 9)),
            dma((3,)),
            pltpu.VMEM((2, 4, 4) + block, BF16),
            pltpu.VMEM((2, 3, 2) + block, BF16),
            pltpu.VMEM((2, 3) + block, BF16),
            pltpu.VMEM((2, 4) + block, BF16),
            pltpu.VMEM((2, 6) + block, BF16),
            dma((2, 6)),
            dma((2,)),
            pltpu.VMEM((2, 8) + block, BF16),
            dma((2, 2, 4)),
            dma,
            pltpu.VMEM((2, ROWS, WIDTH), BF16),
            dma((2,)),
            pltpu.VMEM((2, 2, 4, 4, ROWS, HEAD), BF16),
            pltpu.VMEM((2, 2, 4, 4, ROWS, HEAD), BF16),
            pltpu.VMEM((2, 2, 4) + block, BF16),
            pltpu.VMEM((2, 2, 3) + block, BF16),
            dma((2, 2, 2)),
            dma((2, 2)),
            pltpu.VMEM((ROWS, WIDTH), F32),
            pltpu.VMEM((2, 3, ROWS, WIDTH), F32),
            pltpu.VMEM((2, 16) + block, BF16),
            pltpu.VMEM((512, HEAD), BF16),
            pltpu.VMEM((512, 2 * HEAD), BF16),
            pltpu.VMEM((256, 512), F32),
            pltpu.VMEM((2, 2, ROWS, WIDTH), F32),
            pltpu.SMEM((64,), jnp.int32),
            pltpu.SMEM((1, 4), jnp.int32),
            pltpu.VMEM((3, HEAD), F32),
        ],
        compiler_params=pltpu.CompilerParams(
            collective_id=0, has_side_effects=True, vmem_limit_bytes=56 * 1024 * 1024
        ),
    )(
        image_prompt,
        image_lengths,
        prompt_states.reshape(256, 256),
        ctx_weight,
        latents[0],
        jnp.transpose(img_mod[0], (0, 2, 1, 3)),
        txt_mod[0],
        jnp.transpose(img_qkv, (1, 0, 2)),
        txt_kv.reshape(2 * WIDTH, HEAD),
        qk_gain,
        img_proj,
    )
    return denoised[None]


def solution(mesh):
    placed = (
        P("group", None, "tp"),
        P("tp", None),
        P(),
        P("group", None),
        P("group", "tp", None),
        P("group", None, None, None, None),
        P("group", None, None, None, None),
        P(None, None, "tp"),
        P(None, None, "tp"),
        P(),
        P("tp", None),
    )
    return jax.shard_map(
        on_device, mesh=mesh, in_specs=placed, out_specs=P("group", "tp", None), check_vma=False
    )
```

```python
import functools

import jax
import jax.numpy as jnp
from jax import lax
from jax.experimental import pallas as pl
from jax.experimental.pallas import tpu as pltpu
from jax.sharding import PartitionSpec as P

MESH = pl.DeviceIdType.MESH
F32, BF16 = jnp.float32, jnp.bfloat16
WIDTH, HALF = 3072, 1536
ROWS = 16
SIDE = 4
DEPTH = 8
HEAD = 128
STEPS = (1, -1, 2)
LINES = (0, -1, 1, 2)


def layer_norm(values):
    centered = values - jnp.mean(values, -1, keepdims=True)
    return centered * lax.rsqrt(jnp.mean(centered * centered, -1, keepdims=True) + 1e-6)


def rms_scale(values, gain_row):
    return values * lax.rsqrt(jnp.mean(values * values, -1, keepdims=True) + 1e-6) * gain_row


class Place:
    def __init__(self):
        self.group, self.tp = lax.axis_index("group"), lax.axis_index("tp")
        self.x, self.y = lax.rem(self.tp, SIDE), self.tp // SIDE
        self.z, self.core = self.group // 2, lax.rem(self.group, 2)

    def along(self, axis, step):
        if axis == 0:
            return (self.group, self.y * SIDE + lax.rem(self.x + step + SIDE, SIDE))
        return (self.group, lax.rem(self.y + step + SIDE, SIDE) * SIDE + self.x)

    def slot(self, half, first, second):
        dx, dy = (first, second) if half == 0 else (second, first)
        return lax.rem(self.y + dy + SIDE, SIDE) * SIDE + lax.rem(self.x + dx + SIDE, SIDE)

    def up(self, step):
        return (lax.rem(self.z + step + DEPTH, DEPTH) * 2 + self.core, self.tp)

    def sibling(self):
        return (self.z * 2 + 1 - self.core, self.tp)


def await_bytes(ref, sem):
    pltpu.make_async_copy(ref, ref, sem).wait()


def push(src, dst, send, recv, device):
    pltpu.make_async_remote_copy(
        src_ref=src, dst_ref=dst, send_sem=send, recv_sem=recv, device_id=device, device_id_type=MESH
    ).start()


class Gather:
    def __init__(self, place, buf, sems, send):
        self.place, self.buf, self.sems, self.send = place, buf, sems, send

    def pass_on(self, half, first, second, axis, step, sem):
        ref = self.buf.at[half, self.place.slot(half, first, second)]
        push(ref, ref, self.send, self.sems.at[half, sem], self.place.along(axis, step))

    def start(self):
        for index in (0, 1, 2):
            for half in (0, 1):
                self.pass_on(half, 0, 0, half, STEPS[index], index)
            if index == 1:
                for half in (0, 1):
                    self.pass_on(half, 0, 0, 1 - half, 2, 5)
        for index in (0, 1):
            for half in (0, 1):
                self.pass_on(half, 0, 0, 1 - half, STEPS[index], 3 + index)

    def forward(self):
        for index in (0, 1, 2):
            step = STEPS[index]
            for half in (0, 1):
                await_bytes(self.buf.at[half, self.place.slot(half, -step, 0)], self.sems.at[half, index])
                for other in (0, 1):
                    self.pass_on(half, -step, 0, 1 - half, STEPS[other], 6 + other)
            if index == 1:
                for half in (0, 1):
                    await_bytes(self.buf.at[half, self.place.slot(half, 0, 2)], self.sems.at[half, 5])
                    for onward in (2, 1, -1):
                        self.pass_on(half, 0, 2, half, onward, 8)

    def finish_line(self, half, index):
        if index in (1, 2):
            await_bytes(self.buf.at[half, self.place.slot(half, 0, LINES[index])], self.sems.at[half, 2 + index])
        if index > 0:
            await_bytes(self.buf.at[half, pl.ds(0, 3)], self.sems.at[half, 5 + index])

    def finish(self, half):
        for index in range(4):
            self.finish_line(half, index)

    def close(self):
        await_bytes(self.buf.at[:, pl.ds(0, 15)], self.send)


class Scatter:
    def __init__(self, place, buf, sides, line, mid, landed, sems, send, sent):
        self.place, self.buf, self.sides, self.line = place, buf, sides, line
        self.mid, self.landed, self.sems, self.send, self.sent = mid, landed, sems, send, sent

    def block(self, half, first, second):
        a, b = (self.place.x, self.place.y) if half == 0 else (self.place.y, self.place.x)
        return self.buf.at[half, lax.rem(a + first + SIDE, SIDE), lax.rem(b + second + SIDE, SIDE)]

    def start(self):
        for index in (2, 0, 1):
            for half in (0, 1):
                push(
                    self.block(half, STEPS[index], 2),
                    self.line.at[half, index],
                    self.send.at[0],
                    self.sems.at[half, 3],
                    self.place.along(half, STEPS[index]),
                )
            for half in (0, 1):
                for side in (0, 1):
                    push(
                        self.block(half, STEPS[index], STEPS[side]),
                        self.sides.at[half, index, side],
                        self.send.at[0],
                        self.sems.at[half, index],
                        self.place.along(1 - half, STEPS[side]),
                    )
        for half in (0, 1):
            for side in (0, 1):
                push(
                    self.block(half, 0, STEPS[side]),
                    self.landed.at[half, 3 + side],
                    self.send.at[0],
                    self.sems.at[half, 4],
                    self.place.along(1 - half, STEPS[side]),
                )

    def sums(self):
        for index in (2, 3, 0, 1):
            for half in (0, 1):
                if index < 3:
                    landed, own, axis, step = self.sides.at[half, index], (STEPS[index], 0), half, STEPS[index]
                    count, goal = 2, index
                else:
                    landed, own, axis, step = self.line.at[half], (0, 2), 1 - half, 2
                    count, goal = 3, 5
                await_bytes(landed, self.sems.at[half, index])
                total = self.block(half, *own)[...].astype(F32)
                for other in range(count):
                    total = total + landed[other].astype(F32)
                self.mid[half, index] = total.astype(BF16)
                push(
                    self.mid.at[half, index],
                    self.landed.at[half, goal],
                    self.send.at[1],
                    self.sems.at[half, 5],
                    self.place.along(axis, step),
                )

    def result(self, half):
        await_bytes(self.landed.at[half, pl.ds(0, 2)], self.sems.at[half, 4])
        await_bytes(self.landed.at[half, pl.ds(0, 4)], self.sems.at[half, 5])
        total = self.block(half, 0, 0)[...].astype(F32)
        for other in range(6):
            total = total + self.landed[half, other].astype(F32)
        return total

    def close(self):
        await_bytes(self.sent, self.send.at[0])
        await_bytes(self.mid, self.send.at[1])


class Handoff:
    def __init__(self, place, buf, sems, send):
        self.place, self.buf, self.sems, self.send = place, buf, sems, send

    def slot(self, step):
        return lax.rem(self.place.z + step + DEPTH, DEPTH)

    def onward(self, piece, side, held, goal):
        way = (1, -1)[side]
        ref = self.buf.at[piece, self.slot(-way * held)]
        push(ref, ref, self.send, self.sems.at[piece, side, goal - 1], self.place.up(way * (goal - held)))

    def take(self, piece, side, number):
        await_bytes(self.buf.at[piece, self.slot(-(1, -1)[side] * number)], self.sems.at[piece, side, number - 1])

    def start(self, piece, goal):
        for side in (0, 1):
            self.onward(piece, side, 0, goal)

    def pass_on(self, piece):
        for side in (0, 1):
            self.take(piece, side, 2)
            if piece == side:
                self.onward(piece, side, 2, 4)
            self.onward(piece, side, 2, 3)

    def finish(self, piece):
        for number in (1, 3):
            for side in (0, 1):
                self.take(piece, side, number)
        self.take(piece, piece, 4)

    def close(self):
        await_bytes(self.buf.at[:, pl.ds(0, 7)], self.send)


class Update:
    def __init__(self, place, weights, outgoing, incoming, products, landed, sems, send):
        self.place, self.weights, self.outgoing, self.incoming = place, weights, outgoing, incoming
        self.products, self.landed, self.sems, self.send = products, landed, sems, send

    def positions(self, half):
        return (self.place.x, self.place.y) if half == 0 else (self.place.y, self.place.x)

    def start(self, attended):
        blocks = attended.reshape(SIDE, SIDE, ROWS, HEAD)
        for half in (0, 1):
            if half == 0:
                self.outgoing[0] = blocks
            else:
                for one in range(SIDE):
                    for two in range(SIDE):
                        self.outgoing[1, one, two] = blocks[two, one]
            second = self.positions(half)[1]
            for step in (2, 1, -1):
                push(
                    self.outgoing.at[half, lax.rem(second + step + SIDE, SIDE)],
                    self.incoming.at[half, second],
                    self.send.at[0],
                    self.sems.at[half, 0],
                    self.place.along(1 - half, step),
                )
            self.incoming[half, second] = self.outgoing[half, second]

    def multiply(self):
        for half in (0, 1):
            first = self.positions(half)[0]
            await_bytes(self.incoming.at[half, pl.ds(0, 3)], self.sems.at[half, 0])
            left = jnp.concatenate([self.incoming[half, other].reshape(4 * ROWS, HEAD) for other in range(SIDE)], 1)
            for piece in range(3):
                cols = pl.ds(piece * 512, 512)
                right = self.weights[half, :, :, :, cols].reshape(SIDE * HEAD, 512)
                product = jnp.dot(left, right, preferred_element_type=F32)
                self.products[half, :, :, cols] = product.astype(BF16).reshape(SIDE, ROWS, 512)
            for index, step in ((2, 2), (0, 1), (1, -1)):
                push(
                    self.products.at[half, lax.rem(first + step + SIDE, SIDE)],
                    self.landed.at[half, index],
                    self.send.at[1],
                    self.sems.at[half, 1],
                    self.place.along(half, step),
                )

    def result(self, half):
        first = self.positions(half)[0]
        await_bytes(self.landed.at[half], self.sems.at[half, 1])
        total = self.products[half, first].astype(F32)
        for index in range(3):
            total = total + self.landed[half, index].astype(F32)
        return total

    def close(self):
        await_bytes(self.outgoing.at[:, pl.ds(0, 3)], self.send.at[0])
        await_bytes(self.landed, self.send.at[1])


class ProjectionWeights:
    def __init__(self, place, buf, sems, sibling_sem, send):
        self.place, self.buf, self.sems, self.sibling_sem, self.send = place, buf, sems, sibling_sem, send

    def second(self, half, step):
        return lax.rem((self.place.y if half == 0 else self.place.x) + step + SIDE, SIDE)

    def share(self, half, step):
        ref = self.buf.at[half, self.second(half, step), self.place.core]
        push(ref, ref, self.send, self.sibling_sem, self.place.sibling())

    def start(self):
        for index, step in enumerate((1, -1)):
            for half in (0, 1):
                ref = self.buf.at[half, self.second(half, 0), self.place.core]
                push(ref, ref, self.send, self.sems.at[half, index], self.place.along(1 - half, step))

    def relay(self):
        for index, step in enumerate((1, -1)):
            for half in (0, 1):
                ref = self.buf.at[half, self.second(half, -step), self.place.core]
                await_bytes(ref, self.sems.at[half, index])
                part = self.buf.at[half, self.second(half, -step), self.place.core, pl.ds(index * 32, 32)]
                push(part, part, self.send, self.sems.at[half, 2 + index], self.place.along(1 - half, step))
                self.share(half, -step)

    def last(self):
        for half in (0, 1):
            for index in (0, 1):
                part = self.buf.at[half, self.second(half, 2), self.place.core, pl.ds(index * 32, 32)]
                await_bytes(part, self.sems.at[half, 2 + index])
            self.share(half, 2)

    def finish(self):
        await_bytes(self.buf.at[0, pl.ds(0, 3)], self.sibling_sem)

    def close(self):
        await_bytes(self.buf.at[:, pl.ds(0, 3)], self.send)


def kernel(
    ids_hbm,
    lengths_hbm,
    prompt_hbm,
    ctx_hbm,
    latent_hbm,
    imod_hbm,
    tmod_hbm,
    qkv_hbm,
    txt_hbm,
    gain_hbm,
    proj_hbm,
    out,
    prompt,
    ctx,
    latent,
    imod,
    tmod,
    qkv_w,
    txt_raw,
    txt_w,
    proj_w,
    local_sems,
    proj_sems,
    proj_sibling,
    proj_send,
    gathered,
    gather_sems,
    gather_sends,
    sc_buf,
    sc_sides,
    sc_line,
    sc_mid,
    sc_landed,
    sc_sems,
    sc_sends,
    handed,
    hand_sems,
    hand_send,
    crossing,
    cross_sems,
    up_outgoing,
    up_incoming,
    up_products,
    up_landed,
    up_sems,
    up_sends,
    x_state,
    rows_mod,
    text_in,
    keys_all,
    values_all,
    bias,
    tscale,
    prompt_ids,
    lengths,
    gain,
):
    place = Place()

    barrier = pltpu.get_barrier_semaphore()
    partners = [place.along(axis, step) for axis in (0, 1) for step in STEPS]
    partners += [place.up(1), place.up(-1), place.up(2), place.up(-2), place.sibling()]
    for partner in partners:
        pl.semaphore_signal(barrier, inc=1, device_id=partner, device_id_type=MESH)

    loads = []

    def load(src, dst):
        copy = pltpu.make_async_copy(src, dst, local_sems.at[len(loads)])
        copy.start()
        loads.append(copy)
        return copy

    halves = (pl.ds(0, HALF), pl.ds(HALF, HALF))
    load_prompt = load(prompt_hbm, prompt)
    load_ctx = [load(ctx_hbm.at[:, cols], ctx.at[:, cols]) for cols in halves]
    load_lengths = load(lengths_hbm, lengths)
    load_latent = load(latent_hbm, latent)
    load_imod = load(imod_hbm, imod)

    def segments_of(row_ids):
        return sum((row_ids >= bound).astype(jnp.int32) for bound in bounds)

    rows_iota = lax.broadcasted_iota(jnp.int32, (16 * ROWS, 1), 0)
    lanes_iota = lax.broadcasted_iota(jnp.int32, (1, 16 * ROWS), 1)

    load_prompt.wait()
    row = lax.broadcasted_iota(jnp.int32, (256, 256), 0)
    col = lax.broadcasted_iota(jnp.int32, (256, 256), 1)
    ordered = []
    for half in (0, 1):
        block = row // 16
        owner = block if half == 1 else lax.rem(block, 4) * 4 + block // 4
        source = lax.rem(row // 4, 4) * 64 + owner * 4 + lax.rem(row, 4)
        order = (col == source).astype(BF16)
        ordered.append(jnp.dot(order, prompt[...], preferred_element_type=F32).astype(BF16))
    for half in (0, 1):
        load_ctx[half].wait()
        for piece in range(3):
            product = jnp.dot(ordered[half], ctx[:, pl.ds(half * HALF + piece * 512, 512)], preferred_element_type=F32)
            sc_buf[half, :, :, :, pl.ds(piece * 512, 512)] = product.astype(BF16).reshape(4, 4, ROWS, 512)

    pl.semaphore_wait(barrier, len(partners))
    text_scatter = Scatter(
        place, sc_buf, sc_sides, sc_line, sc_mid, sc_landed, sc_sems, sc_sends, gathered.at[1, :, pl.ds(0, 11)]
    )
    text_scatter.start()
    load_ids = load(ids_hbm, prompt_ids)
    load_gain = load(gain_hbm, gain)
    load_proj = [
        load(
            proj_hbm.at[pl.ds(share * 64, 64), pl.ds(half * HALF, HALF)],
            proj_w.at[half, place.y if half == 0 else place.x, share],
        )
        for half in (0, 1)
        for share in (0, 1)
    ]
    load_txt = load(txt_hbm, txt_raw)
    load_tmod = load(tmod_hbm, tmod)
    load_qkv = [load(qkv_hbm.at[part], qkv_w.at[:, pl.ds(part * HEAD, HEAD)]) for part in range(3)]

    load_lengths.wait()
    bounds, running = [], 0
    for image in range(4):
        running = running + lengths[0, image]
        bounds.append(running)

    load_imod.wait()
    mine = segments_of(place.tp * ROWS + lax.broadcasted_iota(jnp.int32, (ROWS, 1), 0))
    for step in (0, 1):
        for kind in range(3):
            rows = jnp.zeros((ROWS, WIDTH), F32)
            for image in range(4):
                rows = jnp.where(mine == image, imod[image, kind, step : step + 1, :], rows)
            rows_mod[step, kind] = rows + 1.0 if kind == 1 else rows
    load_latent.wait()
    x_state[...] = latent[...].astype(F32)

    def put_block(which, values):
        for half in (0, 1):
            gathered[which, half, place.tp] = values[:, half * HALF : (half + 1) * HALF]

    def put_image(step):
        values = layer_norm(x_state[...])
        put_block(step, (values * rows_mod[step, 1] + rows_mod[step, 0]).astype(BF16))

    def gather_of(which):
        return Gather(place, gathered.at[which], gather_sems.at[which // 2], gather_sends.at[which])

    put_image(0)
    text_scatter.sums()
    first_gather = gather_of(0)
    first_gather.start()

    handoff = Handoff(place, handed, hand_sems, hand_send)
    for half in (0, 1):
        handed[half, place.z] = text_scatter.result(half).astype(BF16)
        handoff.start(half, 2)
    for half in (0, 1):
        handoff.start(half, 1)
    first_gather.forward()
    for half in (0, 1):
        handoff.pass_on(half)
    for copy in load_proj:
        copy.wait()
    weights = ProjectionWeights(place, proj_w, proj_sems, proj_sibling, proj_send)
    weights.start()

    load_txt.wait()
    unweave = (col == lax.rem(row, 128) * 2 + row // 128).astype(BF16)

    def part_weights(chunk, carry):
        mixed = txt_raw[pl.ds(pl.multiple_of(chunk * 256, 256), 256), :]
        parted = jnp.dot(unweave, mixed, preferred_element_type=F32).astype(BF16)
        at = pl.ds(pl.multiple_of(chunk * 128, 128), 128)
        txt_w[at, 0:HEAD] = parted[:128]
        txt_w[at, HEAD:] = parted[128:]
        return carry

    lax.fori_loop(0, 24, part_weights, 0)
    load_tmod.wait()
    slot_image = lax.broadcasted_iota(jnp.int32, (ROWS, 1), 0) // 4
    for step in (0, 1):
        for kind in (0, 1):
            rows = jnp.zeros((ROWS, WIDTH), F32)
            for image in range(4):
                rows = jnp.where(slot_image == image, tmod[image, step, kind : kind + 1, :], rows)
            tscale[step, kind] = rows + float(kind)

    segment_rows = segments_of(rows_iota)
    bias[:, :256] = jnp.where(segment_rows == lax.rem(lanes_iota // 4, 4), 0.0, -1e30)
    bias[:, 256:] = jnp.where(segment_rows == segments_of(lanes_iota), 0.0, -1e30)
    values_all[:, HEAD:] = jnp.ones((512, HEAD), BF16)

    pick_row = lax.broadcasted_iota(jnp.int32, (2 * ROWS, HEAD), 0)
    pick_col = lax.broadcasted_iota(jnp.int32, (2 * ROWS, HEAD), 1)
    load_ids.wait()
    wanted = jnp.full((2 * ROWS, HEAD), -1, jnp.int32)
    for whose, group in enumerate((place.group, place.z * 2 + 1 - place.core)):
        for image in range(4):
            prompt_id = prompt_ids[group * 4 + image]
            held_at = prompt_id // 8 * 16 + lax.rem(prompt_id, 4) * 4
            held_at = jnp.where(lax.rem(prompt_id // 4, 2) == place.core, held_at, -64)
            wanted = jnp.where(pick_row // 4 == whose * 4 + image, held_at, wanted)
    pick = (pick_col == wanted + lax.rem(pick_row, 4)).astype(BF16)
    taken = []
    for half in (0, 1):
        handoff.finish(half)
        for piece in range(3):
            held = handed[half, :, :, pl.ds(piece * 512, 512)].reshape(HEAD, 512)
            both = jnp.dot(pick, held, preferred_element_type=F32)
            taken.append(both[:ROWS])
            crossing[0, :, pl.ds(half * HALF + piece * 512, 512)] = both[ROWS:].astype(BF16)
    push(crossing.at[0], crossing.at[1], cross_sems.at[0], cross_sems.at[1], place.sibling())
    await_bytes(crossing.at[1], cross_sems.at[1])
    taken = jnp.concatenate(taken, axis=1) + crossing[1].astype(F32)
    put_block(2, layer_norm(taken).astype(BF16))
    text_gather = gather_of(2)
    text_gather.start()
    weights.relay()
    text_gather.forward()

    def project_image(which, gather):
        total = None
        for half in (0, 1):
            gather.finish(half)
            term = jnp.dot(
                gathered[which, half].reshape(256, HALF),
                qkv_w[pl.ds(half * HALF, HALF), :],
                preferred_element_type=F32,
            )
            total = term if total is None else total + term
        keys_all[256:, :] = rms_scale(total[:, HEAD : 2 * HEAD], gain[1:2]).astype(BF16)
        values_all[256:, :HEAD] = total[:, 2 * HEAD :].astype(BF16)
        return rms_scale(total[:, :HEAD], gain[0:1]).astype(BF16)

    def modulate_text(step, half, slot):
        normed = gathered[2, half, slot].astype(F32)
        scaled = normed * tscale[step, 1, :, halves[half]] + tscale[step, 0, :, halves[half]]
        text_in[half, slot] = scaled.astype(BF16)

    def project_text():
        total = None
        for half in (0, 1):
            term = jnp.dot(
                text_in[half].reshape(256, HALF),
                txt_w[pl.ds(half * HALF, HALF), :],
                preferred_element_type=F32,
            )
            total = term if total is None else total + term
        keys_all[:256, :] = rms_scale(total[:, :HEAD], gain[2:3]).astype(BF16)
        values_all[:256, :HEAD] = total[:, HEAD:].astype(BF16)

    def attend(queries):
        scores = lax.dot_general(queries, keys_all[...], (((1,), (1,)), ((), ())), preferred_element_type=F32)
        parts = jnp.exp(scores * HEAD**-0.5 + bias[...]).astype(BF16)
        mixed = jnp.dot(parts, values_all[...], preferred_element_type=F32)
        return (mixed[:, :HEAD] / mixed[:, HEAD:]).astype(BF16)

    def update_of(which):
        parts = (up_outgoing, up_incoming, up_products, up_landed, up_sems, up_sends)
        return Update(place, proj_w, *[ref.at[which] for ref in parts])

    def advance(step, update):
        for half in (0, 1):
            gate = rows_mod[step, 2, :, halves[half]]
            state = (x_state[:, halves[half]] + gate * update.result(half)).astype(BF16)
            if step == 0:
                x_state[:, halves[half]] = state.astype(F32)
            else:
                out[:, halves[half]] = state

    for copy in load_qkv:
        copy.wait()
    load_gain.wait()
    queries = project_image(0, first_gather)
    weights.last()
    for index in range(4):
        for half in (0, 1):
            text_gather.finish_line(half, index)

            def modulate_line(first, carry):
                modulate_text(0, half, place.slot(half, first, LINES[index]))
                return carry

            lax.fori_loop(0, SIDE, modulate_line, 0)
    project_text()

    first_update = update_of(0)
    first_update.start(attend(queries))
    weights.finish()
    first_update.multiply()
    for half in (0, 1):

        def modulate_block(slot, carry):
            modulate_text(1, half, slot)
            return carry

        lax.fori_loop(0, 16, modulate_block, 0)
    project_text()
    advance(0, first_update)

    put_image(1)
    second_gather = gather_of(1)
    second_gather.start()
    second_gather.forward()
    queries = project_image(1, second_gather)
    second_update = update_of(1)
    second_update.start(attend(queries))
    second_update.multiply()
    advance(1, second_update)

    for part in (text_scatter, first_gather, handoff, weights, text_gather, first_update, second_gather, second_update):
        part.close()
    await_bytes(crossing.at[0], cross_sems.at[0])


def on_device(
    prompt_states,
    ctx_weight,
    image_prompt,
    image_lengths,
    latents,
    img_mod,
    txt_mod,
    img_qkv,
    txt_kv,
    qk_gain,
    img_proj,
):
    anywhere = pl.BlockSpec(memory_space=pl.ANY)
    scalars = pl.BlockSpec(memory_space=pltpu.SMEM)
    in_vmem = pl.BlockSpec(memory_space=pltpu.VMEM)
    dma = pltpu.SemaphoreType.DMA
    block = (ROWS, HALF)
    denoised = pl.pallas_call(
        kernel,
        out_shape=pltpu.VMEM((ROWS, WIDTH), BF16),
        in_specs=[anywhere] * 11,
        out_specs=in_vmem,
        scratch_shapes=[
            pltpu.VMEM((256, 256), BF16),
            pltpu.VMEM((256, WIDTH), BF16),
            pltpu.VMEM((ROWS, WIDTH), BF16),
            pltpu.VMEM((4, 3, 2, WIDTH), F32),
            pltpu.VMEM((4, 2, 2, WIDTH), F32),
            pltpu.VMEM((WIDTH, 3 * HEAD), BF16),
            pltpu.VMEM((2 * WIDTH, HEAD), BF16),
            pltpu.VMEM((WIDTH, 2 * HEAD), BF16),
            pltpu.VMEM((2, 4, 2, 64, HALF), BF16),
            dma((17,)),
            dma((2, 4)),
            dma,
            dma,
            pltpu.VMEM((3, 2, 16) + block, BF16),
            dma((2, 2, 9)),
            dma((3,)),
            pltpu.VMEM((2, 4, 4) + block, BF16),
            pltpu.VMEM((2, 3, 2) + block, BF16),
            pltpu.VMEM((2, 3) + block, BF16),
            pltpu.VMEM((2, 4) + block, BF16),
            pltpu.VMEM((2, 6) + block, BF16),
            dma((2, 6)),
            dma((2,)),
            pltpu.VMEM((2, 8) + block, BF16),
            dma((2, 2, 4)),
            dma,
            pltpu.VMEM((2, ROWS, WIDTH), BF16),
            dma((2,)),
            pltpu.VMEM((2, 2, 4, 4, ROWS, HEAD), BF16),
            pltpu.VMEM((2, 2, 4, 4, ROWS, HEAD), BF16),
            pltpu.VMEM((2, 2, 4) + block, BF16),
            pltpu.VMEM((2, 2, 3) + block, BF16),
            dma((2, 2, 2)),
            dma((2, 2)),
            pltpu.VMEM((ROWS, WIDTH), F32),
            pltpu.VMEM((2, 3, ROWS, WIDTH), F32),
            pltpu.VMEM((2, 16) + block, BF16),
            pltpu.VMEM((512, HEAD), BF16),
            pltpu.VMEM((512, 2 * HEAD), BF16),
            pltpu.VMEM((256, 512), F32),
            pltpu.VMEM((2, 2, ROWS, WIDTH), F32),
            pltpu.SMEM((64,), jnp.int32),
            pltpu.SMEM((1, 4), jnp.int32),
            pltpu.VMEM((3, HEAD), F32),
        ],
        compiler_params=pltpu.CompilerParams(
            collective_id=0, has_side_effects=True, vmem_limit_bytes=56 * 1024 * 1024
        ),
    )(
        image_prompt,
        image_lengths,
        prompt_states.reshape(256, 256),
        ctx_weight,
        latents[0],
        jnp.transpose(img_mod[0], (0, 2, 1, 3)),
        txt_mod[0],
        jnp.transpose(img_qkv, (1, 0, 2)),
        txt_kv.reshape(2 * WIDTH, HEAD),
        qk_gain,
        img_proj,
    )
    return denoised[None]


def solution(mesh):
    placed = (
        P("group", None, "tp"),
        P("tp", None),
        P(),
        P("group", None),
        P("group", "tp", None),
        P("group", None, None, None, None),
        P("group", None, None, None, None),
        P(None, None, "tp"),
        P(None, None, "tp"),
        P(),
        P("tp", None),
    )
    return jax.shard_map(
        on_device, mesh=mesh, in_specs=placed, out_specs=P("group", "tp", None), check_vma=False
    )
```

```python
import functools

import jax
import jax.numpy as jnp
from jax import lax
from jax.experimental import pallas as pl
from jax.experimental.pallas import tpu as pltpu
from jax.sharding import PartitionSpec as P

MESH = pl.DeviceIdType.MESH
F32, BF16 = jnp.float32, jnp.bfloat16
WIDTH, HALF = 3072, 1536
ROWS = 16
SIDE = 4
DEPTH = 8
HEAD = 128
STEPS = (1, -1, 2)
LINES = (0, -1, 1, 2)


def layer_norm(values):
    centered = values - jnp.mean(values, -1, keepdims=True)
    return centered * lax.rsqrt(jnp.mean(centered * centered, -1, keepdims=True) + 1e-6)


def rms_scale(values, gain_row):
    return values * lax.rsqrt(jnp.mean(values * values, -1, keepdims=True) + 1e-6) * gain_row


class Place:
    def __init__(self):
        self.group, self.tp = lax.axis_index("group"), lax.axis_index("tp")
        self.x, self.y = lax.rem(self.tp, SIDE), self.tp // SIDE
        self.z, self.core = self.group // 2, lax.rem(self.group, 2)

    def along(self, axis, step):
        if axis == 0:
            return (self.group, self.y * SIDE + lax.rem(self.x + step + SIDE, SIDE))
        return (self.group, lax.rem(self.y + step + SIDE, SIDE) * SIDE + self.x)

    def slot(self, half, first, second):
        dx, dy = (first, second) if half == 0 else (second, first)
        return lax.rem(self.y + dy + SIDE, SIDE) * SIDE + lax.rem(self.x + dx + SIDE, SIDE)

    def up(self, step):
        return (lax.rem(self.z + step + DEPTH, DEPTH) * 2 + self.core, self.tp)

    def sibling(self):
        return (self.z * 2 + 1 - self.core, self.tp)


def await_bytes(ref, sem):
    pltpu.make_async_copy(ref, ref, sem).wait()


def push(src, dst, send, recv, device):
    pltpu.make_async_remote_copy(
        src_ref=src, dst_ref=dst, send_sem=send, recv_sem=recv, device_id=device, device_id_type=MESH
    ).start()


class Gather:
    def __init__(self, place, buf, sems, send):
        self.place, self.buf, self.sems, self.send = place, buf, sems, send

    def pass_on(self, half, first, second, axis, step, sem):
        ref = self.buf.at[half, self.place.slot(half, first, second)]
        push(ref, ref, self.send, self.sems.at[half, sem], self.place.along(axis, step))

    def start(self):
        for index in (0, 1, 2):
            for half in (0, 1):
                self.pass_on(half, 0, 0, half, STEPS[index], index)
            if index == 1:
                for half in (0, 1):
                    self.pass_on(half, 0, 0, 1 - half, 2, 5)
        for index in (0, 1):
            for half in (0, 1):
                self.pass_on(half, 0, 0, 1 - half, STEPS[index], 3 + index)

    def forward(self):
        for index in (0, 1, 2):
            step = STEPS[index]
            for half in (0, 1):
                await_bytes(self.buf.at[half, self.place.slot(half, -step, 0)], self.sems.at[half, index])
                for other in (0, 1):
                    self.pass_on(half, -step, 0, 1 - half, STEPS[other], 6 + other)
            if index == 1:
                for half in (0, 1):
                    await_bytes(self.buf.at[half, self.place.slot(half, 0, 2)], self.sems.at[half, 5])
                    for onward in (2, 1, -1):
                        self.pass_on(half, 0, 2, half, onward, 8)

    def finish_line(self, half, index):
        if index in (1, 2):
            await_bytes(self.buf.at[half, self.place.slot(half, 0, LINES[index])], self.sems.at[half, 2 + index])
        if index > 0:
            await_bytes(self.buf.at[half, pl.ds(0, 3)], self.sems.at[half, 5 + index])

    def finish(self, half):
        for index in range(4):
            self.finish_line(half, index)

    def close(self):
        await_bytes(self.buf.at[:, pl.ds(0, 15)], self.send)


class Scatter:
    def __init__(self, place, buf, sides, line, mid, landed, sems, send, sent):
        self.place, self.buf, self.sides, self.line = place, buf, sides, line
        self.mid, self.landed, self.sems, self.send, self.sent = mid, landed, sems, send, sent

    def block(self, half, first, second):
        a, b = (self.place.x, self.place.y) if half == 0 else (self.place.y, self.place.x)
        return self.buf.at[half, lax.rem(a + first + SIDE, SIDE), lax.rem(b + second + SIDE, SIDE)]

    def start(self):
        for index in (2, 0, 1):
            for half in (0, 1):
                push(
                    self.block(half, STEPS[index], 2),
                    self.line.at[half, index],
                    self.send.at[0],
                    self.sems.at[half, 3],
                    self.place.along(half, STEPS[index]),
                )
            for half in (0, 1):
                for side in (0, 1):
                    push(
                        self.block(half, STEPS[index], STEPS[side]),
                        self.sides.at[half, index, side],
                        self.send.at[0],
                        self.sems.at[half, index],
                        self.place.along(1 - half, STEPS[side]),
                    )
        for half in (0, 1):
            for side in (0, 1):
                push(
                    self.block(half, 0, STEPS[side]),
                    self.landed.at[half, 3 + side],
                    self.send.at[0],
                    self.sems.at[half, 4],
                    self.place.along(1 - half, STEPS[side]),
                )

    def sums(self):
        for index in (2, 3, 0, 1):
            for half in (0, 1):
                if index < 3:
                    landed, own, axis, step = self.sides.at[half, index], (STEPS[index], 0), half, STEPS[index]
                    count, goal = 2, index
                else:
                    landed, own, axis, step = self.line.at[half], (0, 2), 1 - half, 2
                    count, goal = 3, 5
                await_bytes(landed, self.sems.at[half, index])
                total = self.block(half, *own)[...].astype(F32)
                for other in range(count):
                    total = total + landed[other].astype(F32)
                self.mid[half, index] = total.astype(BF16)
                push(
                    self.mid.at[half, index],
                    self.landed.at[half, goal],
                    self.send.at[1],
                    self.sems.at[half, 5],
                    self.place.along(axis, step),
                )

    def result(self, half):
        await_bytes(self.landed.at[half, pl.ds(0, 2)], self.sems.at[half, 4])
        await_bytes(self.landed.at[half, pl.ds(0, 4)], self.sems.at[half, 5])
        total = self.block(half, 0, 0)[...].astype(F32)
        for other in range(6):
            total = total + self.landed[half, other].astype(F32)
        return total

    def close(self):
        await_bytes(self.sent, self.send.at[0])
        await_bytes(self.mid, self.send.at[1])


class Handoff:
    def __init__(self, place, buf, sems, send):
        self.place, self.buf, self.sems, self.send = place, buf, sems, send

    def slot(self, step):
        return lax.rem(self.place.z + step + DEPTH, DEPTH)

    def onward(self, piece, side, held, goal):
        way = (1, -1)[side]
        ref = self.buf.at[piece, self.slot(-way * held)]
        push(ref, ref, self.send, self.sems.at[piece, side, goal - 1], self.place.up(way * (goal - held)))

    def take(self, piece, side, number):
        await_bytes(self.buf.at[piece, self.slot(-(1, -1)[side] * number)], self.sems.at[piece, side, number - 1])

    def start(self, piece, goal):
        for side in (0, 1):
            self.onward(piece, side, 0, goal)

    def pass_on(self, piece):
        for side in (0, 1):
            self.take(piece, side, 2)
            if piece == side:
                self.onward(piece, side, 2, 4)
            self.onward(piece, side, 2, 3)

    def finish(self, piece):
        for number in (1, 3):
            for side in (0, 1):
                self.take(piece, side, number)
        self.take(piece, piece, 4)

    def close(self):
        await_bytes(self.buf.at[:, pl.ds(0, 7)], self.send)


class Update:
    def __init__(self, place, weights, outgoing, incoming, products, landed, sems, send):
        self.place, self.weights, self.outgoing, self.incoming = place, weights, outgoing, incoming
        self.products, self.landed, self.sems, self.send = products, landed, sems, send

    def positions(self, half):
        return (self.place.x, self.place.y) if half == 0 else (self.place.y, self.place.x)

    def start(self, attended):
        blocks = attended.reshape(SIDE, SIDE, ROWS, HEAD)
        for half in (0, 1):
            if half == 0:
                self.outgoing[0] = blocks
            else:
                for one in range(SIDE):
                    for two in range(SIDE):
                        self.outgoing[1, one, two] = blocks[two, one]
            second = self.positions(half)[1]
            for step in (2, 1, -1):
                push(
                    self.outgoing.at[half, lax.rem(second + step + SIDE, SIDE)],
                    self.incoming.at[half, second],
                    self.send.at[0],
                    self.sems.at[half, 0],
                    self.place.along(1 - half, step),
                )
            self.incoming[half, second] = self.outgoing[half, second]

    def multiply(self):
        for half in (0, 1):
            first = self.positions(half)[0]
            await_bytes(self.incoming.at[half, pl.ds(0, 3)], self.sems.at[half, 0])
            left = jnp.concatenate([self.incoming[half, other].reshape(4 * ROWS, HEAD) for other in range(SIDE)], 1)
            for piece in range(2):
                cols = pl.ds(piece * 768, 768)
                right = self.weights[half, :, :, :, cols].reshape(SIDE * HEAD, 768)
                product = jnp.dot(left, right, preferred_element_type=F32)
                self.products[half, :, :, cols] = product.astype(BF16).reshape(SIDE, ROWS, 768)
            for index, step in ((2, 2), (0, 1), (1, -1)):
                push(
                    self.products.at[half, lax.rem(first + step + SIDE, SIDE)],
                    self.landed.at[half, index],
                    self.send.at[1],
                    self.sems.at[half, 1],
                    self.place.along(half, step),
                )

    def result(self, half):
        first = self.positions(half)[0]
        await_bytes(self.landed.at[half], self.sems.at[half, 1])
        total = self.products[half, first].astype(F32)
        for index in range(3):
            total = total + self.landed[half, index].astype(F32)
        return total

    def close(self):
        await_bytes(self.outgoing.at[:, pl.ds(0, 3)], self.send.at[0])
        await_bytes(self.landed, self.send.at[1])


class ProjectionWeights:
    def __init__(self, place, buf, sems, sibling_sem, send):
        self.place, self.buf, self.sems, self.sibling_sem, self.send = place, buf, sems, sibling_sem, send

    def second(self, half, step):
        return lax.rem((self.place.y if half == 0 else self.place.x) + step + SIDE, SIDE)

    def share(self, half, step):
        ref = self.buf.at[half, self.second(half, step), self.place.core]
        push(ref, ref, self.send, self.sibling_sem, self.place.sibling())

    def start(self):
        for index, step in enumerate((1, -1)):
            for half in (0, 1):
                ref = self.buf.at[half, self.second(half, 0), self.place.core]
                push(ref, ref, self.send, self.sems.at[half, index], self.place.along(1 - half, step))

    def relay(self):
        for index, step in enumerate((1, -1)):
            for half in (0, 1):
                ref = self.buf.at[half, self.second(half, -step), self.place.core]
                await_bytes(ref, self.sems.at[half, index])
                part = self.buf.at[half, self.second(half, -step), self.place.core, pl.ds(index * 32, 32)]
                push(part, part, self.send, self.sems.at[half, 2 + index], self.place.along(1 - half, step))
                self.share(half, -step)

    def last(self):
        for half in (0, 1):
            for index in (0, 1):
                part = self.buf.at[half, self.second(half, 2), self.place.core, pl.ds(index * 32, 32)]
                await_bytes(part, self.sems.at[half, 2 + index])
            self.share(half, 2)

    def finish(self):
        await_bytes(self.buf.at[0, pl.ds(0, 3)], self.sibling_sem)

    def close(self):
        await_bytes(self.buf.at[:, pl.ds(0, 3)], self.send)


def kernel(
    ids_hbm,
    lengths_hbm,
    prompt_hbm,
    ctx_hbm,
    latent_hbm,
    imod_hbm,
    tmod_hbm,
    qkv_hbm,
    txt_hbm,
    gain_hbm,
    proj_hbm,
    out,
    prompt,
    ctx,
    latent,
    imod,
    tmod,
    qkv_w,
    txt_raw,
    txt_w,
    proj_w,
    local_sems,
    proj_sems,
    proj_sibling,
    proj_send,
    gathered,
    gather_sems,
    gather_sends,
    sc_buf,
    sc_sides,
    sc_line,
    sc_mid,
    sc_landed,
    sc_sems,
    sc_sends,
    handed,
    hand_sems,
    hand_send,
    crossing,
    cross_sems,
    up_outgoing,
    up_incoming,
    up_products,
    up_landed,
    up_sems,
    up_sends,
    x_state,
    rows_mod,
    text_in,
    keys_all,
    values_all,
    bias,
    tscale,
    prompt_ids,
    lengths,
    gain,
):
    place = Place()

    barrier = pltpu.get_barrier_semaphore()
    partners = [place.along(axis, step) for axis in (0, 1) for step in STEPS]
    partners += [place.up(1), place.up(-1), place.up(2), place.up(-2), place.sibling()]
    for partner in partners:
        pl.semaphore_signal(barrier, inc=1, device_id=partner, device_id_type=MESH)

    loads = []

    def load(src, dst):
        copy = pltpu.make_async_copy(src, dst, local_sems.at[len(loads)])
        copy.start()
        loads.append(copy)
        return copy

    halves = (pl.ds(0, HALF), pl.ds(HALF, HALF))
    load_prompt = load(prompt_hbm, prompt)
    load_ctx = [load(ctx_hbm.at[:, cols], ctx.at[:, cols]) for cols in halves]
    load_lengths = load(lengths_hbm, lengths)
    load_latent = load(latent_hbm, latent)
    load_imod = load(imod_hbm, imod)

    def segments_of(row_ids):
        return sum((row_ids >= bound).astype(jnp.int32) for bound in bounds)

    rows_iota = lax.broadcasted_iota(jnp.int32, (16 * ROWS, 1), 0)
    lanes_iota = lax.broadcasted_iota(jnp.int32, (1, 16 * ROWS), 1)

    load_prompt.wait()
    row = lax.broadcasted_iota(jnp.int32, (256, 256), 0)
    col = lax.broadcasted_iota(jnp.int32, (256, 256), 1)
    ordered = []
    for half in (0, 1):
        block = row // 16
        owner = block if half == 1 else lax.rem(block, 4) * 4 + block // 4
        source = lax.rem(row // 4, 4) * 64 + owner * 4 + lax.rem(row, 4)
        order = (col == source).astype(BF16)
        ordered.append(jnp.dot(order, prompt[...], preferred_element_type=F32).astype(BF16))
    for half in (0, 1):
        load_ctx[half].wait()
        for piece in range(3):
            product = jnp.dot(ordered[half], ctx[:, pl.ds(half * HALF + piece * 512, 512)], preferred_element_type=F32)
            sc_buf[half, :, :, :, pl.ds(piece * 512, 512)] = product.astype(BF16).reshape(4, 4, ROWS, 512)

    pl.semaphore_wait(barrier, len(partners))
    text_scatter = Scatter(
        place, sc_buf, sc_sides, sc_line, sc_mid, sc_landed, sc_sems, sc_sends, gathered.at[1, :, pl.ds(0, 11)]
    )
    text_scatter.start()
    load_ids = load(ids_hbm, prompt_ids)
    load_gain = load(gain_hbm, gain)
    load_proj = [
        load(
            proj_hbm.at[pl.ds(share * 64, 64), pl.ds(half * HALF, HALF)],
            proj_w.at[half, place.y if half == 0 else place.x, share],
        )
        for half in (0, 1)
        for share in (0, 1)
    ]
    load_txt = load(txt_hbm, txt_raw)
    load_tmod = load(tmod_hbm, tmod)
    load_qkv = [load(qkv_hbm.at[part], qkv_w.at[:, pl.ds(part * HEAD, HEAD)]) for part in range(3)]

    load_lengths.wait()
    bounds, running = [], 0
    for image in range(4):
        running = running + lengths[0, image]
        bounds.append(running)

    load_imod.wait()
    mine = segments_of(place.tp * ROWS + lax.broadcasted_iota(jnp.int32, (ROWS, 1), 0))
    for step in (0, 1):
        for kind in range(3):
            rows = jnp.zeros((ROWS, WIDTH), F32)
            for image in range(4):
                rows = jnp.where(mine == image, imod[image, kind, step : step + 1, :], rows)
            rows_mod[step, kind] = rows + 1.0 if kind == 1 else rows
    load_latent.wait()
    x_state[...] = latent[...].astype(F32)

    def put_block(which, values):
        for half in (0, 1):
            gathered[which, half, place.tp] = values[:, half * HALF : (half + 1) * HALF]

    def put_image(step):
        values = layer_norm(x_state[...])
        put_block(step, (values * rows_mod[step, 1] + rows_mod[step, 0]).astype(BF16))

    def gather_of(which):
        return Gather(place, gathered.at[which], gather_sems.at[which // 2], gather_sends.at[which])

    put_image(0)
    text_scatter.sums()
    first_gather = gather_of(0)
    first_gather.start()

    handoff = Handoff(place, handed, hand_sems, hand_send)
    for half in (0, 1):
        handed[half, place.z] = text_scatter.result(half).astype(BF16)
        handoff.start(half, 2)
    for half in (0, 1):
        handoff.start(half, 1)
    first_gather.forward()
    for half in (0, 1):
        handoff.pass_on(half)
    for copy in load_proj:
        copy.wait()
    weights = ProjectionWeights(place, proj_w, proj_sems, proj_sibling, proj_send)
    weights.start()

    load_txt.wait()
    unweave = (col == lax.rem(row, 128) * 2 + row // 128).astype(BF16)

    def part_weights(chunk, carry):
        mixed = txt_raw[pl.ds(pl.multiple_of(chunk * 256, 256), 256), :]
        parted = jnp.dot(unweave, mixed, preferred_element_type=F32).astype(BF16)
        at = pl.ds(pl.multiple_of(chunk * 128, 128), 128)
        txt_w[at, 0:HEAD] = parted[:128]
        txt_w[at, HEAD:] = parted[128:]
        return carry

    lax.fori_loop(0, 24, part_weights, 0)
    load_tmod.wait()
    slot_image = lax.broadcasted_iota(jnp.int32, (ROWS, 1), 0) // 4
    for step in (0, 1):
        for kind in (0, 1):
            rows = jnp.zeros((ROWS, WIDTH), F32)
            for image in range(4):
                rows = jnp.where(slot_image == image, tmod[image, step, kind : kind + 1, :], rows)
            tscale[step, kind] = rows + float(kind)

    segment_rows = segments_of(rows_iota)
    bias[:, :256] = jnp.where(segment_rows == lax.rem(lanes_iota // 4, 4), 0.0, -1e30)
    bias[:, 256:] = jnp.where(segment_rows == segments_of(lanes_iota), 0.0, -1e30)
    values_all[:, HEAD:] = jnp.ones((512, HEAD), BF16)

    pick_row = lax.broadcasted_iota(jnp.int32, (2 * ROWS, HEAD), 0)
    pick_col = lax.broadcasted_iota(jnp.int32, (2 * ROWS, HEAD), 1)
    load_ids.wait()
    wanted = jnp.full((2 * ROWS, HEAD), -1, jnp.int32)
    for whose, group in enumerate((place.group, place.z * 2 + 1 - place.core)):
        for image in range(4):
            prompt_id = prompt_ids[group * 4 + image]
            held_at = prompt_id // 8 * 16 + lax.rem(prompt_id, 4) * 4
            held_at = jnp.where(lax.rem(prompt_id // 4, 2) == place.core, held_at, -64)
            wanted = jnp.where(pick_row // 4 == whose * 4 + image, held_at, wanted)
    pick = (pick_col == wanted + lax.rem(pick_row, 4)).astype(BF16)
    taken = []
    for half in (0, 1):
        handoff.finish(half)
        for piece in range(3):
            held = handed[half, :, :, pl.ds(piece * 512, 512)].reshape(HEAD, 512)
            both = jnp.dot(pick, held, preferred_element_type=F32)
            taken.append(both[:ROWS])
            crossing[0, :, pl.ds(half * HALF + piece * 512, 512)] = both[ROWS:].astype(BF16)
    push(crossing.at[0], crossing.at[1], cross_sems.at[0], cross_sems.at[1], place.sibling())
    await_bytes(crossing.at[1], cross_sems.at[1])
    taken = jnp.concatenate(taken, axis=1) + crossing[1].astype(F32)
    put_block(2, layer_norm(taken).astype(BF16))
    text_gather = gather_of(2)
    text_gather.start()
    weights.relay()
    text_gather.forward()

    def project_image(which, gather):
        total = None
        for half in (0, 1):
            gather.finish(half)
            term = jnp.dot(
                gathered[which, half].reshape(256, HALF),
                qkv_w[pl.ds(half * HALF, HALF), :],
                preferred_element_type=F32,
            )
            total = term if total is None else total + term
        keys_all[256:, :] = rms_scale(total[:, HEAD : 2 * HEAD], gain[1:2]).astype(BF16)
        values_all[256:, :HEAD] = total[:, 2 * HEAD :].astype(BF16)
        return rms_scale(total[:, :HEAD], gain[0:1]).astype(BF16)

    def modulate_text(step, half, slot):
        normed = gathered[2, half, slot].astype(F32)
        scaled = normed * tscale[step, 1, :, halves[half]] + tscale[step, 0, :, halves[half]]
        text_in[half, slot] = scaled.astype(BF16)

    def project_text():
        total = None
        for half in (0, 1):
            term = jnp.dot(
                text_in[half].reshape(256, HALF),
                txt_w[pl.ds(half * HALF, HALF), :],
                preferred_element_type=F32,
            )
            total = term if total is None else total + term
        keys_all[:256, :] = rms_scale(total[:, :HEAD], gain[2:3]).astype(BF16)
        values_all[:256, :HEAD] = total[:, HEAD:].astype(BF16)

    def attend(queries):
        scores = lax.dot_general(queries, keys_all[...], (((1,), (1,)), ((), ())), preferred_element_type=F32)
        parts = jnp.exp(scores * HEAD**-0.5 + bias[...]).astype(BF16)
        mixed = jnp.dot(parts, values_all[...], preferred_element_type=F32)
        return (mixed[:, :HEAD] / mixed[:, HEAD:]).astype(BF16)

    def update_of(which):
        parts = (up_outgoing, up_incoming, up_products, up_landed, up_sems, up_sends)
        return Update(place, proj_w, *[ref.at[which] for ref in parts])

    def advance(step, update):
        for half in (0, 1):
            gate = rows_mod[step, 2, :, halves[half]]
            state = (x_state[:, halves[half]] + gate * update.result(half)).astype(BF16)
            if step == 0:
                x_state[:, halves[half]] = state.astype(F32)
            else:
                out[:, halves[half]] = state

    for copy in load_qkv:
        copy.wait()
    load_gain.wait()
    queries = project_image(0, first_gather)
    weights.last()
    for index in range(4):
        for half in (0, 1):
            text_gather.finish_line(half, index)

            def modulate_line(first, carry):
                modulate_text(0, half, place.slot(half, first, LINES[index]))
                return carry

            lax.fori_loop(0, SIDE, modulate_line, 0)
    project_text()

    first_update = update_of(0)
    first_update.start(attend(queries))
    weights.finish()
    first_update.multiply()
    for half in (0, 1):

        def modulate_block(slot, carry):
            modulate_text(1, half, slot)
            return carry

        lax.fori_loop(0, 16, modulate_block, 0)
    project_text()
    advance(0, first_update)

    put_image(1)
    second_gather = gather_of(1)
    second_gather.start()
    second_gather.forward()
    queries = project_image(1, second_gather)
    second_update = update_of(1)
    second_update.start(attend(queries))
    second_update.multiply()
    advance(1, second_update)

    for part in (text_scatter, first_gather, handoff, weights, text_gather, first_update, second_gather, second_update):
        part.close()
    await_bytes(crossing.at[0], cross_sems.at[0])


def on_device(
    prompt_states,
    ctx_weight,
    image_prompt,
    image_lengths,
    latents,
    img_mod,
    txt_mod,
    img_qkv,
    txt_kv,
    qk_gain,
    img_proj,
):
    anywhere = pl.BlockSpec(memory_space=pl.ANY)
    scalars = pl.BlockSpec(memory_space=pltpu.SMEM)
    in_vmem = pl.BlockSpec(memory_space=pltpu.VMEM)
    dma = pltpu.SemaphoreType.DMA
    block = (ROWS, HALF)
    denoised = pl.pallas_call(
        kernel,
        out_shape=pltpu.VMEM((ROWS, WIDTH), BF16),
        in_specs=[anywhere] * 11,
        out_specs=in_vmem,
        scratch_shapes=[
            pltpu.VMEM((256, 256), BF16),
            pltpu.VMEM((256, WIDTH), BF16),
            pltpu.VMEM((ROWS, WIDTH), BF16),
            pltpu.VMEM((4, 3, 2, WIDTH), F32),
            pltpu.VMEM((4, 2, 2, WIDTH), F32),
            pltpu.VMEM((WIDTH, 3 * HEAD), BF16),
            pltpu.VMEM((2 * WIDTH, HEAD), BF16),
            pltpu.VMEM((WIDTH, 2 * HEAD), BF16),
            pltpu.VMEM((2, 4, 2, 64, HALF), BF16),
            dma((17,)),
            dma((2, 4)),
            dma,
            dma,
            pltpu.VMEM((3, 2, 16) + block, BF16),
            dma((2, 2, 9)),
            dma((3,)),
            pltpu.VMEM((2, 4, 4) + block, BF16),
            pltpu.VMEM((2, 3, 2) + block, BF16),
            pltpu.VMEM((2, 3) + block, BF16),
            pltpu.VMEM((2, 4) + block, BF16),
            pltpu.VMEM((2, 6) + block, BF16),
            dma((2, 6)),
            dma((2,)),
            pltpu.VMEM((2, 8) + block, BF16),
            dma((2, 2, 4)),
            dma,
            pltpu.VMEM((2, ROWS, WIDTH), BF16),
            dma((2,)),
            pltpu.VMEM((2, 2, 4, 4, ROWS, HEAD), BF16),
            pltpu.VMEM((2, 2, 4, 4, ROWS, HEAD), BF16),
            pltpu.VMEM((2, 2, 4) + block, BF16),
            pltpu.VMEM((2, 2, 3) + block, BF16),
            dma((2, 2, 2)),
            dma((2, 2)),
            pltpu.VMEM((ROWS, WIDTH), F32),
            pltpu.VMEM((2, 3, ROWS, WIDTH), F32),
            pltpu.VMEM((2, 16) + block, BF16),
            pltpu.VMEM((512, HEAD), BF16),
            pltpu.VMEM((512, 2 * HEAD), BF16),
            pltpu.VMEM((256, 512), F32),
            pltpu.VMEM((2, 2, ROWS, WIDTH), F32),
            pltpu.SMEM((64,), jnp.int32),
            pltpu.SMEM((1, 4), jnp.int32),
            pltpu.VMEM((3, HEAD), F32),
        ],
        compiler_params=pltpu.CompilerParams(
            collective_id=0, has_side_effects=True, vmem_limit_bytes=56 * 1024 * 1024
        ),
    )(
        image_prompt,
        image_lengths,
        prompt_states.reshape(256, 256),
        ctx_weight,
        latents[0],
        jnp.transpose(img_mod[0], (0, 2, 1, 3)),
        txt_mod[0],
        jnp.transpose(img_qkv, (1, 0, 2)),
        txt_kv.reshape(2 * WIDTH, HEAD),
        qk_gain,
        img_proj,
    )
    return denoised[None]


def solution(mesh):
    placed = (
        P("group", None, "tp"),
        P("tp", None),
        P(),
        P("group", None),
        P("group", "tp", None),
        P("group", None, None, None, None),
        P("group", None, None, None, None),
        P(None, None, "tp"),
        P(None, None, "tp"),
        P(),
        P("tp", None),
    )
    return jax.shard_map(
        on_device, mesh=mesh, in_specs=placed, out_specs=P("group", "tp", None), check_vma=False
    )
```
